32 devices in a mesh: col: 8 (over z, y), disp: 4 (over x, core).
Axes of the slice: x: 2, y: 2, z: 4, core: 2. Of those that a mesh axis runs over, the one named last changes fastest.
Arguments:
- left: bfloat16 [320, 64, 128], P(None, 'col'), may hold values from -6 to 6
- right: bfloat16 [320, 64, 128], P(None, 'col'), may hold values from -6 to 6
- kernel: bfloat16 [3, 3, 3, 32, 40], replicated, may hold values from -0.1875 to 0.1875
- cotangent: bfloat16 [32, 48, 64, 128], P(None, 'disp', 'col'), may hold values from -14 to 14
Outputs:
- grad_left: bfloat16 [320, 64, 128], P('disp', 'col')
- grad_right: bfloat16 [320, 64, 128], P('disp', 'col')
- grad_kernel: float32 [3, 3, 3, 32, 40], replicated
The draws below stay inside these ranges and needn't reach their ends.
All inputs are finite; a program needn't handle non-finite values.
Results may differ from the reference program's by a relative error of at most 0.0034.
The reference program's roundings to bfloat16 on the way count: a program that leaves them out, or rounds other values in their place, can miss the bound.
Values may be sent and summed in bfloat16 or wider, within the bound.
No kernel may reach another device: no remote copies, remote signals or barrier semaphores. Data moves between devices by JAX's collectives and lax.ppermute only.
A program may use at most 128 MiB of HBM per device.

```python
import math
import jax
import jax.numpy as jnp
from jax import lax

C = 320
G = 40
D = 48
O = 32
ROWS = 128
NX = 64


def draw_cotangent(key, part):
    first_key = jax.random.fold_in(jax.random.fold_in(key, 17), 0)
    column_ramp = 0.5 + 1.5 * jnp.arange(NX, dtype=jnp.float32) / max(NX - 1, 1)
    base_draw = jnp.clip(jax.random.normal(first_key, (O, D, NX, ROWS), jnp.float32), -4.0, 4.0)
    return (base_draw * column_ramp[None, None, :, None]).astype(jnp.bfloat16)


def steps_of(stream_key, extent, pieces, smallest, high):
    gain, own = 1.0, jax.random.fold_in(stream_key, 6)
    for axis_at, parts in pieces:
        steps = jnp.exp(jax.random.uniform(jax.random.fold_in(own, axis_at), (parts,), jnp.float32, smallest / len(pieces), high / len(pieces)))
        gain = gain * jnp.repeat(steps, extent[axis_at] // parts).reshape([-1 if axis == axis_at else 1 for axis in range(len(extent))])
    return gain


def centred(key, shape, scale, limit, pieces=(), kind=jnp.bfloat16):
    factor_of = steps_of(key, shape, pieces, -0.22, 0.18) if pieces else 1.0
    drawn = jax.random.normal(key, shape, jnp.float32) * scale * factor_of
    return jnp.minimum(jnp.maximum(drawn, -limit), limit).astype(kind)


def setup_inputs(seed: int = 0) -> dict:
    keys = jax.random.split(jax.random.key(seed), 5)
    left = centred(keys[0], (C, NX, ROWS), 1.0, 6.0, ((1, 8),))
    right = centred(keys[1], (C, NX, ROWS), 1.0, 6.0, ((1, 8),))
    kernel = centred(keys[2], (3, 3, 3, O, G), (27 * G) ** -0.5, 0.1875)
    cotangent = draw_cotangent(jax.random.fold_in(keys[4], 71), 0)
    return dict(left=left, right=right, kernel=kernel, cotangent=cotangent)


def shifted(feature, amount):
    columns = feature.shape[1]
    padded = jnp.pad(feature, ((0, 0), (D, 0), (0, 0)))
    return lax.dynamic_slice_in_dim(padded, (D - amount).astype(jnp.int32), columns, 1)

def volume_of(left, right, amount):
    channels, columns, row_count = left.shape
    group_size = C // G
    inside = ((amount >= 0) & (amount < D)).astype(jnp.float32)
    clipped = jnp.clip(amount, 0, D - 1).astype(jnp.int32)
    product = left.astype(jnp.float32) * shifted(right, clipped).astype(jnp.float32)
    volume = product.reshape(G, group_size, columns, row_count).sum(1) / group_size
    return (volume * inside).astype(jnp.bfloat16)

def reference(left, right, kernel, cotangent):
    channels, columns, row_count = left.shape
    group_size = C // G
    kernel_float = kernel.astype(jnp.float32)
    cotangent_pad = jnp.pad(cotangent, ((0, 0), (1, 1), (1, 1), (1, 1)))

    def advance(state_now, amount):
        kernel_grad, left_grad, right_grad = state_now
        cotangent_now = lax.dynamic_index_in_dim(cotangent, amount, 1, keepdims=False).astype(jnp.float32)
        updates = []
        for depth_tap in range(3):
            volume = volume_of(left, right, amount + depth_tap - 1)
            volume_pad = jnp.pad(volume, ((0, 0), (1, 1), (1, 1))).astype(jnp.float32)
            for column_tap in range(3):
                for row_tap in range(3):
                    window = volume_pad[:, column_tap:column_tap + columns, row_tap:row_tap + row_count]
                    updates.append(jnp.einsum('owh,gwh->og', cotangent_now, window))
        kernel_grad = kernel_grad + jnp.stack(updates, 0).reshape(3, 3, 3, O, G)
        grad_vol = jnp.zeros((G, columns, row_count), jnp.float32)
        for depth_tap in range(3):
            slab = lax.dynamic_index_in_dim(cotangent_pad, amount + 2 - depth_tap, 1, keepdims=False).astype(jnp.float32)
            for column_tap in range(3):
                for row_tap in range(3):
                    window = slab[:, 2 - column_tap:2 - column_tap + columns, 2 - row_tap:2 - row_tap + row_count]
                    grad_vol = grad_vol + jnp.einsum('og,owh->gwh', kernel_float[depth_tap, column_tap, row_tap], window)
        grad_vol = lax.optimization_barrier(grad_vol.astype(jnp.bfloat16)).astype(jnp.float32)
        spread = jnp.broadcast_to(grad_vol[:, None], (G, group_size, columns, row_count)).reshape(channels, columns, row_count)
        left_grad = left_grad + spread * shifted(right, amount).astype(jnp.float32)
        start = (D - amount).astype(jnp.int32)
        current = lax.dynamic_slice_in_dim(right_grad, start, columns, 1)
        right_grad = lax.dynamic_update_slice_in_dim(right_grad, current + spread * left.astype(jnp.float32), start, 1)
        return ((kernel_grad, left_grad, right_grad), None)
    initial = (jnp.zeros((3, 3, 3, O, G), jnp.float32), jnp.zeros((channels, columns, row_count), jnp.float32), jnp.zeros((channels, D + columns, row_count), jnp.float32))
    final, unused = lax.scan(advance, initial, jnp.arange(D, dtype=jnp.int32))
    kernel_grad, left_grad, right_grad = final
    grad_left = (left_grad / group_size).astype(jnp.bfloat16)
    grad_right = (right_grad[:, D:] / group_size).astype(jnp.bfloat16)
    grad_kernel = kernel_grad * (1.0 / math.sqrt(D * columns * row_count))
    return (grad_left, grad_right, grad_kernel)
```

```python
import functools
import math

import jax
import jax.numpy as jnp
import numpy as np
from jax import lax
from jax.experimental import pallas as pl
from jax.experimental.pallas import tpu as pltpu
from jax.sharding import PartitionSpec as P

C = 320
G = 40
D = 48
GROUP = C // G
HIGHEST = lax.Precision.HIGHEST


def shifted(value, axis, steps):
    count = lax.axis_size(axis)
    leading, last = (max(0, -steps), min(count, count - steps))
    return lax.ppermute(value, axis, [(source, source + steps) for source in range(leading, last)])


def conv_rows(outs, width):
    main = np.tile(np.arange(width), outs)
    return np.concatenate([main, np.full(outs, -1), np.full(outs, width)])


def toeplitz(kernel_local, width):
    outs, groups = kernel_local.shape[3:]
    row_col = conv_rows(outs, width)
    row_out = np.concatenate([np.repeat(np.arange(outs), width), np.tile(np.arange(outs), 2)])
    spread = np.zeros((outs, row_col.size), np.float32)
    spread[row_out, np.arange(row_col.size)] = 1
    taps = jnp.transpose(kernel_local[::-1], (1, 2, 4, 0, 3))
    wide = jnp.einsum(
        "qrgpo,ok->qrgpk", taps, jnp.asarray(spread, jnp.bfloat16),
        preferred_element_type=jnp.float32,
    ).astype(jnp.bfloat16)
    out_col = np.arange(width)
    column_tap = out_col[:, None] - row_col[None, :] + 1
    total = jnp.zeros((3, groups, width, 3, row_col.size), jnp.bfloat16)
    for tap in range(3):
        mask = jnp.asarray(column_tap == tap)[None, None, :, None, :]
        total = jnp.where(mask, wide[tap][:, :, None], total)
    return total.reshape(3 * groups * width, 3 * row_col.size)


def roll_zero(value, steps):
    size = value.shape[-1]
    lane = lax.broadcasted_iota(jnp.int32, value.shape, value.ndim - 1)
    moved = pltpu.roll(value, steps % size, value.ndim - 1)
    return jnp.where(lane == (0 if steps > 0 else size - 1), 0.0, moved)


def work(
    hops, places, left_ref, right_ref, cot_ref, halo_ref, weight_ref, fold_ref,
    grad_left_ref, own_ref, *rest
):
    sent_refs, (sums_ref, left_s, right_s, vol_s, cot_s, gv_s, grad_s, prod_s) = (
        rest[:hops], rest[hops:],
    )
    channels, width, rows = left_ref.shape
    groups = channels // GROUP
    blocks, outs, levels = cot_ref.shape[:3]
    main = outs * width
    span = main + 2 * outs
    reach = hops * width
    f32, bf16 = jnp.float32, jnp.bfloat16

    left_s[...] = left_ref[...].astype(f32)
    for hop in range(hops + 1):
        place = places[0] - hop
        block = right_ref[jnp.maximum(place, 0)].astype(f32)
        at = reach - hop * width
        right_s[:, at : at + width] = jnp.where(place >= 0, block, 0.0)

    def volume_step(group, carry):
        first = group * GROUP
        lefts = [left_s[first + k] for k in range(GROUP)]
        rows_at = pl.ds(pl.multiple_of(group * width, width), width)
        for d in range(D):
            total = lefts[0] * right_s[first, reach - d : reach - d + width]
            for k in range(1, GROUP):
                total = total + lefts[k] * right_s[first + k, reach - d : reach - d + width]
            value = (total * (1.0 / GROUP)).astype(bf16).astype(f32)
            vol_s[d, 0, rows_at] = roll_zero(value, 1)
            vol_s[d, 1, rows_at] = value
            vol_s[d, 2, rows_at] = roll_zero(value, -1)
        return carry

    lax.fori_loop(0, groups, volume_step, 0)

    cot_s[0] = jnp.zeros((span, rows), bf16)
    cot_s[D + 1] = jnp.zeros((span, rows), bf16)
    for block in range(blocks):

        def assemble(level, carry, block=block):
            at = block * levels + level + 1
            value = cot_ref[block, :, level].astype(f32).reshape(main, rows)
            cot_s[at, 0:main] = value.astype(bf16)
            cot_s[at, main:span] = halo_ref[block, level]
            return carry

        lax.fori_loop(0, levels, assemble, 0)

    def grad_volume_step(pair, carry):
        first = pair * 2
        near = cot_s[pl.ds(first, 3)].reshape(3 * span, rows)
        far = cot_s[pl.ds(first + 1, 3)].reshape(3 * span, rows)
        result = jnp.dot(
            weight_ref[...], jnp.concatenate([near, far], axis=1), preferred_element_type=f32
        )
        size = groups * width
        for half in range(2):
            part = result[:, half * rows : (half + 1) * rows]
            total = (
                part[size : 2 * size]
                + roll_zero(part[:size], -1)
                + roll_zero(part[2 * size :], 1)
            )
            gv_s[first + half] = total.astype(bf16).astype(f32)
        return carry

    lax.fori_loop(0, D // 2, grad_volume_step, 0)

    chunk = 4
    prod_s[...] = jnp.zeros(prod_s.shape, f32)

    def kernel_step(step, carry):
        first = step * chunk
        volume = jnp.concatenate(
            [vol_s[first + k].reshape(3 * groups * width, rows).astype(bf16) for k in range(chunk)],
            axis=1,
        )
        for tap in range(3):
            value = jnp.concatenate([cot_s[first + k + tap] for k in range(chunk)], axis=1)
            prod_s[tap] += lax.dot_general(
                value, volume, (((1,), (1,)), ((), ())), preferred_element_type=f32
            )
        return carry

    lax.fori_loop(0, D // chunk, kernel_step, 0)

    size = 3 * groups * width
    col_in = lax.broadcasted_iota(jnp.int32, (width, size), 0)
    col_out = lax.broadcasted_iota(jnp.int32, (width, size), 1) % width
    edge = lax.broadcasted_iota(jnp.int32, (outs, size), 1) % width
    for column_tap in range(3):
        mask = col_out - col_in + 1 == column_tap
        parts = []
        for tap in range(3):
            value = prod_s[tap, 0:main].reshape(outs, width, size)
            total = jnp.sum(jnp.where(mask[None], value, 0.0), axis=1)
            if column_tap == 2:
                total = total + jnp.where(edge == 0, prod_s[tap, main : main + outs], 0.0)
            if column_tap == 0:
                total = total + jnp.where(edge == width - 1, prod_s[tap, main + outs : span], 0.0)
            parts.append(total)
        gathered = jnp.concatenate(parts, axis=0)
        sums_ref[column_tap] = lax.dot_general(
            fold_ref[...], gathered, (((1,), (1,)), ((), ())),
            precision=HIGHEST, preferred_element_type=f32,
        )

    grad_s[...] = jnp.zeros(grad_s.shape, f32)

    def grads_step(group, carry):
        first = group * GROUP
        lefts = [left_s[first + k] for k in range(GROUP)]
        totals = [jnp.zeros((width, rows), f32) for k in range(GROUP)]
        rows_at = pl.ds(pl.multiple_of(group * width, width), width)
        for d in range(D):
            value = gv_s[d, rows_at]
            for k in range(GROUP):
                totals[k] = totals[k] + value * right_s[first + k, reach - d : reach - d + width]
                grad_s[first + k, reach - d : reach - d + width] += value * lefts[k]
        for k in range(GROUP):
            grad_left_ref[first + k] = (totals[k] * (1.0 / GROUP)).astype(bf16)
        return carry

    lax.fori_loop(0, groups, grads_step, 0)
    own_ref[...] = grad_s[:, reach : reach + width] * (1.0 / GROUP)
    for hop in range(1, hops + 1):
        at = reach - hop * width
        sent_refs[hop - 1][...] = (grad_s[:, at : at + width] * (1.0 / GROUP)).astype(bf16)


def run_work(place, left, right_blocks, cot_blocks, halo_blocks, weights, fold, hops):
    channels, width, rows = left.shape
    groups = channels // GROUP
    blocks, outs, levels = cot_blocks.shape[:3]
    span = outs * (width + 2)
    size = 3 * groups * width
    f32, bf16 = jnp.float32, jnp.bfloat16
    vmem = pl.BlockSpec(memory_space=pltpu.VMEM)
    return pl.pallas_call(
        functools.partial(work, hops),
        out_shape=[
            jax.ShapeDtypeStruct((channels, width, rows), bf16),
            jax.ShapeDtypeStruct((channels, width, rows), f32),
            *[jax.ShapeDtypeStruct((channels, width, rows), bf16)] * hops,
            jax.ShapeDtypeStruct((3, fold.shape[0], 3 * outs), f32),
        ],
        in_specs=[pl.BlockSpec(memory_space=pltpu.SMEM)] + [vmem] * 6,
        out_specs=[vmem] * (hops + 3),
        scratch_shapes=[
            pltpu.VMEM((channels, width, rows), f32),
            pltpu.VMEM((channels, (hops + 1) * width, rows), f32),
            pltpu.VMEM((D, 3, groups * width, rows), f32),
            pltpu.VMEM((D + 2, span, rows), bf16),
            pltpu.VMEM((D, groups * width, rows), f32),
            pltpu.VMEM((channels, (hops + 1) * width, rows), f32),
            pltpu.VMEM((3, span, size), f32),
        ],
        compiler_params=pltpu.CompilerParams(vmem_limit_bytes=48 * 1024 * 1024),
    )(place, left, right_blocks, cot_blocks, halo_blocks, weights, fold)


def body(left, right, kernel, cotangent):
    outs, levels, width, rows = cotangent.shape
    parts = lax.axis_size("disp")
    channels = C // parts
    groups = G // parts
    hops = (D + width - 2) // width
    part = lax.axis_index("disp")

    right_own = lax.dynamic_slice_in_dim(right, part * channels, channels, 0)
    right_blocks = lax.all_gather(right_own, "col")
    cot_blocks = lax.all_gather(cotangent, "disp")
    low = shifted(jnp.transpose(cotangent[:, :, width - 1], (1, 0, 2)), "col", 1)
    high = shifted(jnp.transpose(cotangent[:, :, 0], (1, 0, 2)), "col", -1)
    halo_blocks = lax.all_gather(jnp.concatenate([low, high], axis=1), "disp")

    left_own = lax.dynamic_slice_in_dim(left, part * channels, channels, 0)
    weights = toeplitz(lax.dynamic_slice_in_dim(kernel, part * groups, groups, 4), width)
    pad_rows = -(-3 * groups // 8) * 8
    fold = np.zeros((pad_rows, 3 * groups * width), np.float32)
    fold[np.arange(3 * groups * width) // width, np.arange(3 * groups * width)] = 1
    place = lax.axis_index("col").astype(jnp.int32)[None]
    results = run_work(
        place, left_own, right_blocks, cot_blocks, halo_blocks, weights, jnp.asarray(fold), hops
    )
    grad_left, own, sent, sums = results[0], results[1], results[2:-1], results[-1]

    sums = jnp.pad(sums, ((0, 0), (0, 0), (0, 128 - 3 * outs)))
    everyone = lax.all_gather(sums, ("col", "disp"))
    everyone = everyone.reshape(lax.axis_size("col"), parts, 3, pad_rows, 128)
    total = jnp.sum(everyone, axis=0)[:, :, : 3 * groups, : 3 * outs]
    total = total.reshape(parts, 3, 3, groups, 3, outs)
    cell_count = D * width * lax.axis_size("col") * rows
    grad_kernel = jnp.transpose(total, (4, 1, 2, 5, 0, 3))[::-1].reshape(3, 3, 3, outs, G)
    grad_kernel = grad_kernel * (1.0 / math.sqrt(cell_count))

    total_right = own
    for hop in range(1, hops + 1):
        total_right = total_right + shifted(sent[hop - 1], "col", -hop).astype(jnp.float32)
    return (grad_left, total_right.astype(jnp.bfloat16), grad_kernel)


def solution(mesh):
    return jax.shard_map(
        body,
        mesh=mesh,
        in_specs=(P(None, "col", None), P(None, "col", None), P(), P(None, "disp", "col", None)),
        out_specs=(P("disp", "col", None), P("disp", "col", None), P()),
        check_vma=False,
    )
```

```python
import functools
import math

import jax
import jax.numpy as jnp
import numpy as np
from jax import lax
from jax.experimental import pallas as pl
from jax.experimental.pallas import tpu as pltpu
from jax.sharding import PartitionSpec as P

C = 320
G = 40
D = 48
GROUP = C // G
HIGHEST = lax.Precision.HIGHEST


def shifted(value, axis, steps):
    count = lax.axis_size(axis)
    leading, last = (max(0, -steps), min(count, count - steps))
    return lax.ppermute(value, axis, [(source, source + steps) for source in range(leading, last)])


def conv_rows(outs, width):
    main = np.tile(np.arange(width), outs)
    return np.concatenate([main, np.full(outs, -1), np.full(outs, width)])


def toeplitz(kernel_local, width):
    outs, groups = kernel_local.shape[3:]
    row_col = conv_rows(outs, width)
    row_out = np.concatenate([np.repeat(np.arange(outs), width), np.tile(np.arange(outs), 2)])
    spread = np.zeros((outs, row_col.size), np.float32)
    spread[row_out, np.arange(row_col.size)] = 1
    taps = jnp.transpose(kernel_local[::-1], (1, 2, 4, 0, 3))
    wide = jnp.einsum(
        "qrgpo,ok->qrgpk", taps, jnp.asarray(spread, jnp.bfloat16),
        preferred_element_type=jnp.float32,
    ).astype(jnp.bfloat16)
    out_col = np.arange(width)
    column_tap = out_col[:, None] - row_col[None, :] + 1
    total = jnp.zeros((3, groups, width, 3, row_col.size), jnp.bfloat16)
    for tap in range(3):
        mask = jnp.asarray(column_tap == tap)[None, None, :, None, :]
        total = jnp.where(mask, wide[tap][:, :, None], total)
    return total.reshape(3 * groups * width, 3 * row_col.size)


def roll_zero(value, steps):
    size = value.shape[-1]
    lane = lax.broadcasted_iota(jnp.int32, value.shape, value.ndim - 1)
    moved = pltpu.roll(value, steps % size, value.ndim - 1)
    return jnp.where(lane == (0 if steps > 0 else size - 1), 0.0, moved)


def spread_grad_volume(places, *refs):
    count = (len(refs) - 3) // 2
    cot_refs, halo_refs = refs[:count], refs[count : 2 * count]
    weight_ref, cot_s, gv_s = refs[2 * count :]
    outs, levels, width, rows = cot_refs[0].shape
    main = outs * width
    span = cot_s.shape[1]
    size = gv_s.shape[1]
    f32, bf16 = jnp.float32, jnp.bfloat16

    cot_s[0] = jnp.zeros((span, rows), bf16)
    cot_s[D + 1] = jnp.zeros((span, rows), bf16)
    for other in range(count):
        start = (places[0] ^ other) * levels + 1

        def assemble(level, carry, other=other, start=start):
            value = cot_refs[other][:, level].astype(f32).reshape(main, rows)
            cot_s[start + level, 0:main] = value.astype(bf16)
            cot_s[start + level, main:span] = halo_refs[other][level]
            return carry

        lax.fori_loop(0, levels, assemble, 0)

    def grad_volume_step(pair, carry):
        first = pair * 2
        near = cot_s[pl.ds(first, 3)].reshape(3 * span, rows)
        far = cot_s[pl.ds(first + 1, 3)].reshape(3 * span, rows)
        result = jnp.dot(
            weight_ref[...], jnp.concatenate([near, far], axis=1), preferred_element_type=f32
        )
        for half in range(2):
            part = result[:, half * rows : (half + 1) * rows]
            total = (
                part[size : 2 * size]
                + roll_zero(part[:size], -1)
                + roll_zero(part[2 * size :], 1)
            )
            gv_s[first + half] = total.astype(bf16).astype(f32)
        return carry

    lax.fori_loop(0, D // 2, grad_volume_step, 0)


def load_right(places, right_ref, right_s, hops, width):
    reach = hops * width
    for hop in range(hops + 1):
        place = places[1] - hop
        block = right_ref[jnp.maximum(place, 0)].astype(jnp.float32)
        at = reach - hop * width
        right_s[:, at : at + width] = jnp.where(place >= 0, block, 0.0)


def feature_grads(hops, places, left_ref, right_ref, gv_s, grad_left_ref, own_ref, *rest):
    sent_refs, (right_out, right_s, grad_s) = rest[:hops], rest[hops:]
    channels, width, rows = left_ref.shape
    groups = channels // GROUP
    reach = hops * width
    f32, bf16 = jnp.float32, jnp.bfloat16
    load_right(places, right_ref, right_s, hops, width)
    grad_s[...] = jnp.zeros(grad_s.shape, f32)

    def grads_step(group, carry):
        first = group * GROUP
        lefts = [left_ref[first + k].astype(f32) for k in range(GROUP)]
        totals = [jnp.zeros((width, rows), f32) for k in range(GROUP)]
        rows_at = pl.ds(pl.multiple_of(group * width, width), width)
        for d in range(D):
            value = gv_s[d, rows_at]
            for k in range(GROUP):
                totals[k] = totals[k] + value * right_s[first + k, reach - d : reach - d + width]
                grad_s[first + k, reach - d : reach - d + width] += value * lefts[k]
        for k in range(GROUP):
            grad_left_ref[first + k] = (totals[k] * (1.0 / GROUP)).astype(bf16)
        return carry

    lax.fori_loop(0, groups, grads_step, 0)
    right_out[...] = right_s[...]
    own_ref[...] = grad_s[:, reach : reach + width] * (1.0 / GROUP)
    for hop in range(1, hops + 1):
        at = reach - hop * width
        sent_refs[hop - 1][...] = (grad_s[:, at : at + width] * (1.0 / GROUP)).astype(bf16)


def kernel_sums(left_ref, right_s, cot_s, fold_ref, sums_ref, vol_s, prod_s):
    channels, width, rows = left_ref.shape
    groups = channels // GROUP
    span = cot_s.shape[1]
    outs = span // (width + 2)
    main = outs * width
    reach = right_s.shape[1] - width
    f32, bf16 = jnp.float32, jnp.bfloat16

    def volume_step(group, carry):
        first = group * GROUP
        lefts = [left_ref[first + k].astype(f32) for k in range(GROUP)]
        rows_at = pl.ds(pl.multiple_of(group * width, width), width)
        for d in range(D):
            total = lefts[0] * right_s[first, reach - d : reach - d + width]
            for k in range(1, GROUP):
                total = total + lefts[k] * right_s[first + k, reach - d : reach - d + width]
            value = (total * (1.0 / GROUP)).astype(bf16).astype(f32)
            vol_s[d, 0, rows_at] = roll_zero(value, 1)
            vol_s[d, 1, rows_at] = value
            vol_s[d, 2, rows_at] = roll_zero(value, -1)
        return carry

    lax.fori_loop(0, groups, volume_step, 0)

    chunk = 4
    size = 3 * groups * width
    prod_s[...] = jnp.zeros(prod_s.shape, f32)

    def kernel_step(step, carry):
        first = step * chunk
        volume = jnp.concatenate(
            [vol_s[first + k].reshape(size, rows).astype(bf16) for k in range(chunk)], axis=1
        )
        for tap in range(3):
            value = jnp.concatenate([cot_s[first + k + tap] for k in range(chunk)], axis=1)
            prod_s[tap] += lax.dot_general(
                value, volume, (((1,), (1,)), ((), ())), preferred_element_type=f32
            )
        return carry

    lax.fori_loop(0, D // chunk, kernel_step, 0)

    col_in = lax.broadcasted_iota(jnp.int32, (width, size), 0)
    col_out = lax.broadcasted_iota(jnp.int32, (width, size), 1) % width
    edge = lax.broadcasted_iota(jnp.int32, (outs, size), 1) % width
    for column_tap in range(3):
        mask = col_out - col_in + 1 == column_tap
        parts = []
        for tap in range(3):
            value = prod_s[tap, 0:main].reshape(outs, width, size)
            total = jnp.sum(jnp.where(mask[None], value, 0.0), axis=1)
            if column_tap == 2:
                total = total + jnp.where(edge == 0, prod_s[tap, main : main + outs], 0.0)
            if column_tap == 0:
                total = total + jnp.where(edge == width - 1, prod_s[tap, main + outs : span], 0.0)
            parts.append(total)
        gathered = jnp.concatenate(parts, axis=0)
        sums_ref[column_tap] = lax.dot_general(
            fold_ref[...], gathered, (((1,), (1,)), ((), ())),
            precision=HIGHEST, preferred_element_type=f32,
        )


VMEM = pl.BlockSpec(memory_space=pltpu.VMEM)
SMEM = pl.BlockSpec(memory_space=pltpu.SMEM)
PARAMS = pltpu.CompilerParams(vmem_limit_bytes=40 * 1024 * 1024)


def run_grad_volume(places, cots, halos, weights):
    outs, levels, width, rows = cots[0].shape
    return pl.pallas_call(
        spread_grad_volume,
        out_shape=[
            jax.ShapeDtypeStruct((D + 2, outs * (width + 2), rows), jnp.bfloat16),
            jax.ShapeDtypeStruct((D, weights.shape[0] // 3, rows), jnp.float32),
        ],
        in_specs=[SMEM] + [VMEM] * (2 * len(cots) + 1),
        out_specs=[VMEM] * 2,
        compiler_params=PARAMS,
        cost_estimate=pl.CostEstimate(flops=4000000000, bytes_accessed=10000000, transcendentals=0),
    )(places, *cots, *halos, weights)


def run_feature_grads(places, left, right_blocks, grad_volume, hops):
    channels, width, rows = left.shape
    f32, bf16 = jnp.float32, jnp.bfloat16
    wide = (channels, (hops + 1) * width, rows)
    return pl.pallas_call(
        functools.partial(feature_grads, hops),
        out_shape=[
            jax.ShapeDtypeStruct((channels, width, rows), bf16),
            jax.ShapeDtypeStruct((channels, width, rows), f32),
            *[jax.ShapeDtypeStruct((channels, width, rows), bf16)] * hops,
            jax.ShapeDtypeStruct(wide, f32),
        ],
        in_specs=[SMEM] + [VMEM] * 3,
        out_specs=[VMEM] * (hops + 3),
        scratch_shapes=[pltpu.VMEM(wide, f32), pltpu.VMEM(wide, f32)],
        compiler_params=PARAMS,
        cost_estimate=pl.CostEstimate(flops=4000000000, bytes_accessed=10000000, transcendentals=0),
    )(places, left, right_blocks, grad_volume)


def run_kernel_sums(left, right_wide, cot_wide, fold):
    channels, width, rows = left.shape
    size = fold.shape[1]
    span = cot_wide.shape[1]
    f32 = jnp.float32
    return pl.pallas_call(
        kernel_sums,
        out_shape=jax.ShapeDtypeStruct((3, fold.shape[0], 3 * span // (width + 2)), f32),
        in_specs=[VMEM] * 4,
        out_specs=VMEM,
        scratch_shapes=[pltpu.VMEM((D, 3, size // 3, rows), f32), pltpu.VMEM((3, span, size), f32)],
        compiler_params=PARAMS,
        cost_estimate=pl.CostEstimate(flops=4000000000, bytes_accessed=10000000, transcendentals=0),
    )(left, right_wide, cot_wide, fold)


def swapped(value, axis, bit):
    count = lax.axis_size(axis)
    return lax.ppermute(value, axis, [(source, source ^ bit) for source in range(count)])


def gather_swapping(value, axis):
    held = {0: value}
    bit = lax.axis_size(axis) // 2
    while bit:
        held.update({key | bit: swapped(item, axis, bit) for key, item in list(held.items())})
        bit //= 2
    return [held[key] for key in range(len(held))]


def body(left, right, kernel, cotangent):
    outs, levels, width, rows = cotangent.shape
    parts = lax.axis_size("disp")
    channels = C // parts
    groups = G // parts
    hops = (D + width - 2) // width
    part = lax.axis_index("disp")
    places = jnp.stack([part, lax.axis_index("col")]).astype(jnp.int32)

    cots = gather_swapping(cotangent, "disp")
    right_own = lax.dynamic_slice_in_dim(right, part * channels, channels, 0)
    right_blocks = lax.all_gather(right_own, "col")
    low = shifted(jnp.transpose(cotangent[:, :, width - 1], (1, 0, 2)), "col", 1)
    high = shifted(jnp.transpose(cotangent[:, :, 0], (1, 0, 2)), "col", -1)
    halos = gather_swapping(jnp.concatenate([low, high], axis=1), "disp")

    left_own = lax.dynamic_slice_in_dim(left, part * channels, channels, 0)
    weights = toeplitz(lax.dynamic_slice_in_dim(kernel, part * groups, groups, 4), width)
    pad_rows = -(-3 * groups // 8) * 8
    fold = np.zeros((pad_rows, 3 * groups * width), np.float32)
    fold[np.arange(3 * groups * width) // width, np.arange(3 * groups * width)] = 1

    cot_wide, grad_volume = run_grad_volume(places, cots, halos, weights)
    results = run_feature_grads(places, left_own, right_blocks, grad_volume, hops)
    grad_left, own, sent, right_wide = results[0], results[1], results[2:-1], results[-1]
    sums = run_kernel_sums(left_own, right_wide, cot_wide, jnp.asarray(fold))

    sums = jnp.pad(sums, ((0, 0), (0, 0), (0, 128 - 3 * outs)))
    total = jnp.sum(lax.all_gather(sums, "col"), axis=0)
    total = lax.all_gather(total, "disp")[:, :, : 3 * groups, : 3 * outs]
    total = total.reshape(parts, 3, 3, groups, 3, outs)
    cell_count = D * width * lax.axis_size("col") * rows
    grad_kernel = jnp.transpose(total, (4, 1, 2, 5, 0, 3))[::-1].reshape(3, 3, 3, outs, G)
    grad_kernel = grad_kernel * (1.0 / math.sqrt(cell_count))

    total_right = own
    for hop in range(hops, 0, -1):
        total_right = total_right + shifted(sent[hop - 1], "col", -hop).astype(jnp.float32)
    return (grad_left, total_right.astype(jnp.bfloat16), grad_kernel)


def solution(mesh):
    return jax.shard_map(
        body,
        mesh=mesh,
        in_specs=(P(None, "col", None), P(None, "col", None), P(), P(None, "disp", "col", None)),
        out_specs=(P("disp", "col", None), P("disp", "col", None), P()),
        check_vma=False,
    )
```

```python
import functools
import math

import jax
import jax.numpy as jnp
import numpy as np
from jax import lax
from jax.experimental import pallas as pl
from jax.experimental.pallas import tpu as pltpu
from jax.sharding import PartitionSpec as P

C = 320
G = 40
D = 48
GROUP = C // G
HIGHEST = lax.Precision.HIGHEST


def shifted(value, axis, steps):
    count = lax.axis_size(axis)
    leading, last = (max(0, -steps), min(count, count - steps))
    return lax.ppermute(value, axis, [(source, source + steps) for source in range(leading, last)])


def conv_rows(outs, width):
    main = np.tile(np.arange(width), outs)
    return np.concatenate([main, np.full(outs, -1), np.full(outs, width)])


def toeplitz(kernel_local, width):
    outs, groups = kernel_local.shape[3:]
    row_col = conv_rows(outs, width)
    row_out = np.concatenate([np.repeat(np.arange(outs), width), np.tile(np.arange(outs), 2)])
    spread = np.zeros((outs, row_col.size), np.float32)
    spread[row_out, np.arange(row_col.size)] = 1
    taps = jnp.transpose(kernel_local[::-1], (1, 2, 4, 0, 3))
    wide = jnp.einsum(
        "qrgpo,ok->qrgpk", taps, jnp.asarray(spread, jnp.bfloat16),
        preferred_element_type=jnp.float32,
    ).astype(jnp.bfloat16)
    out_col = np.arange(width)
    column_tap = out_col[:, None] - row_col[None, :] + 1
    total = jnp.zeros((3, groups, width, 3, row_col.size), jnp.bfloat16)
    for tap in range(3):
        mask = jnp.asarray(column_tap == tap)[None, None, :, None, :]
        total = jnp.where(mask, wide[tap][:, :, None], total)
    return total.reshape(3 * groups * width, 3 * row_col.size)


def roll_zero(value, steps):
    size = value.shape[-1]
    lane = lax.broadcasted_iota(jnp.int32, value.shape, value.ndim - 1)
    moved = pltpu.roll(value, steps % size, value.ndim - 1)
    return jnp.where(lane == (0 if steps > 0 else size - 1), 0.0, moved)


def convolution_grads(parts, hops, places, *refs):
    cot_refs, halo_refs, refs = refs[:parts], refs[parts : 2 * parts], refs[2 * parts :]
    right_refs, refs = refs[: hops + 1], refs[hops + 1 :]
    left_ref, weight_ref, fold_ref, right_s, gv_s, sums_ref, cot_s, vol_s, prod_s = refs
    channels, width, rows = left_ref.shape
    groups = channels // GROUP
    outs, levels = cot_refs[0].shape[:2]
    main = outs * width
    span = main + 2 * outs
    size = groups * width
    reach = hops * width
    f32, bf16 = jnp.float32, jnp.bfloat16

    cot_s[0] = jnp.zeros((span, rows), bf16)
    cot_s[D + 1] = jnp.zeros((span, rows), bf16)
    for other in range(parts):
        start = (places[0] ^ other) * levels + 1

        def assemble(level, carry, other=other, start=start):
            value = cot_refs[other][:, level].reshape(main, rows)
            cot_s[start + level, 0:main] = value
            cot_s[start + level, main:span] = halo_refs[other][level]
            return carry

        lax.fori_loop(0, levels, assemble, 0)

    def grad_volume_step(pair, carry):
        first = pair * 2
        near = cot_s[pl.ds(first, 3)].reshape(3 * span, rows)
        far = cot_s[pl.ds(first + 1, 3)].reshape(3 * span, rows)
        result = jnp.dot(
            weight_ref[...], jnp.concatenate([near, far], axis=1), preferred_element_type=f32
        )
        for half in range(2):
            part = result[:, half * rows : (half + 1) * rows]
            total = (
                part[size : 2 * size]
                + roll_zero(part[:size], -1)
                + roll_zero(part[2 * size :], 1)
            )
            gv_s[first + half] = total.astype(bf16).astype(f32)
        return carry

    lax.fori_loop(0, D // 2, grad_volume_step, 0)

    for hop in range(hops + 1):
        at = reach - hop * width
        right_s[:, at : at + width] = right_refs[hop][...].astype(f32)

    def volume_step(group, carry):
        first = group * GROUP
        lefts = [left_ref[first + k].astype(f32) for k in range(GROUP)]
        rows_at = pl.ds(pl.multiple_of(group * width, width), width)
        for d in range(D):
            total = lefts[0] * right_s[first, reach - d : reach - d + width]
            for k in range(1, GROUP):
                total = total + lefts[k] * right_s[first + k, reach - d : reach - d + width]
            value = (total * (1.0 / GROUP)).astype(bf16).astype(f32)
            vol_s[d, 0, rows_at] = roll_zero(value, 1)
            vol_s[d, 1, rows_at] = value
            vol_s[d, 2, rows_at] = roll_zero(value, -1)
        return carry

    lax.fori_loop(0, groups, volume_step, 0)

    chunk = 4
    prod_s[...] = jnp.zeros(prod_s.shape, f32)

    def kernel_step(step, carry):
        first = step * chunk
        volume = jnp.concatenate(
            [vol_s[first + k].reshape(3 * size, rows).astype(bf16) for k in range(chunk)], axis=1
        )
        for tap in range(3):
            value = jnp.concatenate([cot_s[first + k + tap] for k in range(chunk)], axis=1)
            prod_s[tap] += lax.dot_general(
                value, volume, (((1,), (1,)), ((), ())), preferred_element_type=f32
            )
        return carry

    lax.fori_loop(0, D // chunk, kernel_step, 0)

    col_in = lax.broadcasted_iota(jnp.int32, (width, 3 * size), 0)
    col_out = lax.broadcasted_iota(jnp.int32, (width, 3 * size), 1) % width
    edge = lax.broadcasted_iota(jnp.int32, (outs, 3 * size), 1) % width
    for column_tap in range(3):
        mask = col_out - col_in + 1 == column_tap
        taps = []
        for tap in range(3):
            value = prod_s[tap, 0:main].reshape(outs, width, 3 * size)
            total = jnp.sum(jnp.where(mask[None], value, 0.0), axis=1)
            if column_tap == 2:
                total = total + jnp.where(edge == 0, prod_s[tap, main : main + outs], 0.0)
            if column_tap == 0:
                total = total + jnp.where(edge == width - 1, prod_s[tap, main + outs : span], 0.0)
            taps.append(total)
        gathered = jnp.concatenate(taps, axis=0)
        sums_ref[column_tap] = lax.dot_general(
            fold_ref[...], gathered, (((1,), (1,)), ((), ())),
            precision=HIGHEST, preferred_element_type=f32,
        )


def feature_grads(hops, left_ref, right_s, gv_s, grad_left_ref, own_ref, *rest):
    sent_refs, (grad_s,) = rest[:hops], rest[hops:]
    channels, width, rows = left_ref.shape
    groups = channels // GROUP
    reach = hops * width
    f32, bf16 = jnp.float32, jnp.bfloat16
    grad_s[...] = jnp.zeros(grad_s.shape, f32)

    def grads_step(group, carry):
        first = group * GROUP
        lefts = [left_ref[first + k].astype(f32) for k in range(GROUP)]
        totals = [jnp.zeros((width, rows), f32) for k in range(GROUP)]
        rows_at = pl.ds(pl.multiple_of(group * width, width), width)
        for d in range(D):
            value = gv_s[d, rows_at]
            for k in range(GROUP):
                totals[k] = totals[k] + value * right_s[first + k, reach - d : reach - d + width]
                grad_s[first + k, reach - d : reach - d + width] += value * lefts[k]
        for k in range(GROUP):
            grad_left_ref[first + k] = (totals[k] * (1.0 / GROUP)).astype(bf16)
        return carry

    lax.fori_loop(0, groups, grads_step, 0)
    own_ref[...] = grad_s[:, reach : reach + width] * (1.0 / GROUP)
    for hop in range(1, hops + 1):
        at = reach - hop * width
        sent_refs[hop - 1][...] = (grad_s[:, at : at + width] * (1.0 / GROUP)).astype(bf16)


VMEM = pl.BlockSpec(memory_space=pltpu.VMEM)
SMEM = pl.BlockSpec(memory_space=pltpu.SMEM)
MIB = 1024 * 1024


def run_convolution_grads(places, cots, halos, rights, left, weights, fold):
    outs, levels, width, rows = cots[0].shape
    channels = left.shape[0]
    size = fold.shape[1]
    span = outs * (width + 2)
    f32 = jnp.float32
    return pl.pallas_call(
        functools.partial(convolution_grads, len(cots), len(rights) - 1),
        out_shape=[
            jax.ShapeDtypeStruct((channels, len(rights) * width, rows), f32),
            jax.ShapeDtypeStruct((D, size // 3, rows), f32),
            jax.ShapeDtypeStruct((3, fold.shape[0], 3 * outs), f32),
        ],
        in_specs=[SMEM] + [VMEM] * (2 * len(cots) + len(rights) + 3),
        out_specs=[VMEM] * 3,
        scratch_shapes=[
            pltpu.VMEM((D + 2, span, rows), jnp.bfloat16),
            pltpu.VMEM((D, 3, size // 3, rows), f32),
            pltpu.VMEM((3, span, size), f32),
        ],
        compiler_params=pltpu.CompilerParams(vmem_limit_bytes=24 * MIB),
        cost_estimate=pl.CostEstimate(flops=8000000000, bytes_accessed=20000000, transcendentals=0),
    )(places, *cots, *halos, *rights, left, weights, fold)


def run_feature_grads(left, right_wide, grad_volume, hops):
    channels, width, rows = left.shape
    f32, bf16 = jnp.float32, jnp.bfloat16
    return pl.pallas_call(
        functools.partial(feature_grads, hops),
        out_shape=[
            jax.ShapeDtypeStruct((channels, width, rows), bf16),
            jax.ShapeDtypeStruct((channels, width, rows), f32),
            *[jax.ShapeDtypeStruct((channels, width, rows), bf16)] * hops,
        ],
        in_specs=[VMEM] * 3,
        out_specs=[VMEM] * (hops + 2),
        scratch_shapes=[pltpu.VMEM((channels, (hops + 1) * width, rows), f32)],
        compiler_params=pltpu.CompilerParams(vmem_limit_bytes=12 * MIB),
        cost_estimate=pl.CostEstimate(flops=4000000000, bytes_accessed=10000000, transcendentals=0),
    )(left, right_wide, grad_volume)


def swapped(value, axis, bit):
    count = lax.axis_size(axis)
    return lax.ppermute(value, axis, [(source, source ^ bit) for source in range(count)])


def gather_swapping(value, axis):
    held = {0: value}
    bit = lax.axis_size(axis) // 2
    while bit:
        held.update({key | bit: swapped(item, axis, bit) for key, item in list(held.items())})
        bit //= 2
    return [held[key] for key in range(len(held))]


def total_swapping(value, axis):
    bit = lax.axis_size(axis) // 2
    while bit:
        value = value + swapped(value, axis, bit)
        bit //= 2
    return value


def body(left, right, kernel, cotangent):
    outs, levels, width, rows = cotangent.shape
    parts = lax.axis_size("disp")
    channels = C // parts
    groups = G // parts
    hops = (D + width - 2) // width
    part = lax.axis_index("disp")
    places = part.astype(jnp.int32)[None]

    cots = gather_swapping(cotangent, "disp")
    low = shifted(jnp.transpose(cotangent[:, :, width - 1], (1, 0, 2)), "col", 1)
    high = shifted(jnp.transpose(cotangent[:, :, 0], (1, 0, 2)), "col", -1)
    halos = gather_swapping(jnp.concatenate([low, high], axis=1), "disp")
    right_own = lax.dynamic_slice_in_dim(right, part * channels, channels, 0)
    rights = [right_own] + [shifted(right_own, "col", hop) for hop in range(1, hops + 1)]

    left_own = lax.dynamic_slice_in_dim(left, part * channels, channels, 0)
    weights = toeplitz(lax.dynamic_slice_in_dim(kernel, part * groups, groups, 4), width)
    pad_rows = -(-3 * groups // 8) * 8
    fold = np.zeros((pad_rows, 3 * groups * width), np.float32)
    fold[np.arange(3 * groups * width) // width, np.arange(3 * groups * width)] = 1

    right_wide, grad_volume, sums = run_convolution_grads(
        places, cots, halos, rights, left_own, weights, jnp.asarray(fold)
    )
    results = run_feature_grads(left_own, right_wide, grad_volume, hops)
    grad_left, own, sent = results[0], results[1], results[2:]

    total = total_swapping(sums, "col")
    pieces = jnp.stack(gather_swapping(total, "disp"))
    pieces = pieces[jnp.arange(parts) ^ part][:, :, : 3 * groups]
    total = pieces.reshape(parts, 3, 3, groups, 3, outs)
    cell_count = D * width * lax.axis_size("col") * rows
    grad_kernel = jnp.transpose(total, (4, 1, 2, 5, 0, 3))[::-1].reshape(3, 3, 3, outs, G)
    grad_kernel = grad_kernel * (1.0 / math.sqrt(cell_count))

    total_right = own
    for hop in range(hops, 0, -1):
        total_right = total_right + shifted(sent[hop - 1], "col", -hop).astype(jnp.float32)
    return (grad_left, total_right.astype(jnp.bfloat16), grad_kernel)


def solution(mesh):
    return jax.shard_map(
        body,
        mesh=mesh,
        in_specs=(P(None, "col", None), P(None, "col", None), P(), P(None, "disp", "col", None)),
        out_specs=(P("disp", "col", None), P("disp", "col", None), P()),
        check_vma=False,
    )
```

```python
import functools
import math

import jax
import jax.numpy as jnp
import numpy as np
from jax import lax
from jax.experimental import pallas as pl
from jax.experimental.pallas import tpu as pltpu
from jax.sharding import PartitionSpec as P

C = 320
G = 40
D = 48
GROUP = C // G
HIGHEST = lax.Precision.HIGHEST


def shifted(value, axis, steps):
    count = lax.axis_size(axis)
    leading, last = (max(0, -steps), min(count, count - steps))
    return lax.ppermute(value, axis, [(source, source + steps) for source in range(leading, last)])


def toeplitz(kernel_local, width, row_out, row_col):
    outs, groups = kernel_local.shape[3:]
    spread = np.zeros((outs, row_col.size), np.float32)
    spread[row_out, np.arange(row_col.size)] = 1
    taps = jnp.transpose(kernel_local[::-1], (1, 2, 4, 0, 3))
    wide = jnp.einsum(
        "qrgpo,ok->qrgpk", taps, jnp.asarray(spread, jnp.bfloat16),
        preferred_element_type=jnp.float32,
    ).astype(jnp.bfloat16)
    column_tap = np.arange(width)[:, None] - row_col[None, :] + 1
    total = jnp.zeros((3, groups, width, 3, row_col.size), jnp.bfloat16)
    for tap in range(3):
        mask = jnp.asarray(column_tap == tap)[None, None, :, None, :]
        total = jnp.where(mask, wide[tap][:, :, None], total)
    return total.reshape(3 * groups * width, 3 * row_col.size)


def roll_zero(value, steps):
    size = value.shape[-1]
    lane = lax.broadcasted_iota(jnp.int32, value.shape, value.ndim - 1)
    moved = pltpu.roll(value, steps % size, value.ndim - 1)
    return jnp.where(lane == (0 if steps > 0 else size - 1), 0.0, moved)


def sum_row_taps(part, size):
    return (
        part[size : 2 * size]
        + roll_zero(part[:size], -1)
        + roll_zero(part[2 * size :], 1)
    )


def segment_grad_volume(places, first_ref, second_ref, weight_ref, cot_s, gv_s, low_ref, high_ref):
    outs, levels, width, rows = first_ref.shape
    main = outs * width
    size = gv_s.shape[1]
    f32, bf16 = jnp.float32, jnp.bfloat16
    second_first = places[0] & 1
    for edge in (0, 1, 2 * levels + 2, 2 * levels + 3):
        cot_s[edge] = jnp.zeros((main, rows), bf16)
    for ref, start in (
        (first_ref, second_first * levels),
        (second_ref, (1 - second_first) * levels),
    ):

        def assemble(level, carry, ref=ref, start=start):
            value = ref[:, level]
            cot_s[start + level + 2] = value.reshape(main, rows)
            wide = value.astype(f32)
            low_ref[start + level] = wide[:, width - 1].astype(bf16)
            high_ref[start + level] = wide[:, 0].astype(bf16)
            return carry

        lax.fori_loop(0, levels, assemble, 0)

    def step(pair, carry):
        at = pair * 2
        near = cot_s[pl.ds(at, 3)].reshape(3 * main, rows)
        far = cot_s[pl.ds(at + 1, 3)].reshape(3 * main, rows)
        result = jnp.dot(
            weight_ref[...], jnp.concatenate([near, far], axis=1), preferred_element_type=f32
        )
        for half in range(2):
            gv_s[at + half] = sum_row_taps(result[:, half * rows : (half + 1) * rows], size)
        return carry

    lax.fori_loop(0, levels + 1, step, 0)


def segment_start(places, segment, levels):
    return ((places[0] ^ (2 * segment)) & ~1) * levels


def fold_columns(fold_ref, value):
    return lax.dot_general(
        fold_ref[...], value, (((1,), (1,)), ((), ())),
        precision=HIGHEST, preferred_element_type=jnp.float32,
    )


def main_kernel_sums(segments, hops, places, *refs):
    seg_refs, refs = refs[:segments], refs[segments:]
    right_refs, refs = refs[: hops + 1], refs[hops + 1 :]
    left_ref, fold_ref, right_s, vol_out, sums_ref, cot_s, vol_s, prod_s = refs
    channels, width, rows = left_ref.shape
    groups = channels // GROUP
    levels = seg_refs[0].shape[0] // 2 - 2
    main = cot_s.shape[1]
    outs = main // width
    size = groups * width
    reach = hops * width
    f32, bf16 = jnp.float32, jnp.bfloat16

    for hop in range(hops + 1):
        at = reach - hop * width
        right_s[:, at : at + width] = right_refs[hop][...].astype(f32)

    cot_s[0] = jnp.zeros((main, rows), bf16)
    cot_s[D + 1] = jnp.zeros((main, rows), bf16)
    for segment in range(segments):
        start = segment_start(places, segment, levels)

        def move(level, carry, segment=segment, start=start):
            cot_s[start + level + 1] = seg_refs[segment][level + 2]
            return carry

        lax.fori_loop(0, 2 * levels, move, 0)

    def volume_step(group, carry):
        first = group * GROUP
        lefts = [left_ref[first + k].astype(f32) for k in range(GROUP)]
        rows_at = pl.ds(pl.multiple_of(group * width, width), width)
        for d in range(D):
            total = lefts[0] * right_s[first, reach - d : reach - d + width]
            for k in range(1, GROUP):
                total = total + lefts[k] * right_s[first + k, reach - d : reach - d + width]
            value = (total * (1.0 / GROUP)).astype(bf16).astype(f32)
            vol_s[d, 0, rows_at] = roll_zero(value, 1)
            vol_s[d, 1, rows_at] = value
            vol_s[d, 2, rows_at] = roll_zero(value, -1)
        return carry

    lax.fori_loop(0, groups, volume_step, 0)

    chunk = 4
    prod_s[...] = jnp.zeros(prod_s.shape, f32)

    def kernel_step(step, carry):
        first = step * chunk
        volumes = [vol_s[first + k].reshape(3 * size, rows).astype(bf16) for k in range(chunk)]
        for k in range(chunk):
            vol_out[first + k] = volumes[k]
        volume = jnp.concatenate(volumes, axis=1)
        for tap in range(3):
            value = jnp.concatenate([cot_s[first + k + tap] for k in range(chunk)], axis=1)
            prod_s[tap] += lax.dot_general(
                value, volume, (((1,), (1,)), ((), ())), preferred_element_type=f32
            )
        return carry

    lax.fori_loop(0, D // chunk, kernel_step, 0)

    col_in = lax.broadcasted_iota(jnp.int32, (width, 3 * size), 0)
    col_out = lax.broadcasted_iota(jnp.int32, (width, 3 * size), 1) % width
    for column_tap in range(3):
        mask = col_out - col_in + 1 == column_tap
        taps = []
        for tap in range(3):
            value = prod_s[tap].reshape(outs, width, 3 * size)
            taps.append(jnp.sum(jnp.where(mask[None], value, 0.0), axis=1))
        sums_ref[column_tap] = fold_columns(fold_ref, jnp.concatenate(taps, axis=0))


def halo_kernel_sums(segments, width, places, *refs):
    low_refs, high_refs, refs = refs[:segments], refs[segments : 2 * segments], refs[2 * segments :]
    vol_ref, part_ref, fold_ref, sums_ref, halo_s, prod_s = refs
    levels, outs, rows = low_refs[0].shape
    size = vol_ref.shape[1]
    f32, bf16 = jnp.float32, jnp.bfloat16
    halo_s[0] = jnp.zeros((2 * outs, rows), bf16)
    halo_s[D + 1] = jnp.zeros((2 * outs, rows), bf16)
    for segment in range(segments):
        start = segment_start(places, segment, levels // 2)

        def move(level, carry, segment=segment, start=start):
            halo_s[start + level + 1, 0:outs] = low_refs[segment][level]
            halo_s[start + level + 1, outs : 2 * outs] = high_refs[segment][level]
            return carry

        lax.fori_loop(0, levels, move, 0)

    chunk = 4
    prod_s[...] = jnp.zeros(prod_s.shape, f32)

    def kernel_step(step, carry):
        first = step * chunk
        volume = jnp.concatenate([vol_ref[first + k] for k in range(chunk)], axis=1)
        value = jnp.concatenate(
            [
                jnp.concatenate([halo_s[first + k + tap] for k in range(chunk)], axis=1)
                for tap in range(3)
            ],
            axis=0,
        )
        prod_s[...] += lax.dot_general(
            value, volume, (((1,), (1,)), ((), ())), preferred_element_type=f32
        )
        return carry

    lax.fori_loop(0, D // chunk, kernel_step, 0)

    edge = lax.broadcasted_iota(jnp.int32, (3 * outs, size), 1) % width
    lows = [prod_s[2 * tap * outs : (2 * tap + 1) * outs] for tap in range(3)]
    highs = [prod_s[(2 * tap + 1) * outs : (2 * tap + 2) * outs] for tap in range(3)]
    low = jnp.where(edge == 0, jnp.concatenate(lows, axis=0), 0.0)
    high = jnp.where(edge == width - 1, jnp.concatenate(highs, axis=0), 0.0)
    sums_ref[0] = part_ref[0] + fold_columns(fold_ref, high)
    sums_ref[1] = part_ref[1]
    sums_ref[2] = part_ref[2] + fold_columns(fold_ref, low)


def total_grad_volume(segments, places, *refs):
    part_refs, (halo_ref, weight_ref, gv_ref, sum_s) = refs[:segments], refs[segments:]
    levels = part_refs[0].shape[0] // 2 - 1
    rows = halo_ref.shape[2]
    span = halo_ref.shape[1]
    size = gv_ref.shape[1]
    f32, bf16 = jnp.float32, jnp.bfloat16
    sum_s[...] = jnp.zeros(sum_s.shape, f32)
    for segment in range(segments):
        start = segment_start(places, segment, levels)

        def move(level, carry, segment=segment, start=start):
            sum_s[start + level] += part_refs[segment][level]
            return carry

        lax.fori_loop(0, 2 * levels + 2, move, 0)

    def step(pair, carry):
        at = pair * 2
        near = halo_ref[pl.ds(at, 3)].reshape(3 * span, rows)
        far = halo_ref[pl.ds(at + 1, 3)].reshape(3 * span, rows)
        result = jnp.dot(
            weight_ref[...], jnp.concatenate([near, far], axis=1), preferred_element_type=f32
        )
        for half in range(2):
            total = sum_row_taps(result[:, half * rows : (half + 1) * rows], size)
            gv_ref[at + half] = (total + sum_s[at + half + 1]).astype(bf16).astype(f32)
        return carry

    lax.fori_loop(0, D // 2, step, 0)


def feature_grads(hops, left_ref, right_s, gv_s, grad_left_ref, own_ref, *rest):
    sent_refs, (grad_s,) = rest[:hops], rest[hops:]
    channels, width, rows = left_ref.shape
    groups = channels // GROUP
    reach = hops * width
    f32, bf16 = jnp.float32, jnp.bfloat16
    grad_s[...] = jnp.zeros(grad_s.shape, f32)

    def grads_step(group, carry):
        first = group * GROUP
        lefts = [left_ref[first + k].astype(f32) for k in range(GROUP)]
        totals = [jnp.zeros((width, rows), f32) for k in range(GROUP)]
        rows_at = pl.ds(pl.multiple_of(group * width, width), width)
        for d in range(D):
            value = gv_s[d, rows_at]
            for k in range(GROUP):
                totals[k] = totals[k] + value * right_s[first + k, reach - d : reach - d + width]
                grad_s[first + k, reach - d : reach - d + width] += value * lefts[k]
        for k in range(GROUP):
            grad_left_ref[first + k] = (totals[k] * (1.0 / GROUP)).astype(bf16)
        return carry

    lax.fori_loop(0, groups, grads_step, 0)
    own_ref[...] = grad_s[:, reach : reach + width] * (1.0 / GROUP)
    for hop in range(1, hops + 1):
        at = reach - hop * width
        sent_refs[hop - 1][...] = (grad_s[:, at : at + width] * (1.0 / GROUP)).astype(bf16)


VMEM = pl.BlockSpec(memory_space=pltpu.VMEM)
SMEM = pl.BlockSpec(memory_space=pltpu.SMEM)
MIB = 1024 * 1024


def run(function, places, operands, outs, scratch, limit, flops):
    return pl.pallas_call(
        function,
        out_shape=[jax.ShapeDtypeStruct(shape, kind) for shape, kind in outs],
        in_specs=[SMEM] + [VMEM] * len(operands),
        out_specs=[VMEM] * len(outs),
        scratch_shapes=[pltpu.VMEM(shape, kind) for shape, kind in scratch],
        compiler_params=pltpu.CompilerParams(vmem_limit_bytes=limit * MIB),
        cost_estimate=pl.CostEstimate(flops=flops, bytes_accessed=4 * MIB, transcendentals=0),
    )(places, *operands)


def run_feature_grads(left, right_wide, grad_volume, hops):
    channels, width, rows = left.shape
    f32, bf16 = jnp.float32, jnp.bfloat16
    return pl.pallas_call(
        functools.partial(feature_grads, hops),
        out_shape=[
            jax.ShapeDtypeStruct((channels, width, rows), bf16),
            jax.ShapeDtypeStruct((channels, width, rows), f32),
            *[jax.ShapeDtypeStruct((channels, width, rows), bf16)] * hops,
        ],
        in_specs=[VMEM] * 3,
        out_specs=[VMEM] * (hops + 2),
        scratch_shapes=[pltpu.VMEM((channels, (hops + 1) * width, rows), f32)],
        compiler_params=pltpu.CompilerParams(vmem_limit_bytes=12 * MIB),
        cost_estimate=pl.CostEstimate(flops=4000000000, bytes_accessed=10000000, transcendentals=0),
    )(left, right_wide, grad_volume)


def swapped(value, axis, bit):
    count = lax.axis_size(axis)
    return lax.ppermute(value, axis, [(source, source ^ bit) for source in range(count)])


def gather_swapping(value, axis):
    held = {0: value}
    bit = lax.axis_size(axis) // 2
    while bit:
        held.update({key | bit: swapped(item, axis, bit) for key, item in list(held.items())})
        bit //= 2
    return [held[key] for key in range(len(held))]


def body(left, right, kernel, cotangent):
    outs, levels, width, rows = cotangent.shape
    parts = lax.axis_size("disp")
    channels = C // parts
    groups = G // parts
    hops = (D + width - 2) // width
    segments = parts // 2
    size = groups * width
    main = outs * width
    f32, bf16 = jnp.float32, jnp.bfloat16
    part = lax.axis_index("disp")
    places = part.astype(jnp.int32)[None]

    cots = gather_swapping(cotangent, "disp")
    right_own = lax.dynamic_slice_in_dim(right, part * channels, channels, 0)
    rights = [right_own] + [shifted(right_own, "col", hop) for hop in range(1, hops + 1)]

    left_own = lax.dynamic_slice_in_dim(left, part * channels, channels, 0)
    kernel_own = lax.dynamic_slice_in_dim(kernel, part * groups, groups, 4)
    channel = np.arange(outs)
    weights = toeplitz(
        kernel_own, width, np.repeat(channel, width), np.tile(np.arange(width), outs)
    )
    halo_weights = toeplitz(
        kernel_own, width, np.tile(channel, 2), np.repeat(np.array([-1, width]), outs)
    )
    pad_rows = -(-3 * groups // 8) * 8
    fold = np.zeros((pad_rows, 3 * size), np.float32)
    fold[np.arange(3 * size) // width, np.arange(3 * size)] = 1
    fold = jnp.asarray(fold)

    edge = ((2 * levels, outs, rows), bf16)
    spread = [
        run(
            segment_grad_volume, places, [cots[2 * k], cots[2 * k + 1], weights],
            [
                ((2 * levels + 4, main, rows), bf16),
                ((2 * levels + 2, size, rows), f32),
                edge, edge,
            ],
            [], 8, 2000000000,
        )
        for k in range(segments)
    ]
    lows = [shifted(item[2], "col", 1) for item in spread]
    highs = [shifted(item[3], "col", -1) for item in spread]

    right_wide, volume, main_sums = run(
        functools.partial(main_kernel_sums, segments, hops), places,
        [item[0] for item in spread] + rights + [left_own, fold],
        [
            ((channels, (hops + 1) * width, rows), f32),
            ((D, 3 * size, rows), bf16),
            ((3, pad_rows, 3 * outs), f32),
        ],
        [
            ((D + 2, main, rows), bf16),
            ((D, 3, size, rows), f32),
            ((3, main, 3 * size), f32),
        ],
        16, 4000000000,
    )
    sums, halo_wide = run(
        functools.partial(halo_kernel_sums, segments, width), places,
        lows + highs + [volume, main_sums, fold],
        [((3, pad_rows, 3 * outs), f32), ((D + 2, 2 * outs, rows), bf16)],
        [((6 * outs, 3 * size), f32)],
        8, 1000000000,
    )
    (grad_volume,) = run(
        functools.partial(total_grad_volume, segments), places,
        [item[1] for item in spread] + [halo_wide, halo_weights],
        [((D, size, rows), f32)], [((D + 2, size, rows), f32)], 8, 1000000000,
    )

    bit = lax.axis_size("col") // 2
    total = sums + swapped(sums, "col", bit)
    grad_volume, total = lax.optimization_barrier((grad_volume, total))
    bit //= 2
    results = run_feature_grads(left_own, right_wide, grad_volume, hops)
    grad_left, own, sent = results[0], results[1], results[2:]
    total = total + swapped(total, "col", bit)
    bit //= 2
    arrived = {hop: shifted(sent[hop - 1], "col", -hop) for hop in range(1, hops + 1)}
    total, arrived[1] = lax.optimization_barrier((total, arrived[1]))
    while bit:
        total = total + swapped(total, "col", bit)
        bit //= 2
    pieces = jnp.stack(gather_swapping(total, "disp"))
    pieces = pieces[jnp.arange(parts) ^ part][:, :, : 3 * groups]
    total = pieces.reshape(parts, 3, 3, groups, 3, outs)
    cell_count = D * width * lax.axis_size("col") * rows
    grad_kernel = jnp.transpose(total, (4, 1, 2, 5, 0, 3))[::-1].reshape(3, 3, 3, outs, G)
    grad_kernel = grad_kernel * (1.0 / math.sqrt(cell_count))

    total_right = own
    for hop in range(1, hops + 1):
        total_right = total_right + arrived[hop].astype(f32)
    return (grad_left, total_right.astype(bf16), grad_kernel)


def solution(mesh):
    return jax.shard_map(
        body,
        mesh=mesh,
        in_specs=(P(None, "col", None), P(None, "col", None), P(), P(None, "disp", "col", None)),
        out_specs=(P("disp", "col", None), P("disp", "col", None), P()),
        check_vma=False,
    )
```

```python
import functools
import math

import jax
import jax.numpy as jnp
import numpy as np
from jax import lax
from jax.experimental import pallas as pl
from jax.experimental.pallas import tpu as pltpu
from jax.sharding import PartitionSpec as P

C = 320
G = 40
D = 48
GROUP = C // G
HIGHEST = lax.Precision.HIGHEST


def shifted(value, axis, steps):
    count = lax.axis_size(axis)
    return lax.ppermute(value, axis, [(source, (source + steps) % count) for source in range(count)])


def conv_rows(outs, width):
    main = np.tile(np.arange(width), outs)
    return np.concatenate([main, np.full(outs, -1), np.full(outs, width)])


def toeplitz(kernel_local, width):
    outs, groups = kernel_local.shape[3:]
    row_col = conv_rows(outs, width)
    row_out = np.concatenate([np.repeat(np.arange(outs), width), np.tile(np.arange(outs), 2)])
    spread = np.zeros((outs, row_col.size), np.float32)
    spread[row_out, np.arange(row_col.size)] = 1
    taps = jnp.transpose(kernel_local[::-1], (1, 2, 4, 0, 3))
    wide = jnp.einsum(
        "qrgpo,ok->qrgpk", taps, jnp.asarray(spread, jnp.bfloat16),
        preferred_element_type=jnp.float32,
    ).astype(jnp.bfloat16)
    out_col = np.arange(width)
    column_tap = out_col[:, None] - row_col[None, :] + 1
    total = jnp.zeros((3, groups, width, 3, row_col.size), jnp.bfloat16)
    for tap in range(3):
        mask = jnp.asarray(column_tap == tap)[None, None, :, None, :]
        total = jnp.where(mask, wide[tap][:, :, None], total)
    return total.reshape(3 * groups * width, 3 * row_col.size)


def roll_zero(value, steps):
    size = value.shape[-1]
    lane = lax.broadcasted_iota(jnp.int32, value.shape, value.ndim - 1)
    moved = pltpu.roll(value, steps % size, value.ndim - 1)
    return jnp.where(lane == (0 if steps > 0 else size - 1), 0.0, moved)


def kernel_sums(parts, hops, places, *refs):
    cot_refs, halo_refs, refs = refs[:parts], refs[parts : 2 * parts], refs[2 * parts :]
    right_refs, refs = refs[: hops + 1], refs[hops + 1 :]
    left_ref, fold_ref, cot_s, right_s, sums_ref = refs[:5]
    cot_b, halo_b, right_b, vol_s, prod_s, sems = refs[5:]
    channels, width, rows = left_ref.shape
    groups = channels // GROUP
    outs, levels = cot_refs[0].shape[:2]
    main = outs * width
    span = main + 2 * outs
    size = groups * width
    reach = hops * width
    f32, bf16 = jnp.float32, jnp.bfloat16

    copies = []
    for buffer, sources in ((right_b, right_refs), (cot_b, cot_refs), (halo_b, halo_refs)):
        for at, source in enumerate(sources):
            copies.append(
                pltpu.make_async_copy(source, buffer.at[at], sems.at[len(copies)])
            )
    for copy in copies:
        copy.start()

    cot_s[0] = jnp.zeros((span, rows), bf16)
    cot_s[D + 1] = jnp.zeros((span, rows), bf16)
    for hop in range(hops + 1):
        copies[hop].wait()
        at = reach - hop * width
        block = right_b[hop].astype(f32)
        right_s[:, at : at + width] = jnp.where(places[1] >= hop, block, 0.0)

    def volume_step(group, carry):
        first = group * GROUP
        lefts = [left_ref[first + k].astype(f32) for k in range(GROUP)]
        rows_at = pl.ds(pl.multiple_of(group * width, width), width)
        for d in range(D):
            total = lefts[0] * right_s[first, reach - d : reach - d + width]
            for k in range(1, GROUP):
                total = total + lefts[k] * right_s[first + k, reach - d : reach - d + width]
            value = (total * (1.0 / GROUP)).astype(bf16).astype(f32)
            vol_s[d, 0, rows_at] = roll_zero(value, 1)
            vol_s[d, 1, rows_at] = value
            vol_s[d, 2, rows_at] = roll_zero(value, -1)
        return carry

    lax.fori_loop(0, groups, volume_step, 0)

    for copy in copies[hops + 1 :]:
        copy.wait()
    for other in range(parts):
        start = (places[0] ^ other) * levels + 1

        def assemble(level, carry, other=other, start=start):
            cot_s[start + level, 0:main] = cot_b[other, :, level].reshape(main, rows)
            cot_s[start + level, main:span] = halo_b[other, level]
            return carry

        lax.fori_loop(0, levels, assemble, 0)

    chunk = 4
    prod_s[...] = jnp.zeros(prod_s.shape, f32)

    def kernel_step(step, carry):
        first = step * chunk
        volume = jnp.concatenate(
            [vol_s[first + k].reshape(3 * size, rows).astype(bf16) for k in range(chunk)], axis=1
        )
        for tap in range(3):
            value = jnp.concatenate([cot_s[first + k + tap] for k in range(chunk)], axis=1)
            prod_s[tap] += lax.dot_general(
                value, volume, (((1,), (1,)), ((), ())), preferred_element_type=f32
            )
        return carry

    lax.fori_loop(0, D // chunk, kernel_step, 0)

    col_in = lax.broadcasted_iota(jnp.int32, (width, 3 * size), 0)
    col_out = lax.broadcasted_iota(jnp.int32, (width, 3 * size), 1) % width
    edge = lax.broadcasted_iota(jnp.int32, (outs, 3 * size), 1) % width
    for column_tap in range(3):
        mask = col_out - col_in + 1 == column_tap
        taps = []
        for tap in range(3):
            value = prod_s[tap, 0:main].reshape(outs, width, 3 * size)
            total = jnp.sum(jnp.where(mask[None], value, 0.0), axis=1)
            if column_tap == 2:
                total = total + jnp.where(edge == 0, prod_s[tap, main : main + outs], 0.0)
            if column_tap == 0:
                total = total + jnp.where(edge == width - 1, prod_s[tap, main + outs : span], 0.0)
            taps.append(total)
        gathered = jnp.concatenate(taps, axis=0)
        sums_ref[column_tap] = lax.dot_general(
            fold_ref[...], gathered, (((1,), (1,)), ((), ())),
            precision=HIGHEST, preferred_element_type=f32,
        )


def grad_volume_levels(first_level, cot_s, weight_ref, gv_s):
    count, size, rows = gv_s.shape
    span = cot_s.shape[1]

    def step(pair, carry):
        at = first_level + pair * 2
        near = cot_s[pl.ds(at, 3)].reshape(3 * span, rows)
        far = cot_s[pl.ds(at + 1, 3)].reshape(3 * span, rows)
        result = jnp.dot(
            weight_ref[...], jnp.concatenate([near, far], axis=1),
            preferred_element_type=jnp.float32,
        )
        for half in range(2):
            part = result[:, half * rows : (half + 1) * rows]
            total = (
                part[size : 2 * size]
                + roll_zero(part[:size], -1)
                + roll_zero(part[2 * size :], 1)
            )
            gv_s[pair * 2 + half] = total.astype(jnp.bfloat16).astype(jnp.float32)
        return carry

    lax.fori_loop(0, count // 2, step, 0)


def feature_grads(hops, pieces, left_ref, right_s, *refs):
    gv_refs, (grad_left_ref, own_ref, *rest) = refs[:pieces], refs[pieces:]
    sent_refs, (grad_s,) = rest[:hops], rest[hops:]
    held = gv_refs[0].shape[0]
    channels, width, rows = left_ref.shape
    groups = channels // GROUP
    reach = hops * width
    f32, bf16 = jnp.float32, jnp.bfloat16
    grad_s[...] = jnp.zeros(grad_s.shape, f32)

    def grads_step(group, carry):
        first = group * GROUP
        lefts = [left_ref[first + k].astype(f32) for k in range(GROUP)]
        totals = [jnp.zeros((width, rows), f32) for k in range(GROUP)]
        rows_at = pl.ds(pl.multiple_of(group * width, width), width)
        for d in range(D):
            value = gv_refs[d // held][d % held, rows_at]
            for k in range(GROUP):
                totals[k] = totals[k] + value * right_s[first + k, reach - d : reach - d + width]
                grad_s[first + k, reach - d : reach - d + width] += value * lefts[k]
        for k in range(GROUP):
            grad_left_ref[first + k] = (totals[k] * (1.0 / GROUP)).astype(bf16)
        return carry

    lax.fori_loop(0, groups, grads_step, 0)
    own_ref[...] = grad_s[:, reach : reach + width] * (1.0 / GROUP)
    for hop in range(1, hops + 1):
        at = reach - hop * width
        sent_refs[hop - 1][...] = (grad_s[:, at : at + width] * (1.0 / GROUP)).astype(bf16)


VMEM = pl.BlockSpec(memory_space=pltpu.VMEM)
SMEM = pl.BlockSpec(memory_space=pltpu.SMEM)
ANY = pl.BlockSpec(memory_space=pl.ANY)
MIB = 1024 * 1024


def cost(flops):
    return pl.CostEstimate(flops=flops, bytes_accessed=4 * MIB, transcendentals=0)


def run_kernel_sums(places, cots, halos, rights, left, fold):
    outs, levels, width, rows = cots[0].shape
    channels = left.shape[0]
    size = fold.shape[1]
    span = outs * (width + 2)
    f32, bf16 = jnp.float32, jnp.bfloat16
    moved = [*cots, *halos, *rights]
    return pl.pallas_call(
        functools.partial(kernel_sums, len(cots), len(rights) - 1),
        out_shape=[
            jax.ShapeDtypeStruct((D + 2, span, rows), bf16),
            jax.ShapeDtypeStruct((channels, len(rights) * width, rows), f32),
            jax.ShapeDtypeStruct((3, fold.shape[0], 3 * outs), f32),
        ],
        in_specs=[SMEM] + [ANY] * len(moved) + [VMEM] * 2,
        out_specs=[VMEM] * 3,
        scratch_shapes=[
            pltpu.VMEM((len(cots), *cots[0].shape), bf16),
            pltpu.VMEM((len(halos), *halos[0].shape), bf16),
            pltpu.VMEM((len(rights), *rights[0].shape), bf16),
            pltpu.VMEM((D, 3, size // 3, rows), f32),
            pltpu.VMEM((3, span, size), f32),
            pltpu.SemaphoreType.DMA((len(moved),)),
        ],
        compiler_params=pltpu.CompilerParams(vmem_limit_bytes=20 * MIB),
        cost_estimate=cost(8000000000),
    )(places, *moved, left, fold)


def run_grad_volume(cot_wide, weights, first_level, count):
    size, rows = weights.shape[0] // 3, cot_wide.shape[2]
    return pl.pallas_call(
        functools.partial(grad_volume_levels, first_level),
        out_shape=jax.ShapeDtypeStruct((count, size, rows), jnp.float32),
        in_specs=[VMEM] * 2,
        out_specs=VMEM,
        compiler_params=pltpu.CompilerParams(vmem_limit_bytes=8 * MIB),
        cost_estimate=cost(4000000000),
    )(cot_wide, weights)


def run_feature_grads(left, right_wide, grad_volumes, hops):
    channels, width, rows = left.shape
    f32, bf16 = jnp.float32, jnp.bfloat16
    return pl.pallas_call(
        functools.partial(feature_grads, hops, len(grad_volumes)),
        out_shape=[
            jax.ShapeDtypeStruct((channels, width, rows), bf16),
            jax.ShapeDtypeStruct((channels, width, rows), f32),
            *[jax.ShapeDtypeStruct((channels, width, rows), bf16)] * hops,
        ],
        in_specs=[VMEM] * (2 + len(grad_volumes)),
        out_specs=[VMEM] * (hops + 2),
        scratch_shapes=[pltpu.VMEM((channels, (hops + 1) * width, rows), f32)],
        compiler_params=pltpu.CompilerParams(vmem_limit_bytes=8 * MIB),
        cost_estimate=cost(4000000000),
    )(left, right_wide, *grad_volumes)


def swapped(value, axis, bit):
    count = lax.axis_size(axis)
    return lax.ppermute(value, axis, [(source, source ^ bit) for source in range(count)])


def gather_swapping(value, axis):
    held = {0: value}
    bit = lax.axis_size(axis) // 2
    while bit:
        held.update({key | bit: swapped(item, axis, bit) for key, item in list(held.items())})
        bit //= 2
    return [held[key] for key in range(len(held))]


def total_swapping(value, bit):
    return value + swapped(value, "col", bit)


def body(left, right, kernel, cotangent):
    outs, levels, width, rows = cotangent.shape
    parts = lax.axis_size("disp")
    columns = lax.axis_size("col")
    channels = C // parts
    groups = G // parts
    hops = (D + width - 2) // width
    part, column = lax.axis_index("disp"), lax.axis_index("col")
    places = jnp.stack([part, column]).astype(jnp.int32)
    f32, bf16 = jnp.float32, jnp.bfloat16

    cots = gather_swapping(cotangent, "disp")
    low = shifted(jnp.transpose(cotangent[:, :, width - 1], (1, 0, 2)), "col", 1)
    high = shifted(jnp.transpose(cotangent[:, :, 0], (1, 0, 2)), "col", -1)
    low = jnp.where(column > 0, low, 0).astype(bf16)
    high = jnp.where(column < columns - 1, high, 0).astype(bf16)
    halos = gather_swapping(jnp.concatenate([low, high], axis=1), "disp")
    right_own = lax.dynamic_slice_in_dim(right, part * channels, channels, 0)
    rights = [right_own] + [shifted(right_own, "col", hop) for hop in range(1, hops + 1)]

    left_own = lax.dynamic_slice_in_dim(left, part * channels, channels, 0)
    weights = toeplitz(lax.dynamic_slice_in_dim(kernel, part * groups, groups, 4), width)
    pad_rows = -(-3 * groups // 8) * 8
    fold = np.zeros((pad_rows, 3 * groups * width), np.float32)
    fold[np.arange(3 * groups * width) // width, np.arange(3 * groups * width)] = 1

    cot_wide, right_wide, total = run_kernel_sums(
        places, cots, halos, rights, left_own, jnp.asarray(fold)
    )
    bits = [1 << k for k in reversed(range(columns.bit_length() - 1))]
    first_half = run_grad_volume(cot_wide, weights, 0, D // 2)
    total = total_swapping(total, bits[0])
    cot_wide, first_half, total = lax.optimization_barrier((cot_wide, first_half, total))
    second_half = run_grad_volume(cot_wide, weights, D // 2, D // 2)
    total = total_swapping(total, bits[1])
    second_half, total = lax.optimization_barrier((second_half, total))
    results = run_feature_grads(left_own, right_wide, [first_half, second_half], hops)
    for bit in bits[2:]:
        total = total_swapping(total, bit)
    *results, total = lax.optimization_barrier((*results, total))
    grad_left, own, sent = results[0], results[1], results[2:]

    total_right = own
    for hop in range(hops, 0, -1):
        arrived = shifted(sent[hop - 1], "col", -hop).astype(f32)
        total_right = total_right + jnp.where(column + hop < columns, arrived, 0.0)

    pieces = jnp.stack(gather_swapping(total, "disp"))
    pieces = pieces[jnp.arange(parts) ^ part][:, :, : 3 * groups]
    total = pieces.reshape(parts, 3, 3, groups, 3, outs)
    cell_count = D * width * columns * rows
    grad_kernel = jnp.transpose(total, (4, 1, 2, 5, 0, 3))[::-1].reshape(3, 3, 3, outs, G)
    grad_kernel = grad_kernel * (1.0 / math.sqrt(cell_count))
    return (grad_left, total_right.astype(bf16), grad_kernel)


def solution(mesh):
    return jax.shard_map(
        body,
        mesh=mesh,
        in_specs=(P(None, "col", None), P(None, "col", None), P(), P(None, "disp", "col", None)),
        out_specs=(P("disp", "col", None), P("disp", "col", None), P()),
        check_vma=False,
    )
```

```python
import functools
import math

import jax
import jax.numpy as jnp
import numpy as np
from jax import lax
from jax.experimental import pallas as pl
from jax.experimental.pallas import tpu as pltpu
from jax.sharding import PartitionSpec as P

C = 320
G = 40
D = 48
GROUP = C // G
HIGHEST = lax.Precision.HIGHEST


def shifted(value, axis, steps):
    count = lax.axis_size(axis)
    return lax.ppermute(value, axis, [(source, (source + steps) % count) for source in range(count)])


def conv_rows(outs, width):
    main = np.tile(np.arange(width), outs)
    return np.concatenate([main, np.full(outs, -1), np.full(outs, width)])


def toeplitz(kernel_local, width):
    outs, groups = kernel_local.shape[3:]
    row_col = conv_rows(outs, width)
    row_out = np.concatenate([np.repeat(np.arange(outs), width), np.tile(np.arange(outs), 2)])
    spread = np.zeros((outs, row_col.size), np.float32)
    spread[row_out, np.arange(row_col.size)] = 1
    taps = jnp.transpose(kernel_local[::-1], (1, 2, 4, 0, 3))
    wide = jnp.einsum(
        "qrgpo,ok->qrgpk", taps, jnp.asarray(spread, jnp.bfloat16),
        preferred_element_type=jnp.float32,
    ).astype(jnp.bfloat16)
    out_col = np.arange(width)
    column_tap = out_col[:, None] - row_col[None, :] + 1
    total = jnp.zeros((3, groups, width, 3, row_col.size), jnp.bfloat16)
    for tap in range(3):
        mask = jnp.asarray(column_tap == tap)[None, None, :, None, :]
        total = jnp.where(mask, wide[tap][:, :, None], total)
    return total.reshape(3 * groups * width, 3 * row_col.size)


def roll_zero(value, steps):
    size = value.shape[-1]
    lane = lax.broadcasted_iota(jnp.int32, value.shape, value.ndim - 1)
    moved = pltpu.roll(value, steps % size, value.ndim - 1)
    return jnp.where(lane == (0 if steps > 0 else size - 1), 0.0, moved)


def kernel_sums(parts, hops, halo_order, places, *refs):
    cot_refs, halo_ref, refs = refs[:parts], refs[parts], refs[parts + 1 :]
    right_refs, refs = refs[: hops + 1], refs[hops + 1 :]
    left_ref, fold_ref, cot_s, right_s, sums_ref = refs[:5]
    cot_b, halo_b, right_b, vol_s, prod_s, sems = refs[5:]
    channels, width, rows = left_ref.shape
    groups = channels // GROUP
    outs, levels = cot_refs[0].shape[:2]
    main = outs * width
    span = main + 2 * outs
    size = groups * width
    reach = hops * width
    f32, bf16 = jnp.float32, jnp.bfloat16

    copies = []
    for buffer, sources in ((right_b, right_refs), (cot_b, cot_refs)):
        for at, source in enumerate(sources):
            copies.append(
                pltpu.make_async_copy(source, buffer.at[at], sems.at[len(copies)])
            )
    copies.append(pltpu.make_async_copy(halo_ref, halo_b, sems.at[len(copies)]))
    for copy in copies:
        copy.start()

    cot_s[0] = jnp.zeros((span, rows), bf16)
    cot_s[D + 1] = jnp.zeros((span, rows), bf16)
    for hop in range(hops + 1):
        copies[hop].wait()
        at = reach - hop * width
        block = right_b[hop].astype(f32)
        right_s[:, at : at + width] = jnp.where(places[1] >= hop, block, 0.0)

    def volume_step(group, carry):
        first = group * GROUP
        lefts = [left_ref[first + k].astype(f32) for k in range(GROUP)]
        rows_at = pl.ds(pl.multiple_of(group * width, width), width)
        for d in range(D):
            total = lefts[0] * right_s[first, reach - d : reach - d + width]
            for k in range(1, GROUP):
                total = total + lefts[k] * right_s[first + k, reach - d : reach - d + width]
            value = (total * (1.0 / GROUP)).astype(bf16).astype(f32)
            vol_s[d, 0, rows_at] = roll_zero(value, 1)
            vol_s[d, 1, rows_at] = value
            vol_s[d, 2, rows_at] = roll_zero(value, -1)
        return carry

    lax.fori_loop(0, groups, volume_step, 0)

    for copy in copies[hops + 1 :]:
        copy.wait()
    for other in range(parts):
        start = (places[0] ^ other) * levels + 1

        def assemble(level, carry, other=other, start=start):
            cot_s[start + level, 0:main] = cot_b[other, :, level].reshape(main, rows)
            cot_s[start + level, main:span] = halo_b[halo_order.index(other), level]
            return carry

        lax.fori_loop(0, levels, assemble, 0)

    chunk = 4
    prod_s[...] = jnp.zeros(prod_s.shape, f32)

    def kernel_step(step, carry):
        first = step * chunk
        volume = jnp.concatenate(
            [vol_s[first + k].reshape(3 * size, rows).astype(bf16) for k in range(chunk)], axis=1
        )
        for tap in range(3):
            value = jnp.concatenate([cot_s[first + k + tap] for k in range(chunk)], axis=1)
            prod_s[tap] += lax.dot_general(
                value, volume, (((1,), (1,)), ((), ())), preferred_element_type=f32
            )
        return carry

    lax.fori_loop(0, D // chunk, kernel_step, 0)

    col_in = lax.broadcasted_iota(jnp.int32, (width, 3 * size), 0)
    col_out = lax.broadcasted_iota(jnp.int32, (width, 3 * size), 1) % width
    edge = lax.broadcasted_iota(jnp.int32, (outs, 3 * size), 1) % width
    for column_tap in range(3):
        mask = col_out - col_in + 1 == column_tap
        taps = []
        for tap in range(3):
            value = prod_s[tap, 0:main].reshape(outs, width, 3 * size)
            total = jnp.sum(jnp.where(mask[None], value, 0.0), axis=1)
            if column_tap == 2:
                total = total + jnp.where(edge == 0, prod_s[tap, main : main + outs], 0.0)
            if column_tap == 0:
                total = total + jnp.where(edge == width - 1, prod_s[tap, main + outs : span], 0.0)
            taps.append(total)
        gathered = jnp.concatenate(taps, axis=0)
        sums_ref[column_tap] = lax.dot_general(
            fold_ref[...], gathered, (((1,), (1,)), ((), ())),
            precision=HIGHEST, preferred_element_type=f32,
        )


def grad_volume_levels(first_level, cot_s, weight_ref, gv_s):
    count, size, rows = gv_s.shape
    span = cot_s.shape[1]

    def step(pair, carry):
        at = first_level + pair * 2
        near = cot_s[pl.ds(at, 3)].reshape(3 * span, rows)
        far = cot_s[pl.ds(at + 1, 3)].reshape(3 * span, rows)
        result = jnp.dot(
            weight_ref[...], jnp.concatenate([near, far], axis=1),
            preferred_element_type=jnp.float32,
        )
        for half in range(2):
            part = result[:, half * rows : (half + 1) * rows]
            total = (
                part[size : 2 * size]
                + roll_zero(part[:size], -1)
                + roll_zero(part[2 * size :], 1)
            )
            gv_s[pair * 2 + half] = total.astype(jnp.bfloat16).astype(jnp.float32)
        return carry

    lax.fori_loop(0, count // 2, step, 0)


def feature_grads(hops, pieces, left_ref, right_s, *refs):
    gv_refs, (grad_left_ref, own_ref, *rest) = refs[:pieces], refs[pieces:]
    sent_refs, (grad_s,) = rest[:hops], rest[hops:]
    held = gv_refs[0].shape[0]
    channels, width, rows = left_ref.shape
    groups = channels // GROUP
    reach = hops * width
    f32, bf16 = jnp.float32, jnp.bfloat16
    grad_s[...] = jnp.zeros(grad_s.shape, f32)

    def grads_step(group, carry):
        first = group * GROUP
        lefts = [left_ref[first + k].astype(f32) for k in range(GROUP)]
        totals = [jnp.zeros((width, rows), f32) for k in range(GROUP)]
        rows_at = pl.ds(pl.multiple_of(group * width, width), width)
        for d in range(D):
            value = gv_refs[d // held][d % held, rows_at]
            for k in range(GROUP):
                totals[k] = totals[k] + value * right_s[first + k, reach - d : reach - d + width]
                grad_s[first + k, reach - d : reach - d + width] += value * lefts[k]
        for k in range(GROUP):
            grad_left_ref[first + k] = (totals[k] * (1.0 / GROUP)).astype(bf16)
        return carry

    lax.fori_loop(0, groups, grads_step, 0)
    own_ref[...] = grad_s[:, reach : reach + width] * (1.0 / GROUP)
    for hop in range(1, hops + 1):
        at = reach - hop * width
        sent_refs[hop - 1][...] = (grad_s[:, at : at + width] * (1.0 / GROUP)).astype(bf16)


VMEM = pl.BlockSpec(memory_space=pltpu.VMEM)
SMEM = pl.BlockSpec(memory_space=pltpu.SMEM)
HBM = pl.BlockSpec(memory_space=pltpu.HBM)
MIB = 1024 * 1024


def cost(flops):
    return pl.CostEstimate(flops=flops, bytes_accessed=4 * MIB, transcendentals=0)


def run_kernel_sums(places, cots, halos, halo_order, rights, left, fold):
    outs, levels, width, rows = cots[0].shape
    channels = left.shape[0]
    size = fold.shape[1]
    span = outs * (width + 2)
    f32, bf16 = jnp.float32, jnp.bfloat16
    moved = [*cots, halos, *rights]
    return pl.pallas_call(
        functools.partial(kernel_sums, len(cots), len(rights) - 1, halo_order),
        out_shape=[
            jax.ShapeDtypeStruct((D + 2, span, rows), bf16),
            jax.ShapeDtypeStruct((channels, len(rights) * width, rows), f32),
            jax.ShapeDtypeStruct((3, fold.shape[0], 3 * outs), f32),
        ],
        in_specs=[SMEM] + [HBM] * len(moved) + [VMEM] * 2,
        out_specs=[VMEM] * 3,
        scratch_shapes=[
            pltpu.VMEM((len(cots), *cots[0].shape), bf16),
            pltpu.VMEM(halos.shape, bf16),
            pltpu.VMEM((len(rights), *rights[0].shape), bf16),
            pltpu.VMEM((D, 3, size // 3, rows), f32),
            pltpu.VMEM((3, span, size), f32),
            pltpu.SemaphoreType.DMA((len(moved),)),
        ],
        compiler_params=pltpu.CompilerParams(vmem_limit_bytes=20 * MIB),
        cost_estimate=cost(8000000000),
    )(places, *moved, left, fold)


def run_grad_volume(cot_wide, weights, first_level, count):
    size, rows = weights.shape[0] // 3, cot_wide.shape[2]
    return pl.pallas_call(
        functools.partial(grad_volume_levels, first_level),
        out_shape=jax.ShapeDtypeStruct((count, size, rows), jnp.float32),
        in_specs=[VMEM] * 2,
        out_specs=VMEM,
        compiler_params=pltpu.CompilerParams(vmem_limit_bytes=8 * MIB),
        cost_estimate=cost(4000000000),
    )(cot_wide, weights)


def run_feature_grads(left, right_wide, grad_volumes, hops):
    channels, width, rows = left.shape
    f32, bf16 = jnp.float32, jnp.bfloat16
    return pl.pallas_call(
        functools.partial(feature_grads, hops, len(grad_volumes)),
        out_shape=[
            jax.ShapeDtypeStruct((channels, width, rows), bf16),
            jax.ShapeDtypeStruct((channels, width, rows), f32),
            *[jax.ShapeDtypeStruct((channels, width, rows), bf16)] * hops,
        ],
        in_specs=[VMEM] * (2 + len(grad_volumes)),
        out_specs=[VMEM] * (hops + 2),
        scratch_shapes=[pltpu.VMEM((channels, (hops + 1) * width, rows), f32)],
        compiler_params=pltpu.CompilerParams(vmem_limit_bytes=8 * MIB),
        cost_estimate=cost(4000000000),
    )(left, right_wide, *grad_volumes)


def swapped(value, axis, bit):
    count = lax.axis_size(axis)
    return lax.ppermute(value, axis, [(source, source ^ bit) for source in range(count)])


def gather_swapping(value, axis, others=()):
    held = {0: value}
    bit = lax.axis_size(axis) // 2
    while bit:
        step = {key | bit: swapped(item, axis, bit) for key, item in held.items()}
        if others and bit == lax.axis_size(axis) // 2:
            (step[bit], *others) = lax.optimization_barrier((step[bit], *others))
        held.update(step)
        bit //= 2
    return [held[key] for key in range(len(held))], others


def gather_joining(value, axis):
    count = lax.axis_size(axis)
    held, order = value[None], [0]
    bit = count // 2
    while bit:
        held = jnp.concatenate([held, swapped(held, axis, bit)], axis=0)
        order = order + [key | bit for key in order]
        bit //= 2
    return held, order


def total_swapping(value, bit):
    return value + swapped(value, "col", bit)


def body(left, right, kernel, cotangent):
    outs, levels, width, rows = cotangent.shape
    parts = lax.axis_size("disp")
    columns = lax.axis_size("col")
    channels = C // parts
    groups = G // parts
    hops = (D + width - 2) // width
    part, column = lax.axis_index("disp"), lax.axis_index("col")
    places = jnp.stack([part, column]).astype(jnp.int32)
    f32, bf16 = jnp.float32, jnp.bfloat16

    low = jnp.transpose(cotangent[:, :, width - 1], (1, 0, 2))
    high = jnp.transpose(cotangent[:, :, 0], (1, 0, 2))
    low, high, right = lax.optimization_barrier((low, high, right))
    low, high = shifted(low, "col", 1), shifted(high, "col", -1)
    right_own = lax.dynamic_slice_in_dim(right, part * channels, channels, 0)
    right_near, low, high = lax.optimization_barrier((right_own, low, high))
    low = jnp.where(column > 0, low, 0).astype(bf16)
    high = jnp.where(column < columns - 1, high, 0).astype(bf16)
    halos, halo_order = gather_joining(jnp.concatenate([low, high], axis=1), "disp")
    rights = [right_own] + [
        shifted(right_own if hop <= 2 else right_near, "col", hop) for hop in range(1, hops + 1)
    ]
    cots, rights = gather_swapping(cotangent, "disp", rights)

    left_own = lax.dynamic_slice_in_dim(left, part * channels, channels, 0)
    weights = toeplitz(lax.dynamic_slice_in_dim(kernel, part * groups, groups, 4), width)
    pad_rows = -(-3 * groups // 8) * 8
    fold = np.zeros((pad_rows, 3 * groups * width), np.float32)
    fold[np.arange(3 * groups * width) // width, np.arange(3 * groups * width)] = 1

    cot_wide, right_wide, total = run_kernel_sums(
        places, cots, halos, halo_order, rights, left_own, jnp.asarray(fold)
    )
    bits = [1 << k for k in reversed(range(columns.bit_length() - 1))]
    first_half = run_grad_volume(cot_wide, weights, 0, D // 2)
    total = total_swapping(total, bits[0])
    cot_wide, first_half, total = lax.optimization_barrier((cot_wide, first_half, total))
    second_half = run_grad_volume(cot_wide, weights, D // 2, D // 2)
    total = total_swapping(total, bits[1])
    second_half, total = lax.optimization_barrier((second_half, total))
    results = run_feature_grads(left_own, right_wide, [first_half, second_half], hops)
    for bit in bits[2:]:
        total = total_swapping(total, bit)
    *results, total = lax.optimization_barrier((*results, total))
    grad_left, own, sent = results[0], results[1], results[2:]

    total_right = own
    for hop in range(hops, 0, -1):
        arrived = shifted(sent[hop - 1], "col", -hop).astype(f32)
        total_right = total_right + jnp.where(column + hop < columns, arrived, 0.0)

    pieces = jnp.stack(gather_swapping(total, "disp")[0])
    pieces = pieces[jnp.arange(parts) ^ part][:, :, : 3 * groups]
    total = pieces.reshape(parts, 3, 3, groups, 3, outs)
    cell_count = D * width * columns * rows
    grad_kernel = jnp.transpose(total, (4, 1, 2, 5, 0, 3))[::-1].reshape(3, 3, 3, outs, G)
    grad_kernel = grad_kernel * (1.0 / math.sqrt(cell_count))
    return (grad_left, total_right.astype(bf16), grad_kernel)


def solution(mesh):
    return jax.shard_map(
        body,
        mesh=mesh,
        in_specs=(P(None, "col", None), P(None, "col", None), P(), P(None, "disp", "col", None)),
        out_specs=(P("disp", "col", None), P("disp", "col", None), P()),
        check_vma=False,
    )
```

```python
import functools
import math

import jax
import jax.numpy as jnp
import numpy as np
from jax import lax
from jax.experimental import pallas as pl
from jax.experimental.pallas import tpu as pltpu
from jax.sharding import PartitionSpec as P

C = 320
G = 40
D = 48
GROUP = C // G
HIGHEST = lax.Precision.HIGHEST


def shifted(value, axis, steps):
    count = lax.axis_size(axis)
    return lax.ppermute(value, axis, [(source, (source + steps) % count) for source in range(count)])


def conv_rows(outs, width):
    main = np.tile(np.arange(width), outs)
    return np.concatenate([main, np.full(outs, -1), np.full(outs, width)])


def toeplitz(kernel_local, width):
    outs, groups = kernel_local.shape[3:]
    row_col = conv_rows(outs, width)
    row_out = np.concatenate([np.repeat(np.arange(outs), width), np.tile(np.arange(outs), 2)])
    spread = np.zeros((outs, row_col.size), np.float32)
    spread[row_out, np.arange(row_col.size)] = 1
    taps = jnp.transpose(kernel_local[::-1], (1, 2, 4, 0, 3))
    wide = jnp.einsum(
        "qrgpo,ok->qrgpk", taps, jnp.asarray(spread, jnp.bfloat16),
        preferred_element_type=jnp.float32,
    ).astype(jnp.bfloat16)
    out_col = np.arange(width)
    column_tap = out_col[:, None] - row_col[None, :] + 1
    total = jnp.zeros((3, groups, width, 3, row_col.size), jnp.bfloat16)
    for tap in range(3):
        mask = jnp.asarray(column_tap == tap)[None, None, :, None, :]
        total = jnp.where(mask, wide[tap][:, :, None], total)
    return total.reshape(3 * groups * width, 3 * row_col.size)


def roll_zero(value, steps):
    size = value.shape[-1]
    lane = lax.broadcasted_iota(jnp.int32, value.shape, value.ndim - 1)
    moved = pltpu.roll(value, steps % size, value.ndim - 1)
    return jnp.where(lane == (0 if steps > 0 else size - 1), 0.0, moved)


def add_grads(first_level, count, cot_s, weight_ref, left_s, right_s, left_sum, grad_s):
    channels, width, rows = left_s.shape
    groups = channels // GROUP
    size = groups * width
    span = cot_s.shape[1]
    reach = right_s.shape[1] - width
    shift = right_s.shape[1] - grad_s.shape[1]
    f32, bf16 = jnp.float32, jnp.bfloat16

    def pair_values(at):
        near = cot_s[pl.ds(at, 3)].reshape(3 * span, rows)
        far = cot_s[pl.ds(at + 1, 3)].reshape(3 * span, rows)
        result = jnp.dot(
            weight_ref[...], jnp.concatenate([near, far], axis=1), preferred_element_type=f32
        )
        values = []
        for half in range(2):
            part = result[:, half * rows : (half + 1) * rows]
            total = (
                part[size : 2 * size]
                + roll_zero(part[:size], -1)
                + roll_zero(part[2 * size :], 1)
            )
            values.append(total.astype(bf16).astype(f32))
        return values

    def step(number, carry):
        level = first_level + number * width
        base = pl.multiple_of(reach - first_level - width - number * width, width)
        rights = right_s.at[:, pl.ds(base, 2 * width)]
        grads = grad_s.at[:, pl.ds(pl.multiple_of(base - shift, width), 2 * width)]

        def use(pair, values):
            at = width - 2 * pair
            for group in range(groups):
                ones = [value[group * width : (group + 1) * width] for value in values]
                for c in range(group * GROUP, (group + 1) * GROUP):
                    left = left_s[c]
                    left_sum[c] += (
                        ones[0] * rights[c, at : at + width]
                        + ones[1] * rights[c, at - 1 : at - 1 + width]
                    )
                    grads[c, at : at + width] += ones[0] * left
                    grads[c, at - 1 : at - 1 + width] += ones[1] * left

        waiting = pair_values(level)
        for pair in range(1, width // 2):
            later = pair_values(level + 2 * pair)
            use(pair - 1, waiting)
            waiting = later
        use(width // 2 - 1, waiting)
        return carry

    lax.fori_loop(0, count // width, step, 0)


def upper_grads(parts, hops, far, halo_order, places, *refs):
    cot_refs, halo_refs, refs = refs[:parts], refs[parts : parts + 2], refs[parts + 2 :]
    right_refs, refs = refs[: hops + 1], refs[hops + 1 :]
    left_ref, weight_ref, cot_s, right_s, left_sum, grad_out = refs[:6]
    sent_refs, refs = refs[6 : 6 + far], refs[6 + far :]
    cot_b, halo_b, right_b, left_s, grad_s, sems = refs
    channels, width, rows = left_ref.shape
    outs, levels = cot_refs[0].shape[:2]
    main = outs * width
    span = main + 2 * outs
    reach = hops * width
    f32, bf16 = jnp.float32, jnp.bfloat16

    copies = []
    for buffer, sources in ((right_b, right_refs), (cot_b, cot_refs)):
        for at, source in enumerate(sources):
            copies.append(
                pltpu.make_async_copy(source, buffer.at[at], sems.at[len(copies)])
            )
    half = halo_b.shape[0] // 2
    for at, source in enumerate(halo_refs):
        copies.append(
            pltpu.make_async_copy(source, halo_b.at[pl.ds(at * half, half)], sems.at[len(copies)])
        )
    for copy in copies:
        copy.start()

    left_s[...] = left_ref[...].astype(f32)
    left_sum[...] = jnp.zeros(left_sum.shape, f32)
    grad_s[...] = jnp.zeros(grad_s.shape, f32)
    cot_s[0] = jnp.zeros((span, rows), bf16)
    cot_s[D + 1] = jnp.zeros((span, rows), bf16)
    for hop in range(hops + 1):
        copies[hop].wait()
        at = reach - hop * width
        block = right_b[hop].astype(f32)
        right_s[:, at : at + width] = jnp.where(places[1] >= hop, block, 0.0)
    for copy in copies[hops + 1 :]:
        copy.wait()
    for other in range(parts):
        start = (places[0] ^ other) * levels + 1

        def assemble(level, carry, other=other, start=start):
            cot_s[start + level, 0:main] = cot_b[other, :, level].reshape(main, rows)
            cot_s[start + level, main:span] = halo_b[halo_order.index(other), level]
            return carry

        lax.fori_loop(0, levels, assemble, 0)

    add_grads(D // 2, D // 2, cot_s, weight_ref, left_s, right_s, left_sum, grad_s)
    grad_out[...] = grad_s[:, far * width :]
    for hop in range(hops, hops - far, -1):
        at = reach - hop * width
        sent_refs[hops - hop][...] = (grad_s[:, at : at + width] * (1.0 / GROUP)).astype(bf16)


def lower_grads(
    near, left_ref, weight_ref, cot_s, right_s, left_part, grad_part, grad_left_ref, own_ref, *rest
):
    sent_refs, (left_s, left_sum, grad_s) = rest[:near], rest[near:]
    channels, width, rows = left_ref.shape
    f32, bf16 = jnp.float32, jnp.bfloat16
    left_s[...] = left_ref[...].astype(f32)
    left_sum[...] = left_part[...]
    grad_s[...] = grad_part[...]
    add_grads(0, D // 2, cot_s, weight_ref, left_s, right_s, left_sum, grad_s)
    grad_left_ref[...] = (left_sum[...] * (1.0 / GROUP)).astype(bf16)
    own_ref[...] = grad_s[:, near * width :] * (1.0 / GROUP)
    for hop in range(near, 0, -1):
        at = (near - hop) * width
        sent_refs[near - hop][...] = (grad_s[:, at : at + width] * (1.0 / GROUP)).astype(bf16)


def kernel_sums(left_ref, cot_s, right_s, fold_ref, sums_ref, vol_s, prod_s):
    channels, width, rows = left_ref.shape
    groups = channels // GROUP
    span = cot_s.shape[1]
    outs = span // (width + 2)
    main = outs * width
    size = groups * width
    reach = right_s.shape[1] - width
    f32, bf16 = jnp.float32, jnp.bfloat16

    def volume_step(group, carry):
        first = group * GROUP
        lefts = [left_ref[first + k].astype(f32) for k in range(GROUP)]
        rows_at = pl.ds(pl.multiple_of(group * width, width), width)
        for d in range(D):
            total = lefts[0] * right_s[first, reach - d : reach - d + width]
            for k in range(1, GROUP):
                total = total + lefts[k] * right_s[first + k, reach - d : reach - d + width]
            value = (total * (1.0 / GROUP)).astype(bf16).astype(f32)
            vol_s[d, 0, rows_at] = roll_zero(value, 1)
            vol_s[d, 1, rows_at] = value
            vol_s[d, 2, rows_at] = roll_zero(value, -1)
        return carry

    lax.fori_loop(0, groups, volume_step, 0)

    chunk = 4
    prod_s[...] = jnp.zeros(prod_s.shape, f32)

    def kernel_step(step, carry):
        first = step * chunk
        volume = jnp.concatenate(
            [vol_s[first + k].reshape(3 * size, rows).astype(bf16) for k in range(chunk)], axis=1
        )
        for tap in range(3):
            value = jnp.concatenate([cot_s[first + k + tap] for k in range(chunk)], axis=1)
            prod_s[tap] += lax.dot_general(
                value, volume, (((1,), (1,)), ((), ())), preferred_element_type=f32
            )
        return carry

    lax.fori_loop(0, D // chunk, kernel_step, 0)

    col_in = lax.broadcasted_iota(jnp.int32, (width, 3 * size), 0)
    col_out = lax.broadcasted_iota(jnp.int32, (width, 3 * size), 1) % width
    edge = lax.broadcasted_iota(jnp.int32, (outs, 3 * size), 1) % width
    for column_tap in range(3):
        mask = col_out - col_in + 1 == column_tap
        taps = []
        for tap in range(3):
            value = prod_s[tap, 0:main].reshape(outs, width, 3 * size)
            total = jnp.sum(jnp.where(mask[None], value, 0.0), axis=1)
            if column_tap == 2:
                total = total + jnp.where(edge == 0, prod_s[tap, main : main + outs], 0.0)
            if column_tap == 0:
                total = total + jnp.where(edge == width - 1, prod_s[tap, main + outs : span], 0.0)
            taps.append(total)
        gathered = jnp.concatenate(taps, axis=0)
        sums_ref[column_tap] = lax.dot_general(
            fold_ref[...], gathered, (((1,), (1,)), ((), ())),
            precision=HIGHEST, preferred_element_type=f32,
        )


VMEM = pl.BlockSpec(memory_space=pltpu.VMEM)
SMEM = pl.BlockSpec(memory_space=pltpu.SMEM)
HBM = pl.BlockSpec(memory_space=pltpu.HBM)
MIB = 1024 * 1024


def run(function, operands, outs, scratch, limit, flops):
    return pl.pallas_call(
        function,
        out_shape=[jax.ShapeDtypeStruct(shape, kind) for shape, kind in outs],
        in_specs=[space for space, array in operands],
        out_specs=[VMEM] * len(outs),
        scratch_shapes=scratch,
        compiler_params=pltpu.CompilerParams(vmem_limit_bytes=limit * MIB),
        cost_estimate=pl.CostEstimate(flops=1024, bytes_accessed=1024, transcendentals=0),
    )(*[array for space, array in operands])


def swapped(value, axis, bit):
    count = lax.axis_size(axis)
    return lax.ppermute(value, axis, [(source, source ^ bit) for source in range(count)])


def gather_swapping(value, axis, others=()):
    held = {0: value}
    bit = lax.axis_size(axis) // 2
    while bit:
        step = {key | bit: swapped(item, axis, bit) for key, item in held.items()}
        if others and bit == lax.axis_size(axis) // 2:
            (step[bit], *others) = lax.optimization_barrier((step[bit], *others))
        held.update(step)
        bit //= 2
    return [held[key] for key in range(len(held))], others


def gather_joining(held, axis):
    bit = lax.axis_size(axis) // 2
    order = [0, bit]
    bit //= 2
    while bit:
        joined = jnp.concatenate(held, axis=0)
        held = [joined, swapped(joined, axis, bit)]
        order = order + [key | bit for key in order]
        bit //= 2
    return held, order


def total_swapping(value, bit):
    return value + swapped(value, "col", bit)


def body(left, right, kernel, cotangent):
    outs, levels, width, rows = cotangent.shape
    parts = lax.axis_size("disp")
    columns = lax.axis_size("col")
    channels = C // parts
    groups = G // parts
    size = groups * width
    span = outs * (width + 2)
    hops = (D + width - 2) // width
    far = D // 2 // width
    first = (hops // 2, hops // 2 + 1)
    near = hops - far
    part, column = lax.axis_index("disp"), lax.axis_index("col")
    places = jnp.stack([part, column]).astype(jnp.int32)
    f32, bf16 = jnp.float32, jnp.bfloat16

    low = jnp.transpose(cotangent[:, :, width - 1], (1, 0, 2))
    high = jnp.transpose(cotangent[:, :, 0], (1, 0, 2))
    low, high, right = lax.optimization_barrier((low, high, right))
    low, high = shifted(low, "col", 1), shifted(high, "col", -1)
    right_own = lax.dynamic_slice_in_dim(right, part * channels, channels, 0)
    left_own = lax.dynamic_slice_in_dim(left, part * channels, channels, 0)
    weights = toeplitz(lax.dynamic_slice_in_dim(kernel, part * groups, groups, 4), width)
    right_late, low, high, left_own, weights = lax.optimization_barrier(
        (right_own, low, high, left_own, weights)
    )
    low = jnp.where(column > 0, low, 0).astype(bf16)
    high = jnp.where(column < columns - 1, high, 0).astype(bf16)
    halo = jnp.concatenate([low, high], axis=1)[None]
    halo_across = swapped(halo, "disp", parts // 2)
    rights = [right_own] + [
        shifted(right_own if hop in first else right_late, "col", hop)
        for hop in range(1, hops + 1)
    ]
    cots, (halo_across, *rights[2:hops]) = gather_swapping(
        cotangent, "disp", [halo_across, *rights[2:hops]]
    )
    halos, halo_order = gather_joining([halo, halo_across], "disp")

    pad_rows = -(-3 * groups // 8) * 8
    fold = np.zeros((pad_rows, 3 * size), np.float32)
    fold[np.arange(3 * size) // width, np.arange(3 * size)] = 1

    block = (channels, width, rows)
    wide = (channels, (hops + 1) * width, rows)
    moved = [*cots, *halos, *rights]
    results = run(
        functools.partial(upper_grads, parts, hops, far, halo_order),
        [(SMEM, places)] + [(HBM, item) for item in moved] + [(VMEM, left_own), (VMEM, weights)],
        [
            ((D + 2, span, rows), bf16),
            (wide, f32),
            (block, f32),
            ((channels, (near + 1) * width, rows), f32),
            *[(block, bf16)] * far,
        ],
        [
            pltpu.VMEM((parts, *cotangent.shape), bf16),
            pltpu.VMEM((parts, levels, 2 * outs, rows), bf16),
            pltpu.VMEM((hops + 1, *block), bf16),
            pltpu.VMEM(block, f32),
            pltpu.VMEM(wide, f32),
            pltpu.SemaphoreType.DMA((len(moved),)),
        ],
        20, 8000000000,
    )
    cot_wide, right_wide, left_part, grad_part = results[:4]
    sent = dict(zip(range(hops, hops - far, -1), results[4:]))
    arrived = {hop: shifted(value, "col", -hop) for hop, value in sent.items()}

    (total,) = run(
        kernel_sums,
        [(VMEM, item) for item in (left_own, cot_wide, right_wide, jnp.asarray(fold))],
        [((3, pad_rows, 3 * outs), f32)],
        [pltpu.VMEM((D, 3, size, rows), f32), pltpu.VMEM((3, span, 3 * size), f32)],
        16, 8000000000,
    )
    grad_part, total = lax.optimization_barrier((grad_part, total))
    bits = [1 << k for k in reversed(range(columns.bit_length() - 1))]
    total = total_swapping(total, bits[0])
    results = run(
        functools.partial(lower_grads, near),
        [
            (VMEM, item)
            for item in (left_own, weights, cot_wide, right_wide, left_part, grad_part)
        ],
        [(block, bf16), (block, f32), *[(block, bf16)] * near],
        [
            pltpu.VMEM(block, f32),
            pltpu.VMEM(block, f32),
            pltpu.VMEM((channels, (near + 1) * width, rows), f32),
        ],
        16, 8000000000,
    )
    distant = sorted(arrived)
    *results, total = lax.optimization_barrier((*results, total, *[arrived[hop] for hop in distant]))
    results, held = results[: 2 + near], [*results[2 + near :], total]
    total, held = held[0], held[1:]
    arrived = dict(zip(distant, held))
    grad_left, own = results[:2]
    sent = dict(zip(range(near, 0, -1), results[2:]))
    arrived.update({hop: shifted(value, "col", -hop) for hop, value in sent.items()})
    for bit in bits[1:]:
        total = total_swapping(total, bit)

    total_right = own
    for hop in range(1, hops + 1):
        total_right = total_right + jnp.where(
            column + hop < columns, arrived[hop].astype(f32), 0.0
        )

    pieces = jnp.stack(gather_swapping(total, "disp")[0])
    pieces = pieces[jnp.arange(parts) ^ part][:, :, : 3 * groups]
    total = pieces.reshape(parts, 3, 3, groups, 3, outs)
    cell_count = D * width * columns * rows
    grad_kernel = jnp.transpose(total, (4, 1, 2, 5, 0, 3))[::-1].reshape(3, 3, 3, outs, G)
    grad_kernel = grad_kernel * (1.0 / math.sqrt(cell_count))
    return (grad_left, total_right.astype(bf16), grad_kernel)


def solution(mesh):
    return jax.shard_map(
        body,
        mesh=mesh,
        in_specs=(P(None, "col", None), P(None, "col", None), P(), P(None, "disp", "col", None)),
        out_specs=(P("disp", "col", None), P("disp", "col", None), P()),
        check_vma=False,
    )
```

```python
import functools
import math

import jax
import jax.numpy as jnp
import numpy as np
from jax import lax
from jax.experimental import pallas as pl
from jax.experimental.pallas import tpu as pltpu
from jax.sharding import PartitionSpec as P

C = 320
G = 40
D = 48
GROUP = C // G
HIGHEST = lax.Precision.HIGHEST


def shifted(value, axis, steps):
    count = lax.axis_size(axis)
    return lax.ppermute(value, axis, [(source, (source + steps) % count) for source in range(count)])


def conv_rows(outs, width):
    main = np.tile(np.arange(width), outs)
    return np.concatenate([main, np.full(outs, -1), np.full(outs, width)])


def toeplitz(kernel_local, width):
    outs, groups = kernel_local.shape[3:]
    row_col = conv_rows(outs, width)
    row_out = np.concatenate([np.repeat(np.arange(outs), width), np.tile(np.arange(outs), 2)])
    spread = np.zeros((outs, row_col.size), np.float32)
    spread[row_out, np.arange(row_col.size)] = 1
    taps = jnp.transpose(kernel_local[::-1], (1, 2, 4, 0, 3))
    wide = jnp.einsum(
        "qrgpo,ok->qrgpk", taps, jnp.asarray(spread, jnp.bfloat16),
        preferred_element_type=jnp.float32,
    ).astype(jnp.bfloat16)
    out_col = np.arange(width)
    column_tap = out_col[:, None] - row_col[None, :] + 1
    total = jnp.zeros((3, groups, width, 3, row_col.size), jnp.bfloat16)
    for tap in range(3):
        mask = jnp.asarray(column_tap == tap)[None, None, :, None, :]
        total = jnp.where(mask, wide[tap][:, :, None], total)
    return total.reshape(3 * groups * width, 3 * row_col.size)


def roll_zero(value, steps):
    size = value.shape[-1]
    lane = lax.broadcasted_iota(jnp.int32, value.shape, value.ndim - 1)
    moved = pltpu.roll(value, steps % size, value.ndim - 1)
    return jnp.where(lane == (0 if steps > 0 else size - 1), 0.0, moved)


def add_grads(first_level, count, cot_s, weight_ref, left_s, right_s, left_sum, grad_s):
    channels, width, rows = left_s.shape
    groups = channels // GROUP
    size = groups * width
    span = cot_s.shape[1]
    reach = right_s.shape[1] - width
    shift = right_s.shape[1] - grad_s.shape[1]
    f32, bf16 = jnp.float32, jnp.bfloat16

    def pair_values(at):
        near = cot_s[pl.ds(at, 3)].reshape(3 * span, rows)
        far = cot_s[pl.ds(at + 1, 3)].reshape(3 * span, rows)
        result = jnp.dot(
            weight_ref[...], jnp.concatenate([near, far], axis=1), preferred_element_type=f32
        )
        values = []
        for half in range(2):
            part = result[:, half * rows : (half + 1) * rows]
            total = (
                part[size : 2 * size]
                + roll_zero(part[:size], -1)
                + roll_zero(part[2 * size :], 1)
            )
            values.append(total.astype(bf16).astype(f32))
        return values

    def step(number, carry):
        level = first_level + number * width
        base = pl.multiple_of(reach - first_level - width - number * width, width)
        rights = right_s.at[:, pl.ds(base, 2 * width)]
        grads = grad_s.at[:, pl.ds(pl.multiple_of(base - shift, width), 2 * width)]

        def use(pair, values):
            at = width - 2 * pair
            for group in range(groups):
                ones = [value[group * width : (group + 1) * width] for value in values]
                for c in range(group * GROUP, (group + 1) * GROUP):
                    left = left_s[c]
                    left_sum[c] += (
                        ones[0] * rights[c, at : at + width]
                        + ones[1] * rights[c, at - 1 : at - 1 + width]
                    )
                    grads[c, at : at + width] += ones[0] * left
                    grads[c, at - 1 : at - 1 + width] += ones[1] * left

        waiting = pair_values(level)
        for pair in range(1, width // 2):
            later = pair_values(level + 2 * pair)
            use(pair - 1, waiting)
            waiting = later
        use(width // 2 - 1, waiting)
        return carry

    lax.fori_loop(0, count // width, step, 0)


def upper_grads(far, left_ref, weight_ref, cot_s, right_s, left_sum, grad_out, *rest):
    sent_refs, (left_s, grad_s) = rest[:far], rest[far:]
    width = left_ref.shape[1]
    f32, bf16 = jnp.float32, jnp.bfloat16
    left_s[...] = left_ref[...].astype(f32)
    left_sum[...] = jnp.zeros(left_sum.shape, f32)
    grad_s[...] = jnp.zeros(grad_s.shape, f32)
    add_grads(D // 2, D // 2, cot_s, weight_ref, left_s, right_s, left_sum, grad_s)
    grad_out[...] = grad_s[:, far * width :]
    for at in range(far):
        sent_refs[at][...] = (
            grad_s[:, at * width : (at + 1) * width] * (1.0 / GROUP)
        ).astype(bf16)


def lower_grads(
    near, left_ref, weight_ref, cot_s, right_s, left_part, grad_part, grad_left_ref, own_ref, *rest
):
    sent_refs, (left_s, left_sum, grad_s) = rest[:near], rest[near:]
    channels, width, rows = left_ref.shape
    f32, bf16 = jnp.float32, jnp.bfloat16
    left_s[...] = left_ref[...].astype(f32)
    left_sum[...] = left_part[...]
    grad_s[...] = grad_part[...]
    add_grads(0, D // 2, cot_s, weight_ref, left_s, right_s, left_sum, grad_s)
    grad_left_ref[...] = (left_sum[...] * (1.0 / GROUP)).astype(bf16)
    own_ref[...] = grad_s[:, near * width :] * (1.0 / GROUP)
    for hop in range(near, 0, -1):
        at = (near - hop) * width
        sent_refs[near - hop][...] = (grad_s[:, at : at + width] * (1.0 / GROUP)).astype(bf16)


def kernel_sums(parts, hops, halo_order, places, *refs):
    cot_refs, halo_refs, refs = refs[:parts], refs[parts : parts + 2], refs[parts + 2 :]
    right_refs, refs = refs[: hops + 1], refs[hops + 1 :]
    left_ref, fold_ref, cot_s, right_s, sums_ref = refs[:5]
    cot_b, halo_b, right_b, vol_s, prod_s, sems = refs[5:]
    channels, width, rows = left_ref.shape
    groups = channels // GROUP
    outs, levels = cot_refs[0].shape[:2]
    main = outs * width
    span = main + 2 * outs
    size = groups * width
    reach = hops * width
    f32, bf16 = jnp.float32, jnp.bfloat16

    copies = []
    for buffer, sources in ((right_b, right_refs), (cot_b, cot_refs)):
        for at, source in enumerate(sources):
            copies.append(
                pltpu.make_async_copy(source, buffer.at[at], sems.at[len(copies)])
            )
    half = halo_b.shape[0] // 2
    for at, source in enumerate(halo_refs):
        copies.append(
            pltpu.make_async_copy(source, halo_b.at[pl.ds(at * half, half)], sems.at[len(copies)])
        )
    for copy in copies:
        copy.start()

    cot_s[0] = jnp.zeros((span, rows), bf16)
    cot_s[D + 1] = jnp.zeros((span, rows), bf16)
    for hop in range(hops + 1):
        copies[hop].wait()
        at = reach - hop * width
        block = right_b[hop].astype(f32)
        right_s[:, at : at + width] = jnp.where(places[1] >= hop, block, 0.0)

    def volume_step(group, carry):
        first = group * GROUP
        lefts = [left_ref[first + k].astype(f32) for k in range(GROUP)]
        rows_at = pl.ds(pl.multiple_of(group * width, width), width)
        for d in range(D):
            total = lefts[0] * right_s[first, reach - d : reach - d + width]
            for k in range(1, GROUP):
                total = total + lefts[k] * right_s[first + k, reach - d : reach - d + width]
            value = (total * (1.0 / GROUP)).astype(bf16).astype(f32)
            vol_s[d, 0, rows_at] = roll_zero(value, 1)
            vol_s[d, 1, rows_at] = value
            vol_s[d, 2, rows_at] = roll_zero(value, -1)
        return carry

    lax.fori_loop(0, groups, volume_step, 0)

    for copy in copies[hops + 1 :]:
        copy.wait()
    for other in range(parts):
        start = (places[0] ^ other) * levels + 1

        def assemble(level, carry, other=other, start=start):
            cot_s[start + level, 0:main] = cot_b[other, :, level].reshape(main, rows)
            cot_s[start + level, main:span] = halo_b[halo_order.index(other), level]
            return carry

        lax.fori_loop(0, levels, assemble, 0)

    chunk = 4
    prod_s[...] = jnp.zeros(prod_s.shape, f32)

    def kernel_step(step, carry):
        first = step * chunk
        volume = jnp.concatenate(
            [vol_s[first + k].reshape(3 * size, rows).astype(bf16) for k in range(chunk)], axis=1
        )
        for tap in range(3):
            value = jnp.concatenate([cot_s[first + k + tap] for k in range(chunk)], axis=1)
            prod_s[tap] += lax.dot_general(
                value, volume, (((1,), (1,)), ((), ())), preferred_element_type=f32
            )
        return carry

    lax.fori_loop(0, D // chunk, kernel_step, 0)

    col_in = lax.broadcasted_iota(jnp.int32, (width, 3 * size), 0)
    col_out = lax.broadcasted_iota(jnp.int32, (width, 3 * size), 1) % width
    edge = lax.broadcasted_iota(jnp.int32, (outs, 3 * size), 1) % width
    for column_tap in range(3):
        mask = col_out - col_in + 1 == column_tap
        taps = []
        for tap in range(3):
            value = prod_s[tap, 0:main].reshape(outs, width, 3 * size)
            total = jnp.sum(jnp.where(mask[None], value, 0.0), axis=1)
            if column_tap == 2:
                total = total + jnp.where(edge == 0, prod_s[tap, main : main + outs], 0.0)
            if column_tap == 0:
                total = total + jnp.where(edge == width - 1, prod_s[tap, main + outs : span], 0.0)
            taps.append(total)
        gathered = jnp.concatenate(taps, axis=0)
        sums_ref[column_tap] = lax.dot_general(
            fold_ref[...], gathered, (((1,), (1,)), ((), ())),
            precision=HIGHEST, preferred_element_type=f32,
        )


VMEM = pl.BlockSpec(memory_space=pltpu.VMEM)
SMEM = pl.BlockSpec(memory_space=pltpu.SMEM)
HBM = pl.BlockSpec(memory_space=pltpu.HBM)
MIB = 1024 * 1024


def run(function, operands, outs, scratch, limit, flops):
    return pl.pallas_call(
        function,
        out_shape=[jax.ShapeDtypeStruct(shape, kind) for shape, kind in outs],
        in_specs=[space for space, array in operands],
        out_specs=[VMEM] * len(outs),
        scratch_shapes=scratch,
        compiler_params=pltpu.CompilerParams(vmem_limit_bytes=limit * MIB),
        cost_estimate=pl.CostEstimate(flops=flops, bytes_accessed=1024, transcendentals=0),
    )(*[array for space, array in operands])


def swapped(value, axis, bit):
    count = lax.axis_size(axis)
    return lax.ppermute(value, axis, [(source, source ^ bit) for source in range(count)])


def gather_swapping(value, axis, others=()):
    held = {0: value}
    bit = lax.axis_size(axis) // 2
    while bit:
        step = {key | bit: swapped(item, axis, bit) for key, item in held.items()}
        if others and bit == lax.axis_size(axis) // 2:
            (step[bit], *others) = lax.optimization_barrier((step[bit], *others))
        held.update(step)
        bit //= 2
    return [held[key] for key in range(len(held))], others


def gather_joining(held, axis):
    bit = lax.axis_size(axis) // 2
    order = [0, bit]
    bit //= 2
    while bit:
        joined = jnp.concatenate(held, axis=0)
        held = [joined, swapped(joined, axis, bit)]
        order = order + [key | bit for key in order]
        bit //= 2
    return held, order


def total_swapping(value, bit):
    return value + swapped(value, "col", bit)


def body(left, right, kernel, cotangent):
    outs, levels, width, rows = cotangent.shape
    parts = lax.axis_size("disp")
    columns = lax.axis_size("col")
    channels = C // parts
    groups = G // parts
    size = groups * width
    span = outs * (width + 2)
    hops = (D + width - 2) // width
    far = D // 2 // width
    first = (hops // 2, hops // 2 + 1)
    near = hops - far
    part, column = lax.axis_index("disp"), lax.axis_index("col")
    places = jnp.stack([part, column]).astype(jnp.int32)
    f32, bf16 = jnp.float32, jnp.bfloat16

    low = jnp.transpose(cotangent[:, :, width - 1], (1, 0, 2))
    high = jnp.transpose(cotangent[:, :, 0], (1, 0, 2))
    low, high, right = lax.optimization_barrier((low, high, right))
    low, high = shifted(low, "col", 1), shifted(high, "col", -1)
    right_own = lax.dynamic_slice_in_dim(right, part * channels, channels, 0)
    left_own = lax.dynamic_slice_in_dim(left, part * channels, channels, 0)
    weights = toeplitz(lax.dynamic_slice_in_dim(kernel, part * groups, groups, 4), width)
    right_late, low, high = lax.optimization_barrier((right_own, low, high))
    low = jnp.where(column > 0, low, 0).astype(bf16)
    high = jnp.where(column < columns - 1, high, 0).astype(bf16)
    halo = jnp.concatenate([low, high], axis=1)[None]
    halo_across = swapped(halo, "disp", parts // 2)
    rights = [right_own] + [
        shifted(right_own if hop in first else right_late, "col", hop)
        for hop in range(1, hops + 1)
    ]
    cots, (halo_across, *rights[2:hops]) = gather_swapping(
        cotangent, "disp", [halo_across, *rights[2:hops]]
    )
    halos, halo_order = gather_joining([halo, halo_across], "disp")

    pad_rows = -(-3 * groups // 8) * 8
    fold = np.zeros((pad_rows, 3 * size), np.float32)
    fold[np.arange(3 * size) // width, np.arange(3 * size)] = 1

    block = (channels, width, rows)
    wide = (channels, (hops + 1) * width, rows)
    moved = [*cots, *halos, *rights]
    cot_wide, right_wide, total = run(
        functools.partial(kernel_sums, parts, hops, halo_order),
        [(SMEM, places)]
        + [(HBM, item) for item in moved]
        + [(VMEM, left_own), (VMEM, jnp.asarray(fold))],
        [((D + 2, span, rows), bf16), (wide, f32), ((3, pad_rows, 3 * outs), f32)],
        [
            pltpu.VMEM((parts, *cotangent.shape), bf16),
            pltpu.VMEM((parts, levels, 2 * outs, rows), bf16),
            pltpu.VMEM((hops + 1, *block), bf16),
            pltpu.VMEM((D, 3, size, rows), f32),
            pltpu.VMEM((3, span, 3 * size), f32),
            pltpu.SemaphoreType.DMA((len(moved),)),
        ],
        20, 8000000000,
    )
    bits = [1 << k for k in reversed(range(columns.bit_length() - 1))]
    left_part, grad_part, *sent = run(
        functools.partial(upper_grads, far),
        [(VMEM, item) for item in (left_own, weights, cot_wide, right_wide)],
        [(block, f32), ((channels, (near + 1) * width, rows), f32), *[(block, bf16)] * far],
        [pltpu.VMEM(block, f32), pltpu.VMEM(wide, f32)],
        12, 8000000000,
    )
    total = total_swapping(total, bits[0])
    *sent, grad_part, total = lax.optimization_barrier((*sent, grad_part, total))
    arrived = {
        hop: shifted(value, "col", -hop) for hop, value in zip(range(hops, near, -1), sent)
    }
    grad_left, own, *sent = run(
        functools.partial(lower_grads, near),
        [
            (VMEM, item)
            for item in (left_own, weights, cot_wide, right_wide, left_part, grad_part)
        ],
        [(block, bf16), (block, f32), *[(block, bf16)] * near],
        [
            pltpu.VMEM(block, f32),
            pltpu.VMEM(block, f32),
            pltpu.VMEM((channels, (near + 1) * width, rows), f32),
        ],
        12, 8000000000,
    )
    total = total_swapping(total, bits[1])
    sent, arrived[hops], arrived[hops - 1], total = lax.optimization_barrier(
        (sent, arrived[hops], arrived[hops - 1], total)
    )
    arrived.update(
        {hop: shifted(value, "col", -hop) for hop, value in zip(range(near, 0, -1), sent)}
    )
    for bit in bits[2:]:
        total = total_swapping(total, bit)
    total, arrived[1] = lax.optimization_barrier((total, arrived[1]))

    total_right = own
    for hop in range(1, hops + 1):
        total_right = total_right + jnp.where(
            column + hop < columns, arrived[hop].astype(f32), 0.0
        )

    pieces = jnp.stack(gather_swapping(total, "disp")[0])
    pieces = pieces[jnp.arange(parts) ^ part][:, :, : 3 * groups]
    total = pieces.reshape(parts, 3, 3, groups, 3, outs)
    cell_count = D * width * columns * rows
    grad_kernel = jnp.transpose(total, (4, 1, 2, 5, 0, 3))[::-1].reshape(3, 3, 3, outs, G)
    grad_kernel = grad_kernel * (1.0 / math.sqrt(cell_count))
    return (grad_left, total_right.astype(bf16), grad_kernel)


def solution(mesh):
    return jax.shard_map(
        body,
        mesh=mesh,
        in_specs=(P(None, "col", None), P(None, "col", None), P(), P(None, "disp", "col", None)),
        out_specs=(P("disp", "col", None), P("disp", "col", None), P()),
        check_vma=False,
    )
```

```python
import functools
import math

import jax
import jax.numpy as jnp
import numpy as np
from jax import lax
from jax.experimental import pallas as pl
from jax.experimental.pallas import tpu as pltpu
from jax.sharding import PartitionSpec as P

C = 320
G = 40
D = 48
GROUP = C // G
HIGHEST = lax.Precision.HIGHEST


def shifted(value, axis, steps):
    count = lax.axis_size(axis)
    return lax.ppermute(value, axis, [(source, (source + steps) % count) for source in range(count)])


def conv_rows(outs, width):
    main = np.tile(np.arange(width), outs)
    return np.concatenate([main, np.full(outs, -1), np.full(outs, width)])


def toeplitz(kernel_local, width):
    outs, groups = kernel_local.shape[3:]
    row_col = conv_rows(outs, width)
    row_out = np.concatenate([np.repeat(np.arange(outs), width), np.tile(np.arange(outs), 2)])
    spread = np.zeros((outs, row_col.size), np.float32)
    spread[row_out, np.arange(row_col.size)] = 1
    taps = jnp.transpose(kernel_local[::-1], (1, 2, 4, 0, 3))
    wide = jnp.einsum(
        "qrgpo,ok->qrgpk", taps, jnp.asarray(spread, jnp.bfloat16),
        preferred_element_type=jnp.float32,
    ).astype(jnp.bfloat16)
    out_col = np.arange(width)
    column_tap = out_col[:, None] - row_col[None, :] + 1
    total = jnp.zeros((3, groups, width, 3, row_col.size), jnp.bfloat16)
    for tap in range(3):
        mask = jnp.asarray(column_tap == tap)[None, None, :, None, :]
        total = jnp.where(mask, wide[tap][:, :, None], total)
    return total.reshape(3 * groups * width, 3 * row_col.size)


def roll_zero(value, steps):
    size = value.shape[-1]
    lane = lax.broadcasted_iota(jnp.int32, value.shape, value.ndim - 1)
    moved = pltpu.roll(value, steps % size, value.ndim - 1)
    return jnp.where(lane == (0 if steps > 0 else size - 1), 0.0, moved)


def pack(cot_ref, halo_ref, packed_ref):
    outs, levels, width, rows = cot_ref.shape
    main = outs * width

    def step(level, carry):
        packed_ref[level, 0:main] = cot_ref[:, level].reshape(main, rows)
        packed_ref[level, main:] = halo_ref[level]
        return carry

    lax.fori_loop(0, levels, step, 0)


def add_grads(first_level, count, reach, skipped, cot_s, weight_ref, left_s, right_s, left_sum, grad_s):
    channels, width, rows = left_s.shape
    groups = channels // GROUP
    size = groups * width
    span = cot_s.shape[1]
    f32, bf16 = jnp.float32, jnp.bfloat16

    def pair_values(at):
        near = cot_s[pl.ds(at, 3)].reshape(3 * span, rows)
        far = cot_s[pl.ds(at + 1, 3)].reshape(3 * span, rows)
        result = jnp.dot(
            weight_ref[...], jnp.concatenate([near, far], axis=1), preferred_element_type=f32
        )
        values = []
        for half in range(2):
            part = result[:, half * rows : (half + 1) * rows]
            total = (
                part[size : 2 * size]
                + roll_zero(part[:size], -1)
                + roll_zero(part[2 * size :], 1)
            )
            values.append(total.astype(bf16).astype(f32))
        return values

    def step(number, carry):
        level = first_level + number * width
        base = reach - first_level - width - number * width
        rights = right_s.at[:, pl.ds(pl.multiple_of(base, width), 2 * width)]
        grads = grad_s.at[:, pl.ds(pl.multiple_of(base - skipped, width), 2 * width)]

        def use(pair, values):
            at = width - 2 * pair
            for group in range(groups):
                ones = [value[group * width : (group + 1) * width] for value in values]
                for c in range(group * GROUP, (group + 1) * GROUP):
                    left = left_s[c]
                    left_sum[c] += (
                        ones[0] * rights[c, at : at + width]
                        + ones[1] * rights[c, at - 1 : at - 1 + width]
                    )
                    grads[c, at : at + width] += ones[0] * left
                    grads[c, at - 1 : at - 1 + width] += ones[1] * left

        waiting = pair_values(level)
        for pair in range(1, width // 2):
            later = pair_values(level + 2 * pair)
            use(pair - 1, waiting)
            waiting = later
        use(width // 2 - 1, waiting)
        return carry

    lax.fori_loop(0, count // width, step, 0)


def upper_grads(keys, reach, far, places, *refs):
    block_refs, refs = refs[: len(keys)], refs[len(keys) :]
    right_refs, refs = refs[: far + 1], refs[far + 1 :]
    left_ref, weight_ref, cot_s, left_sum, grad_out = refs[:5]
    sent_refs, (left_s, right_s, grad_s, sems) = refs[5 : 5 + far], refs[5 + far :]
    channels, width, rows = left_ref.shape
    levels, span = block_refs[0].shape[:2]
    f32, bf16 = jnp.float32, jnp.bfloat16

    copies = []
    for at, (key, source) in enumerate(zip(keys, block_refs)):
        start = (places[0] ^ key) * levels + 1
        copies.append(pltpu.make_async_copy(source, cot_s.at[pl.ds(start, levels)], sems.at[at]))
    for copy in copies:
        copy.start()
    cot_s[0] = jnp.zeros((span, rows), bf16)
    cot_s[D + 1] = jnp.zeros((span, rows), bf16)
    left_s[...] = left_ref[...].astype(f32)
    left_sum[...] = jnp.zeros(left_sum.shape, f32)
    grad_s[...] = jnp.zeros(grad_s.shape, f32)
    hops = reach // width
    for at in range(far + 1):
        block = right_refs[at][...].astype(f32)
        right_s[:, at * width : (at + 1) * width] = jnp.where(places[1] >= hops - at, block, 0.0)
    for copy in copies:
        copy.wait()
    add_grads(
        D // 2, D // 2, reach, 0, cot_s, weight_ref, left_s, right_s, left_sum, grad_s
    )
    grad_out[...] = grad_s[:, far * width :]
    for at in range(far):
        sent_refs[at][...] = (
            grad_s[:, at * width : (at + 1) * width] * (1.0 / GROUP)
        ).astype(bf16)


def lower_grads(
    first_level, count, reach, skipped, left_ref, weight_ref, cot_s, right_s, left_part, grad_part,
    left_out, grad_out, *rest
):
    sent_refs, (left_s, left_sum, grad_s) = rest[:-3], rest[-3:]
    channels, width, rows = left_ref.shape
    f32, bf16 = jnp.float32, jnp.bfloat16
    last = first_level == 0
    scale = 1.0 / GROUP if last else 1.0
    left_s[...] = left_ref[...].astype(f32)
    left_sum[...] = left_part[...]
    grad_s[...] = grad_part[...]
    add_grads(
        first_level, count, reach, skipped, cot_s, weight_ref, left_s, right_s, left_sum, grad_s
    )
    left_out[...] = (left_sum[...] * scale).astype(left_out.dtype)
    grad_out[...] = grad_s[:, len(sent_refs) * width :] * scale
    for at, sent_ref in enumerate(sent_refs):
        sent_ref[...] = (grad_s[:, at * width : (at + 1) * width] * (1.0 / GROUP)).astype(bf16)


def kernel_sums(hops, places, *refs):
    right_refs, (left_ref, cot_s, fold_ref, right_s, sums_ref, left_s, prod_s) = (
        refs[: hops + 1], refs[hops + 1 :],
    )
    channels, width, rows = left_ref.shape
    groups = channels // GROUP
    span = cot_s.shape[1]
    outs = span // (width + 2)
    main = outs * width
    size = groups * width
    reach = hops * width
    f32, bf16 = jnp.float32, jnp.bfloat16

    left_s[...] = left_ref[...].astype(f32)
    for hop in range(hops + 1):
        at = reach - hop * width
        block = right_refs[hop][...].astype(f32)
        right_s[:, at : at + width] = jnp.where(places[1] >= hop, block, 0.0)
    prod_s[...] = jnp.zeros(prod_s.shape, f32)
    chunk = width // 2

    def step(number, carry):
        level = number * width
        base = pl.multiple_of(reach - width - level, width)
        rights = right_s.at[:, pl.ds(base, 2 * width)]

        def volume_at(d):
            at = width - d
            shifts = ([], [], [])
            for group in range(groups):
                total = None
                for c in range(group * GROUP, (group + 1) * GROUP):
                    term = left_s[c] * rights[c, at : at + width]
                    total = term if total is None else total + term
                value = (total * (1.0 / GROUP)).astype(bf16).astype(f32)
                shifts[0].append(roll_zero(value, 1))
                shifts[1].append(value)
                shifts[2].append(roll_zero(value, -1))
            return jnp.concatenate(shifts[0] + shifts[1] + shifts[2], axis=0).astype(bf16)

        for half in range(2):
            first = half * chunk
            volume = jnp.concatenate([volume_at(first + k) for k in range(chunk)], axis=1)
            for tap in range(3):
                value = jnp.concatenate(
                    [cot_s[level + first + k + tap] for k in range(chunk)], axis=1
                )
                prod_s[tap] += lax.dot_general(
                    value, volume, (((1,), (1,)), ((), ())), preferred_element_type=f32
                )
        return carry

    lax.fori_loop(0, D // width, step, 0)

    col_in = lax.broadcasted_iota(jnp.int32, (width, 3 * size), 0)
    col_out = lax.broadcasted_iota(jnp.int32, (width, 3 * size), 1) % width
    edge = lax.broadcasted_iota(jnp.int32, (outs, 3 * size), 1) % width
    for column_tap in range(3):
        mask = col_out - col_in + 1 == column_tap
        taps = []
        for tap in range(3):
            value = prod_s[tap, 0:main].reshape(outs, width, 3 * size)
            total = jnp.sum(jnp.where(mask[None], value, 0.0), axis=1)
            if column_tap == 2:
                total = total + jnp.where(edge == 0, prod_s[tap, main : main + outs], 0.0)
            if column_tap == 0:
                total = total + jnp.where(edge == width - 1, prod_s[tap, main + outs : span], 0.0)
            taps.append(total)
        gathered = jnp.concatenate(taps, axis=0)
        sums_ref[column_tap] = lax.dot_general(
            fold_ref[...], gathered, (((1,), (1,)), ((), ())),
            precision=HIGHEST, preferred_element_type=f32,
        )


VMEM = pl.BlockSpec(memory_space=pltpu.VMEM)
SMEM = pl.BlockSpec(memory_space=pltpu.SMEM)
ANY = pl.BlockSpec(memory_space=pl.ANY)
MIB = 1024 * 1024


def run(function, operands, outs, scratch, limit, flops):
    return pl.pallas_call(
        function,
        out_shape=[jax.ShapeDtypeStruct(shape, kind) for shape, kind in outs],
        in_specs=[space for space, array in operands],
        out_specs=[VMEM] * len(outs),
        scratch_shapes=scratch,
        compiler_params=pltpu.CompilerParams(vmem_limit_bytes=limit * MIB),
        cost_estimate=pl.CostEstimate(flops=flops, bytes_accessed=1024, transcendentals=0),
    )(*[array for space, array in operands])


def swapped(value, axis, bit):
    count = lax.axis_size(axis)
    return lax.ppermute(value, axis, [(source, source ^ bit) for source in range(count)])


def gather_swapping(value, axis, last_bit=1):
    held = {0: value}
    bit = lax.axis_size(axis) // 2
    while bit >= last_bit:
        held.update({key | bit: swapped(item, axis, bit) for key, item in list(held.items())})
        bit //= 2
    return held


def total_swapping(value, bit):
    return value + swapped(value, "col", bit)


def body(left, right, kernel, cotangent):
    outs, levels, width, rows = cotangent.shape
    parts = lax.axis_size("disp")
    columns = lax.axis_size("col")
    channels = C // parts
    groups = G // parts
    size = groups * width
    span = outs * (width + 2)
    hops = (D + width - 2) // width
    far = D // 2 // width
    first = (hops // 2, hops // 2 + 1)
    near = hops - far
    part, column = lax.axis_index("disp"), lax.axis_index("col")
    places = jnp.stack([part, column]).astype(jnp.int32)
    f32, bf16 = jnp.float32, jnp.bfloat16

    low = jnp.transpose(cotangent[:, :, width - 1], (1, 0, 2))
    high = jnp.transpose(cotangent[:, :, 0], (1, 0, 2))
    low, high, right = lax.optimization_barrier((low, high, right))
    low, high = shifted(low, "col", 1), shifted(high, "col", -1)
    cots = gather_swapping(cotangent, "disp", 2)
    right_own = lax.dynamic_slice_in_dim(right, part * channels, channels, 0)
    left_own = lax.dynamic_slice_in_dim(left, part * channels, channels, 0)
    weights = toeplitz(lax.dynamic_slice_in_dim(kernel, part * groups, groups, 4), width)
    rights = [right_own] + [None] * hops
    for hop in (4, 3):
        rights[hop] = shifted(right_own, "col", hop)
    right_late, low, high, left_own, weights, *rights[3:5] = lax.optimization_barrier(
        (right_own, low, high, left_own, weights, *rights[3:5])
    )
    low = jnp.where(column > 0, low, 0).astype(bf16)
    high = jnp.where(column < columns - 1, high, 0).astype(bf16)
    halos = gather_swapping(jnp.concatenate([low, high], axis=1), "disp", 2)
    for hop in (5, 6):
        rights[hop] = shifted(right_late, "col", hop)
    blocks = {}
    across = parts // 2
    cots[across], *rights[5:] = lax.optimization_barrier((cots[across], *rights[5:]))
    for key in cots:
        (block,) = run(
            pack, [(VMEM, cots[key]), (VMEM, halos[key])],
            [((levels, span, rows), bf16)], [], 4, 1000000000,
        )
        if key == across:
            right_last = lax.optimization_barrier((right_own, block))[0]
        blocks[key] = block
        blocks[key | 1] = swapped(block, "disp", 1)
    for hop in (2, 1):
        rights[hop] = shifted(right_last, "col", hop)

    pad_rows = -(-3 * groups // 8) * 8
    fold = np.zeros((pad_rows, 3 * size), np.float32)
    fold[np.arange(3 * size) // width, np.arange(3 * size)] = 1

    block = (channels, width, rows)
    wide = (channels, (hops + 1) * width, rows)
    f32_block, bf16_block = (block, f32), (block, bf16)
    reach = hops * width
    keys = sorted(blocks)
    cot_wide, left_part, grad_part, *sent = run(
        functools.partial(upper_grads, keys, reach, far),
        [(SMEM, places)]
        + [(ANY, blocks[key]) for key in keys]
        + [(VMEM, rights[hop]) for hop in range(hops, near - 1, -1)]
        + [(VMEM, left_own), (VMEM, weights)],
        [
            ((D + 2, span, rows), bf16),
            f32_block,
            ((channels, (near + 1) * width, rows), f32),
            *[bf16_block] * far,
        ],
        [
            pltpu.VMEM(block, f32),
            pltpu.VMEM((channels, (far + 1) * width, rows), f32),
            pltpu.VMEM(wide, f32),
            pltpu.SemaphoreType.DMA((parts,)),
        ],
        12, 8000000000,
    )
    arrived = {
        hop: shifted(value, "col", -hop) for hop, value in zip(range(hops, near, -1), sent)
    }
    right_wide, total = run(
        functools.partial(kernel_sums, hops),
        [(SMEM, places)]
        + [(VMEM, item) for item in (*rights, left_own, cot_wide, jnp.asarray(fold))],
        [(wide, f32), ((3, pad_rows, 3 * outs), f32)],
        [pltpu.VMEM(block, f32), pltpu.VMEM((3, span, 3 * size), f32)],
        12, 8000000000,
    )
    bits = [1 << k for k in reversed(range(columns.bit_length() - 1))]
    middle = near - 1

    def lower(first_level, count, done, kind, left_part, grad_part):
        skipped = (far + done) * width
        rest = near + 1 - done
        complete = rest - 1 if first_level == 0 else rest - 2
        return run(
            functools.partial(lower_grads, first_level, count, reach, skipped),
            [
                (VMEM, item)
                for item in (left_own, weights, cot_wide, right_wide, left_part, grad_part)
            ],
            [
                (block, kind),
                ((channels, (rest - complete) * width, rows), f32),
                *[bf16_block] * complete,
            ],
            [
                pltpu.VMEM(block, f32),
                pltpu.VMEM(block, f32),
                pltpu.VMEM((channels, rest * width, rows), f32),
            ],
            8, 4000000000,
        )

    grad_part, total, arrived[hops], arrived[hops - 1] = lax.optimization_barrier(
        (grad_part, total, arrived[hops], arrived[hops - 1])
    )
    left_part, grad_part, *sent = lower(width, D // 2 - width, 0, f32, left_part, grad_part)
    total = total_swapping(total, bits[0])
    sent, grad_part, total, arrived[hops - 2] = lax.optimization_barrier(
        (sent, grad_part, total, arrived[hops - 2])
    )
    arrived.update(
        {hop: shifted(value, "col", -hop) for hop, value in zip(range(near, 1, -1), sent)}
    )
    grad_left, own, *sent = lower(0, width, middle, bf16, left_part, grad_part)
    total = total_swapping(total, bits[1])
    arrived[1] = shifted(sent[0], "col", -1)
    for bit in bits[2:]:
        total = total_swapping(total, bit)
    total, arrived[1] = lax.optimization_barrier((total, arrived[1]))

    total_right = own
    for hop in range(1, hops + 1):
        total_right = total_right + jnp.where(
            column + hop < columns, arrived[hop].astype(f32), 0.0
        )

    held = gather_swapping(total, "disp")
    pieces = jnp.stack([held[key] for key in sorted(held)])
    pieces = pieces[jnp.arange(parts) ^ part][:, :, : 3 * groups]
    total = pieces.reshape(parts, 3, 3, groups, 3, outs)
    cell_count = D * width * columns * rows
    grad_kernel = jnp.transpose(total, (4, 1, 2, 5, 0, 3))[::-1].reshape(3, 3, 3, outs, G)
    grad_kernel = grad_kernel * (1.0 / math.sqrt(cell_count))
    return (grad_left, total_right.astype(bf16), grad_kernel)


def solution(mesh):
    return jax.shard_map(
        body,
        mesh=mesh,
        in_specs=(P(None, "col", None), P(None, "col", None), P(), P(None, "disp", "col", None)),
        out_specs=(P("disp", "col", None), P("disp", "col", None), P()),
        check_vma=False,
    )
```

```python
import functools
import math

import jax
import jax.numpy as jnp
import numpy as np
from jax import lax
from jax.experimental import pallas as pl
from jax.experimental.pallas import tpu as pltpu
from jax.sharding import PartitionSpec as P

C = 320
G = 40
D = 48
GROUP = C // G
HIGHEST = lax.Precision.HIGHEST


def shifted(value, axis, steps):
    count = lax.axis_size(axis)
    return lax.ppermute(value, axis, [(source, (source + steps) % count) for source in range(count)])


def conv_rows(outs, width):
    main = np.tile(np.arange(width), outs)
    return np.concatenate([main, np.full(outs, -1), np.full(outs, width)])


def toeplitz(kernel_local, width):
    outs, groups = kernel_local.shape[3:]
    row_col = conv_rows(outs, width)
    row_out = np.concatenate([np.repeat(np.arange(outs), width), np.tile(np.arange(outs), 2)])
    spread = np.zeros((outs, row_col.size), np.float32)
    spread[row_out, np.arange(row_col.size)] = 1
    taps = jnp.transpose(kernel_local[::-1], (1, 2, 4, 0, 3))
    wide = jnp.einsum(
        "qrgpo,ok->qrgpk", taps, jnp.asarray(spread, jnp.bfloat16),
        preferred_element_type=jnp.float32,
    ).astype(jnp.bfloat16)
    out_col = np.arange(width)
    column_tap = out_col[:, None] - row_col[None, :] + 1
    total = jnp.zeros((3, groups, width, 3, row_col.size), jnp.bfloat16)
    for tap in range(3):
        mask = jnp.asarray(column_tap == tap)[None, None, :, None, :]
        total = jnp.where(mask, wide[tap][:, :, None], total)
    return total.reshape(3 * groups * width, 3 * row_col.size)


def roll_zero(value, steps):
    size = value.shape[-1]
    lane = lax.broadcasted_iota(jnp.int32, value.shape, value.ndim - 1)
    moved = pltpu.roll(value, steps % size, value.ndim - 1)
    return jnp.where(lane == (0 if steps > 0 else size - 1), 0.0, moved)


def pack(cot_ref, halo_ref, packed_ref):
    outs, levels, width, rows = cot_ref.shape
    main = outs * width

    def step(level, carry):
        packed_ref[level, 0:main] = cot_ref[:, level].reshape(main, rows)
        packed_ref[level, main:] = halo_ref[level]
        return carry

    lax.fori_loop(0, levels, step, 0)


def add_grads(first_level, count, reach, skipped, cot_s, weight_ref, left_s, right_s, left_sum, grad_s):
    channels, width, rows = left_s.shape
    groups = channels // GROUP
    size = groups * width
    span = cot_s.shape[1]
    f32, bf16 = jnp.float32, jnp.bfloat16

    def pair_values(at):
        near = cot_s[pl.ds(at, 3)].reshape(3 * span, rows)
        far = cot_s[pl.ds(at + 1, 3)].reshape(3 * span, rows)
        result = jnp.dot(
            weight_ref[...], jnp.concatenate([near, far], axis=1), preferred_element_type=f32
        )
        values = []
        for half in range(2):
            part = result[:, half * rows : (half + 1) * rows]
            total = (
                part[size : 2 * size]
                + roll_zero(part[:size], -1)
                + roll_zero(part[2 * size :], 1)
            )
            values.append(total.astype(bf16).astype(f32))
        return values

    def step(number, carry):
        level = first_level + number * width
        base = reach - first_level - width - number * width
        rights = right_s.at[:, pl.ds(pl.multiple_of(base, width), 2 * width)]
        grads = grad_s.at[:, pl.ds(pl.multiple_of(base - skipped, width), 2 * width)]

        def use(pair, values):
            at = width - 2 * pair
            for group in range(groups):
                ones = [value[group * width : (group + 1) * width] for value in values]
                for c in range(group * GROUP, (group + 1) * GROUP):
                    left = left_s[c]
                    left_sum[c] += (
                        ones[0] * rights[c, at : at + width]
                        + ones[1] * rights[c, at - 1 : at - 1 + width]
                    )
                    grads[c, at : at + width] += ones[0] * left
                    grads[c, at - 1 : at - 1 + width] += ones[1] * left

        waiting = pair_values(level)
        for pair in range(1, width // 2):
            later = pair_values(level + 2 * pair)
            use(pair - 1, waiting)
            waiting = later
        use(width // 2 - 1, waiting)
        return carry

    lax.fori_loop(0, count // width, step, 0)


def upper_grads(keys, reach, far, places, *refs):
    block_refs, refs = refs[: len(keys)], refs[len(keys) :]
    right_refs, refs = refs[: far + 1], refs[far + 1 :]
    left_ref, weight_ref, cot_s, left_sum, grad_out = refs[:5]
    sent_refs, (left_s, right_s, grad_s, sems) = refs[5 : 5 + far], refs[5 + far :]
    channels, width, rows = left_ref.shape
    levels, span = block_refs[0].shape[:2]
    f32, bf16 = jnp.float32, jnp.bfloat16

    copies = []
    for at, (key, source) in enumerate(zip(keys, block_refs)):
        start = (places[0] ^ key) * levels + 1
        copies.append(pltpu.make_async_copy(source, cot_s.at[pl.ds(start, levels)], sems.at[at]))
    for copy in copies:
        copy.start()
    cot_s[0] = jnp.zeros((span, rows), bf16)
    cot_s[D + 1] = jnp.zeros((span, rows), bf16)
    left_s[...] = left_ref[...].astype(f32)
    left_sum[...] = jnp.zeros(left_sum.shape, f32)
    grad_s[...] = jnp.zeros(grad_s.shape, f32)
    hops = reach // width
    for at in range(far + 1):
        block = right_refs[at][...].astype(f32)
        right_s[:, at * width : (at + 1) * width] = jnp.where(places[1] >= hops - at, block, 0.0)
    for copy in copies:
        copy.wait()
    add_grads(
        D // 2, D // 2, reach, 0, cot_s, weight_ref, left_s, right_s, left_sum, grad_s
    )
    grad_out[...] = grad_s[:, far * width :]
    for at in range(far):
        sent_refs[at][...] = (
            grad_s[:, at * width : (at + 1) * width] * (1.0 / GROUP)
        ).astype(bf16)


def lower_grads(
    first_level, count, reach, skipped, left_ref, weight_ref, cot_s, right_s, left_part, grad_part,
    left_out, grad_out, *rest
):
    sent_refs, (left_s, left_sum, grad_s) = rest[:-3], rest[-3:]
    channels, width, rows = left_ref.shape
    f32, bf16 = jnp.float32, jnp.bfloat16
    last = first_level == 0
    scale = 1.0 / GROUP if last else 1.0
    left_s[...] = left_ref[...].astype(f32)
    left_sum[...] = left_part[...]
    grad_s[...] = grad_part[...]
    add_grads(
        first_level, count, reach, skipped, cot_s, weight_ref, left_s, right_s, left_sum, grad_s
    )
    left_out[...] = (left_sum[...] * scale).astype(left_out.dtype)
    grad_out[...] = grad_s[:, len(sent_refs) * width :] * scale
    for at, sent_ref in enumerate(sent_refs):
        sent_ref[...] = (grad_s[:, at * width : (at + 1) * width] * (1.0 / GROUP)).astype(bf16)


def kernel_sums(hops, places, *refs):
    right_refs, (left_ref, cot_s, fold_ref, right_s, sums_ref, left_s, prod_s) = (
        refs[: hops + 1], refs[hops + 1 :],
    )
    channels, width, rows = left_ref.shape
    groups = channels // GROUP
    span = cot_s.shape[1]
    outs = span // (width + 2)
    main = outs * width
    size = groups * width
    reach = hops * width
    f32, bf16 = jnp.float32, jnp.bfloat16

    left_s[...] = left_ref[...].astype(f32)
    for hop in range(hops + 1):
        at = reach - hop * width
        block = right_refs[hop][...].astype(f32)
        right_s[:, at : at + width] = jnp.where(places[1] >= hop, block, 0.0)
    prod_s[...] = jnp.zeros(prod_s.shape, f32)
    chunk = width // 2

    def step(number, carry):
        level = number * width
        base = pl.multiple_of(reach - width - level, width)
        rights = right_s.at[:, pl.ds(base, 2 * width)]

        def volume_at(d):
            at = width - d
            shifts = ([], [], [])
            for group in range(groups):
                total = None
                for c in range(group * GROUP, (group + 1) * GROUP):
                    term = left_s[c] * rights[c, at : at + width]
                    total = term if total is None else total + term
                value = (total * (1.0 / GROUP)).astype(bf16).astype(f32)
                shifts[0].append(roll_zero(value, 1))
                shifts[1].append(value)
                shifts[2].append(roll_zero(value, -1))
            return jnp.concatenate(shifts[0] + shifts[1] + shifts[2], axis=0).astype(bf16)

        for half in range(2):
            first = half * chunk
            volume = jnp.concatenate([volume_at(first + k) for k in range(chunk)], axis=1)
            for tap in range(3):
                value = jnp.concatenate(
                    [cot_s[level + first + k + tap] for k in range(chunk)], axis=1
                )
                prod_s[tap] += lax.dot_general(
                    value, volume, (((1,), (1,)), ((), ())), preferred_element_type=f32
                )
        return carry

    lax.fori_loop(0, D // width, step, 0)

    col_in = lax.broadcasted_iota(jnp.int32, (width, 3 * size), 0)
    col_out = lax.broadcasted_iota(jnp.int32, (width, 3 * size), 1) % width
    edge = lax.broadcasted_iota(jnp.int32, (outs, 3 * size), 1) % width
    for column_tap in range(3):
        mask = col_out - col_in + 1 == column_tap
        taps = []
        for tap in range(3):
            value = prod_s[tap, 0:main].reshape(outs, width, 3 * size)
            total = jnp.sum(jnp.where(mask[None], value, 0.0), axis=1)
            if column_tap == 2:
                total = total + jnp.where(edge == 0, prod_s[tap, main : main + outs], 0.0)
            if column_tap == 0:
                total = total + jnp.where(edge == width - 1, prod_s[tap, main + outs : span], 0.0)
            taps.append(total)
        gathered = jnp.concatenate(taps, axis=0)
        sums_ref[column_tap] = lax.dot_general(
            fold_ref[...], gathered, (((1,), (1,)), ((), ())),
            precision=HIGHEST, preferred_element_type=f32,
        )


VMEM = pl.BlockSpec(memory_space=pltpu.VMEM)
SMEM = pl.BlockSpec(memory_space=pltpu.SMEM)
ANY = pl.BlockSpec(memory_space=pl.ANY)
MIB = 1024 * 1024


def run(function, operands, outs, scratch, limit, flops):
    return pl.pallas_call(
        function,
        out_shape=[jax.ShapeDtypeStruct(shape, kind) for shape, kind in outs],
        in_specs=[space for space, array in operands],
        out_specs=[VMEM] * len(outs),
        scratch_shapes=scratch,
        compiler_params=pltpu.CompilerParams(vmem_limit_bytes=limit * MIB),
        cost_estimate=pl.CostEstimate(flops=flops, bytes_accessed=1024, transcendentals=0),
    )(*[array for space, array in operands])


def swapped(value, axis, bit):
    count = lax.axis_size(axis)
    return lax.ppermute(value, axis, [(source, source ^ bit) for source in range(count)])


def gather_swapping(value, axis, last_bit=1):
    held = {0: value}
    bit = lax.axis_size(axis) // 2
    while bit >= last_bit:
        held.update({key | bit: swapped(item, axis, bit) for key, item in list(held.items())})
        bit //= 2
    return held


def total_swapping(value, bit):
    return value + swapped(value, "col", bit)


def body(left, right, kernel, cotangent):
    outs, levels, width, rows = cotangent.shape
    parts = lax.axis_size("disp")
    columns = lax.axis_size("col")
    channels = C // parts
    groups = G // parts
    size = groups * width
    span = outs * (width + 2)
    hops = (D + width - 2) // width
    far = D // 2 // width
    first = (hops // 2, hops // 2 + 1)
    near = hops - far
    part, column = lax.axis_index("disp"), lax.axis_index("col")
    places = jnp.stack([part, column]).astype(jnp.int32)
    f32, bf16 = jnp.float32, jnp.bfloat16

    low = jnp.transpose(cotangent[:, :, width - 1], (1, 0, 2))
    high = jnp.transpose(cotangent[:, :, 0], (1, 0, 2))
    low, high, right = lax.optimization_barrier((low, high, right))
    low, high = shifted(low, "col", 1), shifted(high, "col", -1)
    cots = gather_swapping(cotangent, "disp", 2)
    right_own = lax.dynamic_slice_in_dim(right, part * channels, channels, 0)
    left_own = lax.dynamic_slice_in_dim(left, part * channels, channels, 0)
    weights = toeplitz(lax.dynamic_slice_in_dim(kernel, part * groups, groups, 4), width)
    rights = [right_own] + [None] * hops
    for hop in (4, 3):
        rights[hop] = shifted(right_own, "col", hop)
    right_late, rights[4] = lax.optimization_barrier((right_own, rights[4]))
    low, high, left_own, weights = lax.optimization_barrier((low, high, left_own, weights))
    low = jnp.where(column > 0, low, 0).astype(bf16)
    high = jnp.where(column < columns - 1, high, 0).astype(bf16)
    halos = gather_swapping(jnp.concatenate([low, high], axis=1), "disp", 2)
    for hop in (5, 6, 2, 1):
        rights[hop] = shifted(right_late, "col", hop)
    blocks = {}
    across = parts // 2
    cots[across], *rights[1:] = lax.optimization_barrier((cots[across], *rights[1:]))
    for key in cots:
        (block,) = run(
            pack, [(VMEM, cots[key]), (VMEM, halos[key])],
            [((levels, span, rows), bf16)], [], 4, 1000000000,
        )
        blocks[key] = block
        blocks[key | 1] = swapped(block, "disp", 1)

    pad_rows = -(-3 * groups // 8) * 8
    fold = np.zeros((pad_rows, 3 * size), np.float32)
    fold[np.arange(3 * size) // width, np.arange(3 * size)] = 1

    block = (channels, width, rows)
    wide = (channels, (hops + 1) * width, rows)
    f32_block, bf16_block = (block, f32), (block, bf16)
    reach = hops * width
    keys = sorted(blocks)
    cot_wide, left_part, grad_part, *sent = run(
        functools.partial(upper_grads, keys, reach, far),
        [(SMEM, places)]
        + [(ANY, blocks[key]) for key in keys]
        + [(VMEM, rights[hop]) for hop in range(hops, near - 1, -1)]
        + [(VMEM, left_own), (VMEM, weights)],
        [
            ((D + 2, span, rows), bf16),
            f32_block,
            ((channels, (near + 1) * width, rows), f32),
            *[bf16_block] * far,
        ],
        [
            pltpu.VMEM(block, f32),
            pltpu.VMEM((channels, (far + 1) * width, rows), f32),
            pltpu.VMEM(wide, f32),
            pltpu.SemaphoreType.DMA((parts,)),
        ],
        12, 8000000000,
    )
    arrived = {
        hop: shifted(value, "col", -hop) for hop, value in zip(range(hops, near, -1), sent)
    }
    right_wide, total = run(
        functools.partial(kernel_sums, hops),
        [(SMEM, places)]
        + [(VMEM, item) for item in (*rights, left_own, cot_wide, jnp.asarray(fold))],
        [(wide, f32), ((3, pad_rows, 3 * outs), f32)],
        [pltpu.VMEM(block, f32), pltpu.VMEM((3, span, 3 * size), f32)],
        12, 8000000000,
    )
    bits = [1 << k for k in reversed(range(columns.bit_length() - 1))]
    middle = near - 1

    def lower(first_level, count, done, kind, left_part, grad_part):
        skipped = (far + done) * width
        rest = near + 1 - done
        complete = rest - 1 if first_level == 0 else rest - 2
        return run(
            functools.partial(lower_grads, first_level, count, reach, skipped),
            [
                (VMEM, item)
                for item in (left_own, weights, cot_wide, right_wide, left_part, grad_part)
            ],
            [
                (block, kind),
                ((channels, (rest - complete) * width, rows), f32),
                *[bf16_block] * complete,
            ],
            [
                pltpu.VMEM(block, f32),
                pltpu.VMEM(block, f32),
                pltpu.VMEM((channels, rest * width, rows), f32),
            ],
            8, 1000000,
        )

    grad_part, total = lax.optimization_barrier((grad_part, total))
    left_part, grad_part, *sent = lower(width, D // 2 - width, 0, f32, left_part, grad_part)
    total = total_swapping(total, bits[0])
    sent, grad_part, total, arrived[near + 1] = lax.optimization_barrier(
        (sent, grad_part, total, arrived[near + 1])
    )
    sent, *items = lax.optimization_barrier((sent, *[arrived[hop] for hop in sorted(arrived)]))
    arrived = dict(zip(sorted(arrived), items))
    arrived.update(
        {hop: shifted(value, "col", -hop) for hop, value in zip(range(near, 1, -1), sent)}
    )
    grad_left, own, *sent = lower(0, width, middle, bf16, left_part, grad_part)
    total = total_swapping(total, bits[1])
    sent, total = lax.optimization_barrier((sent, total))
    arrived[1] = shifted(sent[0], "col", -1)
    for bit in bits[2:]:
        total = total_swapping(total, bit)
    total, arrived[1] = lax.optimization_barrier((total, arrived[1]))

    total_right = own
    for hop in range(1, hops + 1):
        total_right = total_right + jnp.where(
            column + hop < columns, arrived[hop].astype(f32), 0.0
        )

    pieces = jnp.stack([total] + [swapped(total, "disp", key) for key in range(1, parts)])
    pieces = pieces[jnp.arange(parts) ^ part][:, :, : 3 * groups]
    total = pieces.reshape(parts, 3, 3, groups, 3, outs)
    cell_count = D * width * columns * rows
    grad_kernel = jnp.transpose(total, (4, 1, 2, 5, 0, 3))[::-1].reshape(3, 3, 3, outs, G)
    grad_kernel = grad_kernel * (1.0 / math.sqrt(cell_count))
    return (grad_left, total_right.astype(bf16), grad_kernel)


def solution(mesh):
    return jax.shard_map(
        body,
        mesh=mesh,
        in_specs=(P(None, "col", None), P(None, "col", None), P(), P(None, "disp", "col", None)),
        out_specs=(P("disp", "col", None), P("disp", "col", None), P()),
        check_vma=False,
    )
```

```python
import functools
import math

import jax
import jax.numpy as jnp
import numpy as np
from jax import lax
from jax.experimental import pallas as pl
from jax.experimental.pallas import tpu as pltpu
from jax.sharding import PartitionSpec as P

C = 320
G = 40
D = 48
GROUP = C // G
HIGHEST = lax.Precision.HIGHEST


def shifted(value, axis, steps):
    count = lax.axis_size(axis)
    return lax.ppermute(value, axis, [(source, (source + steps) % count) for source in range(count)])


def conv_rows(outs, width):
    main = np.tile(np.arange(width), outs)
    return np.concatenate([main, np.full(outs, -1), np.full(outs, width)])


def toeplitz(kernel_local, width):
    outs, groups = kernel_local.shape[3:]
    row_col = conv_rows(outs, width)
    row_out = np.concatenate([np.repeat(np.arange(outs), width), np.tile(np.arange(outs), 2)])
    spread = np.zeros((outs, row_col.size), np.float32)
    spread[row_out, np.arange(row_col.size)] = 1
    taps = jnp.transpose(kernel_local[::-1], (1, 2, 4, 0, 3))
    wide = jnp.einsum(
        "qrgpo,ok->qrgpk", taps, jnp.asarray(spread, jnp.bfloat16),
        preferred_element_type=jnp.float32,
    ).astype(jnp.bfloat16)
    out_col = np.arange(width)
    column_tap = out_col[:, None] - row_col[None, :] + 1
    total = jnp.zeros((3, groups, width, 3, row_col.size), jnp.bfloat16)
    for tap in range(3):
        mask = jnp.asarray(column_tap == tap)[None, None, :, None, :]
        total = jnp.where(mask, wide[tap][:, :, None], total)
    return total.reshape(3 * groups * width, 3 * row_col.size)


def roll_zero(value, steps):
    size = value.shape[-1]
    lane = lax.broadcasted_iota(jnp.int32, value.shape, value.ndim - 1)
    moved = pltpu.roll(value, steps % size, value.ndim - 1)
    return jnp.where(lane == (0 if steps > 0 else size - 1), 0.0, moved)


def join(*refs):
    for at, ref in enumerate(refs[:-1]):
        refs[-1][at] = ref[...]


def right_block(places, hop, even_refs, odd_refs):
    if hop % 2 == 0:
        block = even_refs[hop // 2][...]
    else:
        second = places[1] & 1
        at = (hop + 1) // 2 - second
        count = odd_refs[1].shape[0]
        block = odd_refs[1][jnp.clip(at - 1, 0, count - 1)]
        if hop == 1:
            block = jnp.where(at > 0, block, odd_refs[0][...])
        if hop == 2 * count + 1:
            block = jnp.where(at <= count, block, odd_refs[2][...])
    return jnp.where(places[1] >= hop, block.astype(jnp.float32), 0.0)


def pack(cot_ref, halo_ref, packed_ref):
    outs, levels, width, rows = cot_ref.shape
    main = outs * width

    def step(level, carry):
        packed_ref[level, 0:main] = cot_ref[:, level].reshape(main, rows)
        packed_ref[level, main:] = halo_ref[level]
        return carry

    lax.fori_loop(0, levels, step, 0)


def add_grads(first_level, count, reach, skipped, cot_s, weight_ref, left_s, right_s, left_sum, grad_s):
    channels, width, rows = left_s.shape
    groups = channels // GROUP
    size = groups * width
    span = cot_s.shape[1]
    f32, bf16 = jnp.float32, jnp.bfloat16

    def pair_values(at):
        near = cot_s[pl.ds(at, 3)].reshape(3 * span, rows)
        far = cot_s[pl.ds(at + 1, 3)].reshape(3 * span, rows)
        result = jnp.dot(
            weight_ref[...], jnp.concatenate([near, far], axis=1), preferred_element_type=f32
        )
        values = []
        for half in range(2):
            part = result[:, half * rows : (half + 1) * rows]
            total = (
                part[size : 2 * size]
                + roll_zero(part[:size], -1)
                + roll_zero(part[2 * size :], 1)
            )
            values.append(total.astype(bf16).astype(f32))
        return values

    def step(number, carry):
        level = first_level + number * width
        base = reach - first_level - width - number * width
        rights = right_s.at[:, pl.ds(pl.multiple_of(base, width), 2 * width)]
        grads = grad_s.at[:, pl.ds(pl.multiple_of(base - skipped, width), 2 * width)]

        def use(pair, values):
            at = width - 2 * pair
            for group in range(groups):
                ones = [value[group * width : (group + 1) * width] for value in values]
                for c in range(group * GROUP, (group + 1) * GROUP):
                    left = left_s[c]
                    left_sum[c] += (
                        ones[0] * rights[c, at : at + width]
                        + ones[1] * rights[c, at - 1 : at - 1 + width]
                    )
                    grads[c, at : at + width] += ones[0] * left
                    grads[c, at - 1 : at - 1 + width] += ones[1] * left

        waiting = pair_values(level)
        for pair in range(1, width // 2):
            later = pair_values(level + 2 * pair)
            use(pair - 1, waiting)
            waiting = later
        use(width // 2 - 1, waiting)
        return carry

    lax.fori_loop(0, count // width, step, 0)


def upper_grads(keys, reach, far, pairs, places, *refs):
    block_refs, refs = refs[: len(keys)], refs[len(keys) :]
    even_refs, odd_refs, refs = refs[:pairs], refs[pairs : pairs + 2], refs[pairs + 2 :]
    left_ref, weight_ref, cot_s, left_sum, grad_out = refs[:5]
    sent_refs, (left_s, right_s, grad_s, sems) = refs[5 : 5 + far], refs[5 + far :]
    channels, width, rows = left_ref.shape
    levels, span = block_refs[0].shape[:2]
    f32, bf16 = jnp.float32, jnp.bfloat16

    copies = []
    for at, (key, source) in enumerate(zip(keys, block_refs)):
        start = (places[0] ^ key) * levels + 1
        copies.append(pltpu.make_async_copy(source, cot_s.at[pl.ds(start, levels)], sems.at[at]))
    for copy in copies:
        copy.start()
    cot_s[0] = jnp.zeros((span, rows), bf16)
    cot_s[D + 1] = jnp.zeros((span, rows), bf16)
    left_s[...] = left_ref[...].astype(f32)
    left_sum[...] = jnp.zeros(left_sum.shape, f32)
    grad_s[...] = jnp.zeros(grad_s.shape, f32)
    hops = reach // width
    for at in range(far + 1):
        block = right_block(places, hops - at, (None, *even_refs), (None, *odd_refs))
        right_s[:, at * width : (at + 1) * width] = block
    for copy in copies:
        copy.wait()
    add_grads(
        D // 2, D // 2, reach, 0, cot_s, weight_ref, left_s, right_s, left_sum, grad_s
    )
    grad_out[...] = grad_s[:, far * width :]
    for at in range(far):
        sent_refs[at][...] = (
            grad_s[:, at * width : (at + 1) * width] * (1.0 / GROUP)
        ).astype(bf16)


def lower_grads(
    first_level, count, reach, skipped, left_ref, weight_ref, cot_s, right_s, left_part, grad_part,
    left_out, grad_out, *rest
):
    sent_refs, (left_s, left_sum, grad_s) = rest[:-3], rest[-3:]
    channels, width, rows = left_ref.shape
    f32, bf16 = jnp.float32, jnp.bfloat16
    last = first_level == 0
    scale = 1.0 / GROUP if last else 1.0
    left_s[...] = left_ref[...].astype(f32)
    left_sum[...] = left_part[...]
    grad_s[...] = grad_part[...]
    add_grads(
        first_level, count, reach, skipped, cot_s, weight_ref, left_s, right_s, left_sum, grad_s
    )
    left_out[...] = (left_sum[...] * scale).astype(left_out.dtype)
    grad_out[...] = grad_s[:, len(sent_refs) * width :] * scale
    for at, sent_ref in enumerate(sent_refs):
        sent_ref[...] = (grad_s[:, at * width : (at + 1) * width] * (1.0 / GROUP)).astype(bf16)


def kernel_sums(hops, places, *refs):
    pairs = hops // 2
    even_refs, odd_refs, refs = refs[: pairs + 1], refs[pairs + 1 : pairs + 4], refs[pairs + 4 :]
    left_ref, cot_s, fold_ref, right_s, sums_ref, left_s, prod_s = refs
    channels, width, rows = left_ref.shape
    groups = channels // GROUP
    span = cot_s.shape[1]
    outs = span // (width + 2)
    main = outs * width
    size = groups * width
    reach = hops * width
    f32, bf16 = jnp.float32, jnp.bfloat16

    left_s[...] = left_ref[...].astype(f32)
    for hop in range(hops + 1):
        at = reach - hop * width
        right_s[:, at : at + width] = right_block(places, hop, even_refs, odd_refs)
    prod_s[...] = jnp.zeros(prod_s.shape, f32)
    chunk = width // 2

    def step(number, carry):
        level = number * width
        base = pl.multiple_of(reach - width - level, width)
        rights = right_s.at[:, pl.ds(base, 2 * width)]

        def volume_at(d):
            at = width - d
            shifts = ([], [], [])
            for group in range(groups):
                total = None
                for c in range(group * GROUP, (group + 1) * GROUP):
                    term = left_s[c] * rights[c, at : at + width]
                    total = term if total is None else total + term
                value = (total * (1.0 / GROUP)).astype(bf16).astype(f32)
                shifts[0].append(roll_zero(value, 1))
                shifts[1].append(value)
                shifts[2].append(roll_zero(value, -1))
            return jnp.concatenate(shifts[0] + shifts[1] + shifts[2], axis=0).astype(bf16)

        for half in range(2):
            first = half * chunk
            volume = jnp.concatenate([volume_at(first + k) for k in range(chunk)], axis=1)
            for tap in range(3):
                value = jnp.concatenate(
                    [cot_s[level + first + k + tap] for k in range(chunk)], axis=1
                )
                prod_s[tap] += lax.dot_general(
                    value, volume, (((1,), (1,)), ((), ())), preferred_element_type=f32
                )
        return carry

    lax.fori_loop(0, D // width, step, 0)

    col_in = lax.broadcasted_iota(jnp.int32, (width, 3 * size), 0)
    col_out = lax.broadcasted_iota(jnp.int32, (width, 3 * size), 1) % width
    edge = lax.broadcasted_iota(jnp.int32, (outs, 3 * size), 1) % width
    for column_tap in range(3):
        mask = col_out - col_in + 1 == column_tap
        taps = []
        for tap in range(3):
            value = prod_s[tap, 0:main].reshape(outs, width, 3 * size)
            total = jnp.sum(jnp.where(mask[None], value, 0.0), axis=1)
            if column_tap == 2:
                total = total + jnp.where(edge == 0, prod_s[tap, main : main + outs], 0.0)
            if column_tap == 0:
                total = total + jnp.where(edge == width - 1, prod_s[tap, main + outs : span], 0.0)
            taps.append(total)
        gathered = jnp.concatenate(taps, axis=0)
        sums_ref[column_tap] = lax.dot_general(
            fold_ref[...], gathered, (((1,), (1,)), ((), ())),
            precision=HIGHEST, preferred_element_type=f32,
        )


VMEM = pl.BlockSpec(memory_space=pltpu.VMEM)
SMEM = pl.BlockSpec(memory_space=pltpu.SMEM)
ANY = pl.BlockSpec(memory_space=pl.ANY)
MIB = 1024 * 1024


def run(function, operands, outs, scratch, limit, flops):
    return pl.pallas_call(
        function,
        out_shape=[jax.ShapeDtypeStruct(shape, kind) for shape, kind in outs],
        in_specs=[space for space, array in operands],
        out_specs=[VMEM] * len(outs),
        scratch_shapes=scratch,
        compiler_params=pltpu.CompilerParams(vmem_limit_bytes=limit * MIB),
        cost_estimate=pl.CostEstimate(flops=flops, bytes_accessed=1024, transcendentals=0),
    )(*[array for space, array in operands])


def swapped(value, axis, bit):
    count = lax.axis_size(axis)
    return lax.ppermute(value, axis, [(source, source ^ bit) for source in range(count)])


def gather_swapping(value, axis, last_bit=1):
    held = {0: value}
    bit = lax.axis_size(axis) // 2
    while bit >= last_bit:
        held.update({key | bit: swapped(item, axis, bit) for key, item in list(held.items())})
        bit //= 2
    return held


def total_swapping(value, bit):
    return value + swapped(value, "col", bit)


def body(left, right, kernel, cotangent):
    outs, levels, width, rows = cotangent.shape
    parts = lax.axis_size("disp")
    columns = lax.axis_size("col")
    channels = C // parts
    groups = G // parts
    size = groups * width
    span = outs * (width + 2)
    hops = (D + width - 2) // width
    far = D // 2 // width
    first = (hops // 2, hops // 2 + 1)
    near = hops - far
    part, column = lax.axis_index("disp"), lax.axis_index("col")
    places = jnp.stack([part, column]).astype(jnp.int32)
    f32, bf16 = jnp.float32, jnp.bfloat16

    low = jnp.transpose(cotangent[:, :, width - 1], (1, 0, 2))
    high = jnp.transpose(cotangent[:, :, 0], (1, 0, 2))
    low, high, right = lax.optimization_barrier((low, high, right))
    low, high = shifted(low, "col", 1), shifted(high, "col", -1)
    cots = gather_swapping(cotangent, "disp", 2)
    right_own = lax.dynamic_slice_in_dim(right, part * channels, channels, 0)
    left_own = lax.dynamic_slice_in_dim(left, part * channels, channels, 0)
    weights = toeplitz(lax.dynamic_slice_in_dim(kernel, part * groups, groups, 4), width)
    pairs = hops // 2
    evens = [right_own] + [shifted(right_own, "col", 2 * k) for k in range(1, pairs + 1)]
    low, high, left_own, weights, *evens[1:pairs] = lax.optimization_barrier(
        (low, high, left_own, weights, *evens[1:pairs])
    )
    low = jnp.where(column > 0, low, 0).astype(bf16)
    high = jnp.where(column < columns - 1, high, 0).astype(bf16)
    halos = gather_swapping(jnp.concatenate([low, high], axis=1), "disp", 2)
    (joined,) = run(
        join, [(VMEM, item) for item in evens[1:pairs]],
        [((pairs - 1, channels, width, rows), bf16)], [], 4, 1000000,
    )
    odds = [swapped(item, "col", 1) for item in (right_own, joined, evens[pairs])]
    blocks = {}
    across = parts // 2
    cots[across], *odds = lax.optimization_barrier((cots[across], *odds))
    for key in cots:
        (block,) = run(
            pack, [(VMEM, cots[key]), (VMEM, halos[key])],
            [((levels, span, rows), bf16)], [], 4, 1000000,
        )
        blocks[key] = block
        blocks[key | 1] = swapped(block, "disp", 1)

    pad_rows = -(-3 * groups // 8) * 8
    fold = np.zeros((pad_rows, 3 * size), np.float32)
    fold[np.arange(3 * size) // width, np.arange(3 * size)] = 1

    block = (channels, width, rows)
    wide = (channels, (hops + 1) * width, rows)
    f32_block, bf16_block = (block, f32), (block, bf16)
    reach = hops * width
    keys = sorted(blocks)
    cot_wide, left_part, grad_part, *sent = run(
        functools.partial(upper_grads, keys, reach, far, pairs),
        [(SMEM, places)]
        + [(ANY, blocks[key]) for key in keys]
        + [(VMEM, item) for item in (*evens[1:], *odds[1:])]
        + [(VMEM, left_own), (VMEM, weights)],
        [
            ((D + 2, span, rows), bf16),
            f32_block,
            ((channels, (near + 1) * width, rows), f32),
            *[bf16_block] * far,
        ],
        [
            pltpu.VMEM(block, f32),
            pltpu.VMEM((channels, (far + 1) * width, rows), f32),
            pltpu.VMEM(wide, f32),
            pltpu.SemaphoreType.DMA((parts,)),
        ],
        12, 8000000000,
    )
    arrived = {
        hop: shifted(value, "col", -hop) for hop, value in zip(range(hops, near, -1), sent)
    }
    right_wide, total = run(
        functools.partial(kernel_sums, hops),
        [(SMEM, places)]
        + [(VMEM, item) for item in (*evens, *odds, left_own, cot_wide, jnp.asarray(fold))],
        [(wide, f32), ((3, pad_rows, 3 * outs), f32)],
        [pltpu.VMEM(block, f32), pltpu.VMEM((3, span, 3 * size), f32)],
        12, 8000000000,
    )
    bits = [1 << k for k in reversed(range(columns.bit_length() - 1))]
    middle = near - 1

    def lower(first_level, count, done, kind, left_part, grad_part):
        skipped = (far + done) * width
        rest = near + 1 - done
        complete = rest - 1 if first_level == 0 else rest - 2
        return run(
            functools.partial(lower_grads, first_level, count, reach, skipped),
            [
                (VMEM, item)
                for item in (left_own, weights, cot_wide, right_wide, left_part, grad_part)
            ],
            [
                (block, kind),
                ((channels, (rest - complete) * width, rows), f32),
                *[bf16_block] * complete,
            ],
            [
                pltpu.VMEM(block, f32),
                pltpu.VMEM(block, f32),
                pltpu.VMEM((channels, rest * width, rows), f32),
            ],
            8, 1000000,
        )

    grad_part, total = lax.optimization_barrier((grad_part, total))
    left_part, grad_part, *sent = lower(width, D // 2 - width, 0, f32, left_part, grad_part)
    total = total_swapping(total, bits[0])
    sent, grad_part, total, arrived[near + 1] = lax.optimization_barrier(
        (sent, grad_part, total, arrived[near + 1])
    )
    sent, *items = lax.optimization_barrier((sent, *[arrived[hop] for hop in sorted(arrived)]))
    arrived = dict(zip(sorted(arrived), items))
    arrived.update(
        {hop: shifted(value, "col", -hop) for hop, value in zip(range(near, 1, -1), sent)}
    )
    grad_left, own, *sent = lower(0, width, middle, bf16, left_part, grad_part)
    total = total_swapping(total, bits[1])
    sent, total = lax.optimization_barrier((sent, total))
    arrived[1] = shifted(sent[0], "col", -1)
    for bit in bits[2:]:
        total = total_swapping(total, bit)
    total, arrived[1] = lax.optimization_barrier((total, arrived[1]))

    total_right = own
    for hop in range(1, hops + 1):
        total_right = total_right + jnp.where(
            column + hop < columns, arrived[hop].astype(f32), 0.0
        )

    pieces = jnp.stack([total] + [swapped(total, "disp", key) for key in range(1, parts)])
    pieces = pieces[jnp.arange(parts) ^ part][:, :, : 3 * groups]
    total = pieces.reshape(parts, 3, 3, groups, 3, outs)
    cell_count = D * width * columns * rows
    grad_kernel = jnp.transpose(total, (4, 1, 2, 5, 0, 3))[::-1].reshape(3, 3, 3, outs, G)
    grad_kernel = grad_kernel * (1.0 / math.sqrt(cell_count))
    return (grad_left, total_right.astype(bf16), grad_kernel)


def solution(mesh):
    return jax.shard_map(
        body,
        mesh=mesh,
        in_specs=(P(None, "col", None), P(None, "col", None), P(), P(None, "disp", "col", None)),
        out_specs=(P("disp", "col", None), P("disp", "col", None), P()),
        check_vma=False,
    )
```

```python
import functools
import math

import jax
import jax.numpy as jnp
import numpy as np
from jax import lax
from jax.experimental import pallas as pl
from jax.experimental.pallas import tpu as pltpu
from jax.sharding import PartitionSpec as P

C = 320
G = 40
D = 48
GROUP = C // G
HIGHEST = lax.Precision.HIGHEST


def shifted(value, axis, steps):
    count = lax.axis_size(axis)
    return lax.ppermute(value, axis, [(source, (source + steps) % count) for source in range(count)])


def conv_rows(outs, width):
    main = np.tile(np.arange(width), outs)
    return np.concatenate([main, np.full(outs, -1), np.full(outs, width)])


def toeplitz(kernel_local, width):
    outs, groups = kernel_local.shape[3:]
    row_col = conv_rows(outs, width)
    row_out = np.concatenate([np.repeat(np.arange(outs), width), np.tile(np.arange(outs), 2)])
    spread = np.zeros((outs, row_col.size), np.float32)
    spread[row_out, np.arange(row_col.size)] = 1
    taps = jnp.transpose(kernel_local[::-1], (1, 2, 4, 0, 3))
    wide = jnp.einsum(
        "qrgpo,ok->qrgpk", taps, jnp.asarray(spread, jnp.bfloat16),
        preferred_element_type=jnp.float32,
    ).astype(jnp.bfloat16)
    out_col = np.arange(width)
    column_tap = out_col[:, None] - row_col[None, :] + 1
    total = jnp.zeros((3, groups, width, 3, row_col.size), jnp.bfloat16)
    for tap in range(3):
        mask = jnp.asarray(column_tap == tap)[None, None, :, None, :]
        total = jnp.where(mask, wide[tap][:, :, None], total)
    return total.reshape(3 * groups * width, 3 * row_col.size)


def roll_zero(value, steps):
    size = value.shape[-1]
    lane = lax.broadcasted_iota(jnp.int32, value.shape, value.ndim - 1)
    moved = pltpu.roll(value, steps % size, value.ndim - 1)
    return jnp.where(lane == (0 if steps > 0 else size - 1), 0.0, moved)


def join(*refs):
    for at, ref in enumerate(refs[:-1]):
        refs[-1][at] = ref[...]


def right_block(places, hop, even_refs, odd_refs):
    if hop % 2 == 0:
        block = even_refs[hop // 2][...]
    else:
        second = places[1] & 1
        at = (hop + 1) // 2 - second
        count = odd_refs[1].shape[0]
        block = odd_refs[1][jnp.clip(at - 1, 0, count - 1)]
        if hop == 1:
            block = jnp.where(at > 0, block, odd_refs[0][...])
        if hop == 2 * count + 1:
            block = jnp.where(at <= count, block, odd_refs[2][...])
    return jnp.where(places[1] >= hop, block.astype(jnp.float32), 0.0)


def pack(cot_ref, halo_ref, packed_ref):
    outs, levels, width, rows = cot_ref.shape
    main = outs * width

    def step(level, carry):
        packed_ref[level, 0:main] = cot_ref[:, level].reshape(main, rows)
        packed_ref[level, main:] = halo_ref[level]
        return carry

    lax.fori_loop(0, levels, step, 0)


def add_grads(first_level, count, reach, skipped, cot_s, weight_ref, left_s, right_s, left_sum, grad_s):
    channels, width, rows = left_s.shape
    groups = channels // GROUP
    size = groups * width
    span = cot_s.shape[1]
    f32, bf16 = jnp.float32, jnp.bfloat16

    def pair_values(at):
        near = cot_s[pl.ds(at, 3)].reshape(3 * span, rows)
        far = cot_s[pl.ds(at + 1, 3)].reshape(3 * span, rows)
        result = jnp.dot(
            weight_ref[...], jnp.concatenate([near, far], axis=1), preferred_element_type=f32
        )
        values = []
        for half in range(2):
            part = result[:, half * rows : (half + 1) * rows]
            total = (
                part[size : 2 * size]
                + roll_zero(part[:size], -1)
                + roll_zero(part[2 * size :], 1)
            )
            values.append(total.astype(bf16).astype(f32))
        return values

    def step(number, carry):
        level = first_level + number * width
        base = reach - first_level - width - number * width
        rights = right_s.at[:, pl.ds(pl.multiple_of(base, width), 2 * width)]
        grads = grad_s.at[:, pl.ds(pl.multiple_of(base - skipped, width), 2 * width)]

        def use(pair, values):
            at = width - 2 * pair
            for group in range(groups):
                ones = [value[group * width : (group + 1) * width] for value in values]
                for c in range(group * GROUP, (group + 1) * GROUP):
                    left = left_s[c]
                    left_sum[c] += (
                        ones[0] * rights[c, at : at + width]
                        + ones[1] * rights[c, at - 1 : at - 1 + width]
                    )
                    grads[c, at : at + width] += ones[0] * left
                    grads[c, at - 1 : at - 1 + width] += ones[1] * left

        waiting = pair_values(level)
        for pair in range(1, width // 2):
            later = pair_values(level + 2 * pair)
            use(pair - 1, waiting)
            waiting = later
        use(width // 2 - 1, waiting)
        return carry

    lax.fori_loop(0, count // width, step, 0)


def upper_grads(reach, far, left_ref, weight_ref, cot_s, right_s, left_sum, grad_out, *rest):
    sent_refs, (left_s, grad_s) = rest[:far], rest[far:]
    width = left_ref.shape[1]
    f32, bf16 = jnp.float32, jnp.bfloat16
    left_s[...] = left_ref[...].astype(f32)
    left_sum[...] = jnp.zeros(left_sum.shape, f32)
    grad_s[...] = jnp.zeros(grad_s.shape, f32)
    add_grads(
        D // 2, D // 2, reach, 0, cot_s, weight_ref, left_s, right_s, left_sum, grad_s
    )
    grad_out[...] = grad_s[:, far * width :]
    for at in range(far):
        sent_refs[at][...] = (
            grad_s[:, at * width : (at + 1) * width] * (1.0 / GROUP)
        ).astype(bf16)


def lower_grads(
    first_level, count, reach, skipped, left_ref, weight_ref, cot_s, right_s, left_part, grad_part,
    left_out, grad_out, *rest
):
    sent_refs, (left_s, left_sum, grad_s) = rest[:-3], rest[-3:]
    channels, width, rows = left_ref.shape
    f32, bf16 = jnp.float32, jnp.bfloat16
    last = first_level == 0
    scale = 1.0 / GROUP if last else 1.0
    left_s[...] = left_ref[...].astype(f32)
    left_sum[...] = left_part[...]
    grad_s[...] = grad_part[...]
    add_grads(
        first_level, count, reach, skipped, cot_s, weight_ref, left_s, right_s, left_sum, grad_s
    )
    left_out[...] = (left_sum[...] * scale).astype(left_out.dtype)
    grad_out[...] = grad_s[:, len(sent_refs) * width :] * scale
    for at, sent_ref in enumerate(sent_refs):
        sent_ref[...] = (grad_s[:, at * width : (at + 1) * width] * (1.0 / GROUP)).astype(bf16)


def kernel_sums(keys, hops, places, *refs):
    block_refs, refs = refs[: len(keys)], refs[len(keys) :]
    pairs = hops // 2
    even_refs, odd_refs, refs = refs[: pairs + 1], refs[pairs + 1 : pairs + 4], refs[pairs + 4 :]
    left_ref, fold_ref, cot_s, right_s, sums_ref, left_s, prod_s, sems = refs
    channels, width, rows = left_ref.shape
    groups = channels // GROUP
    levels, span = block_refs[0].shape[:2]
    outs = span // (width + 2)
    main = outs * width
    size = groups * width
    reach = hops * width
    f32, bf16 = jnp.float32, jnp.bfloat16

    copies = []
    for at, (key, source) in enumerate(zip(keys, block_refs)):
        start = (places[0] ^ key) * levels + 1
        copies.append(pltpu.make_async_copy(source, cot_s.at[pl.ds(start, levels)], sems.at[at]))
    for copy in copies:
        copy.start()
    cot_s[0] = jnp.zeros((span, rows), bf16)
    cot_s[D + 1] = jnp.zeros((span, rows), bf16)
    left_s[...] = left_ref[...].astype(f32)
    for hop in range(hops + 1):
        at = reach - hop * width
        right_s[:, at : at + width] = right_block(places, hop, even_refs, odd_refs)
    for copy in copies:
        copy.wait()
    prod_s[...] = jnp.zeros(prod_s.shape, f32)
    chunk = width // 2

    def step(number, carry):
        level = number * width
        base = pl.multiple_of(reach - width - level, width)
        rights = right_s.at[:, pl.ds(base, 2 * width)]

        def volume_at(d):
            at = width - d
            shifts = ([], [], [])
            for group in range(groups):
                total = None
                for c in range(group * GROUP, (group + 1) * GROUP):
                    term = left_s[c] * rights[c, at : at + width]
                    total = term if total is None else total + term
                value = (total * (1.0 / GROUP)).astype(bf16).astype(f32)
                shifts[0].append(roll_zero(value, 1))
                shifts[1].append(value)
                shifts[2].append(roll_zero(value, -1))
            return jnp.concatenate(shifts[0] + shifts[1] + shifts[2], axis=0).astype(bf16)

        for half in range(2):
            first = half * chunk
            volume = jnp.concatenate([volume_at(first + k) for k in range(chunk)], axis=1)
            for tap in range(3):
                value = jnp.concatenate(
                    [cot_s[level + first + k + tap] for k in range(chunk)], axis=1
                )
                prod_s[tap] += lax.dot_general(
                    value, volume, (((1,), (1,)), ((), ())), preferred_element_type=f32
                )
        return carry

    lax.fori_loop(0, D // width, step, 0)

    col_in = lax.broadcasted_iota(jnp.int32, (width, 3 * size), 0)
    col_out = lax.broadcasted_iota(jnp.int32, (width, 3 * size), 1) % width
    edge = lax.broadcasted_iota(jnp.int32, (outs, 3 * size), 1) % width
    for column_tap in range(3):
        mask = col_out - col_in + 1 == column_tap
        taps = []
        for tap in range(3):
            value = prod_s[tap, 0:main].reshape(outs, width, 3 * size)
            total = jnp.sum(jnp.where(mask[None], value, 0.0), axis=1)
            if column_tap == 2:
                total = total + jnp.where(edge == 0, prod_s[tap, main : main + outs], 0.0)
            if column_tap == 0:
                total = total + jnp.where(edge == width - 1, prod_s[tap, main + outs : span], 0.0)
            taps.append(total)
        gathered = jnp.concatenate(taps, axis=0)
        sums_ref[column_tap] = lax.dot_general(
            fold_ref[...], gathered, (((1,), (1,)), ((), ())),
            precision=HIGHEST, preferred_element_type=f32,
        )


VMEM = pl.BlockSpec(memory_space=pltpu.VMEM)
SMEM = pl.BlockSpec(memory_space=pltpu.SMEM)
ANY = pl.BlockSpec(memory_space=pl.ANY)
MIB = 1024 * 1024


def run(function, operands, outs, scratch, limit, flops):
    return pl.pallas_call(
        function,
        out_shape=[jax.ShapeDtypeStruct(shape, kind) for shape, kind in outs],
        in_specs=[space for space, array in operands],
        out_specs=[VMEM] * len(outs),
        scratch_shapes=scratch,
        compiler_params=pltpu.CompilerParams(vmem_limit_bytes=limit * MIB),
        cost_estimate=pl.CostEstimate(flops=flops, bytes_accessed=1024, transcendentals=0),
    )(*[array for space, array in operands])


def swapped(value, axis, bit):
    count = lax.axis_size(axis)
    return lax.ppermute(value, axis, [(source, source ^ bit) for source in range(count)])


def gather_swapping(value, axis, last_bit=1):
    held = {0: value}
    bit = lax.axis_size(axis) // 2
    while bit >= last_bit:
        held.update({key | bit: swapped(item, axis, bit) for key, item in list(held.items())})
        bit //= 2
    return held


def total_swapping(value, bit):
    return value + swapped(value, "col", bit)


def body(left, right, kernel, cotangent):
    outs, levels, width, rows = cotangent.shape
    parts = lax.axis_size("disp")
    columns = lax.axis_size("col")
    channels = C // parts
    groups = G // parts
    size = groups * width
    span = outs * (width + 2)
    hops = (D + width - 2) // width
    far = D // 2 // width
    first = (hops // 2, hops // 2 + 1)
    near = hops - far
    part, column = lax.axis_index("disp"), lax.axis_index("col")
    places = jnp.stack([part, column]).astype(jnp.int32)
    f32, bf16 = jnp.float32, jnp.bfloat16

    low = jnp.transpose(cotangent[:, :, width - 1], (1, 0, 2))
    high = jnp.transpose(cotangent[:, :, 0], (1, 0, 2))
    low, high, right = lax.optimization_barrier((low, high, right))
    low, high = shifted(low, "col", 1), shifted(high, "col", -1)
    cots = gather_swapping(cotangent, "disp", 2)
    right_own = lax.dynamic_slice_in_dim(right, part * channels, channels, 0)
    left_own = lax.dynamic_slice_in_dim(left, part * channels, channels, 0)
    weights = toeplitz(lax.dynamic_slice_in_dim(kernel, part * groups, groups, 4), width)
    pairs = hops // 2
    evens = [right_own] + [shifted(right_own, "col", 2 * k) for k in range(1, pairs + 1)]
    low, high, left_own, weights, *evens[1:pairs] = lax.optimization_barrier(
        (low, high, left_own, weights, *evens[1:pairs])
    )
    low = jnp.where(column > 0, low, 0).astype(bf16)
    high = jnp.where(column < columns - 1, high, 0).astype(bf16)
    halos = gather_swapping(jnp.concatenate([low, high], axis=1), "disp", 2)
    (joined,) = run(
        join, [(VMEM, item) for item in evens[1:pairs]],
        [((pairs - 1, channels, width, rows), bf16)], [], 4, 1000000,
    )
    odds = [swapped(item, "col", 1) for item in (right_own, joined, evens[pairs])]
    blocks = {}
    across = parts // 2
    cots[across], *odds = lax.optimization_barrier((cots[across], *odds))
    for key in cots:
        (block,) = run(
            pack, [(VMEM, cots[key]), (VMEM, halos[key])],
            [((levels, span, rows), bf16)], [], 4, 1000000,
        )
        blocks[key] = block
        blocks[key | 1] = swapped(block, "disp", 1)

    pad_rows = -(-3 * groups // 8) * 8
    fold = np.zeros((pad_rows, 3 * size), np.float32)
    fold[np.arange(3 * size) // width, np.arange(3 * size)] = 1

    block = (channels, width, rows)
    wide = (channels, (hops + 1) * width, rows)
    f32_block, bf16_block = (block, f32), (block, bf16)
    reach = hops * width
    keys = sorted(blocks)
    cot_wide, right_wide, total = run(
        functools.partial(kernel_sums, keys, hops),
        [(SMEM, places)]
        + [(ANY, blocks[key]) for key in keys]
        + [(VMEM, item) for item in (*evens, *odds, left_own, jnp.asarray(fold))],
        [((D + 2, span, rows), bf16), (wide, f32), ((3, pad_rows, 3 * outs), f32)],
        [
            pltpu.VMEM(block, f32),
            pltpu.VMEM((3, span, 3 * size), f32),
            pltpu.SemaphoreType.DMA((parts,)),
        ],
        12, 8000000000,
    )
    bits = [1 << k for k in reversed(range(columns.bit_length() - 1))]
    left_part, grad_part, *sent = run(
        functools.partial(upper_grads, reach, far),
        [(VMEM, item) for item in (left_own, weights, cot_wide, right_wide)],
        [f32_block, ((channels, (near + 1) * width, rows), f32), *[bf16_block] * far],
        [pltpu.VMEM(block, f32), pltpu.VMEM(wide, f32)],
        12, 8000000000,
    )
    total = total_swapping(total, bits[0])
    sent, grad_part, total = lax.optimization_barrier((sent, grad_part, total))
    arrived = {
        hop: shifted(value, "col", -hop) for hop, value in zip(range(hops, near, -1), sent)
    }
    middle = near - 1

    def lower(first_level, count, done, kind, left_part, grad_part):
        skipped = (far + done) * width
        rest = near + 1 - done
        complete = rest - 1 if first_level == 0 else rest - 2
        return run(
            functools.partial(lower_grads, first_level, count, reach, skipped),
            [
                (VMEM, item)
                for item in (left_own, weights, cot_wide, right_wide, left_part, grad_part)
            ],
            [
                (block, kind),
                ((channels, (rest - complete) * width, rows), f32),
                *[bf16_block] * complete,
            ],
            [
                pltpu.VMEM(block, f32),
                pltpu.VMEM(block, f32),
                pltpu.VMEM((channels, rest * width, rows), f32),
            ],
            8, 1000000,
        )

    left_part, grad_part, *sent = lower(width, D // 2 - width, 0, f32, left_part, grad_part)
    total = total_swapping(total, bits[1])
    grad_part, total = lax.optimization_barrier((grad_part, total))
    grad_left, own, *last = lower(0, width, middle, bf16, left_part, grad_part)
    for bit in bits[2:]:
        total = total_swapping(total, bit)
    distant = sorted(arrived)
    pieces = [total] + [swapped(total, "disp", key) for key in range(1, parts)]
    sent, last, pieces, *items = lax.optimization_barrier(
        (sent, last, pieces, *[arrived[hop] for hop in distant])
    )
    arrived = dict(zip(distant, items))
    for hop, value in zip(range(near, 0, -1), [*sent, *last]):
        arrived[hop] = shifted(value, "col", -hop)

    total_right = own
    for hop in range(1, hops + 1):
        total_right = total_right + jnp.where(
            column + hop < columns, arrived[hop].astype(f32), 0.0
        )

    pieces = jnp.stack(pieces)[jnp.arange(parts) ^ part][:, :, : 3 * groups]
    total = pieces.reshape(parts, 3, 3, groups, 3, outs)
    cell_count = D * width * columns * rows
    grad_kernel = jnp.transpose(total, (4, 1, 2, 5, 0, 3))[::-1].reshape(3, 3, 3, outs, G)
    grad_kernel = grad_kernel * (1.0 / math.sqrt(cell_count))
    return (grad_left, total_right.astype(bf16), grad_kernel)


def solution(mesh):
    return jax.shard_map(
        body,
        mesh=mesh,
        in_specs=(P(None, "col", None), P(None, "col", None), P(), P(None, "disp", "col", None)),
        out_specs=(P("disp", "col", None), P("disp", "col", None), P()),
        check_vma=False,
    )
```

```python
import functools
import math

import jax
import jax.numpy as jnp
import numpy as np
from jax import lax
from jax.experimental import pallas as pl
from jax.experimental.pallas import tpu as pltpu
from jax.sharding import PartitionSpec as P

C = 320
G = 40
D = 48
GROUP = C // G
HIGHEST = lax.Precision.HIGHEST


def shifted(value, axis, steps):
    count = lax.axis_size(axis)
    return lax.ppermute(value, axis, [(source, (source + steps) % count) for source in range(count)])


def conv_rows(outs, width):
    main = np.tile(np.arange(width), outs)
    return np.concatenate([main, np.full(outs, -1), np.full(outs, width)])


def toeplitz(kernel_local, width):
    outs, groups = kernel_local.shape[3:]
    row_col = conv_rows(outs, width)
    row_out = np.concatenate([np.repeat(np.arange(outs), width), np.tile(np.arange(outs), 2)])
    spread = np.zeros((outs, row_col.size), np.float32)
    spread[row_out, np.arange(row_col.size)] = 1
    taps = jnp.transpose(kernel_local[::-1], (1, 2, 4, 0, 3))
    wide = jnp.einsum(
        "qrgpo,ok->qrgpk", taps, jnp.asarray(spread, jnp.bfloat16),
        preferred_element_type=jnp.float32,
    ).astype(jnp.bfloat16)
    out_col = np.arange(width)
    column_tap = out_col[:, None] - row_col[None, :] + 1
    total = jnp.zeros((3, groups, width, 3, row_col.size), jnp.bfloat16)
    for tap in range(3):
        mask = jnp.asarray(column_tap == tap)[None, None, :, None, :]
        total = jnp.where(mask, wide[tap][:, :, None], total)
    return total.reshape(3 * groups * width, 3 * row_col.size)


def roll_zero(value, steps):
    size = value.shape[-1]
    lane = lax.broadcasted_iota(jnp.int32, value.shape, value.ndim - 1)
    moved = pltpu.roll(value, steps % size, value.ndim - 1)
    return jnp.where(lane == (0 if steps > 0 else size - 1), 0.0, moved)


def join(*refs):
    for at, ref in enumerate(refs[:-1]):
        refs[-1][at] = ref[...]


def right_block(places, hop, even_refs, odd_refs):
    if hop % 2 == 0:
        block = even_refs[hop // 2][...]
    else:
        second = places[1] & 1
        at = (hop + 1) // 2 - second
        count = odd_refs[1].shape[0]
        block = odd_refs[1][jnp.clip(at - 1, 0, count - 1)]
        if hop == 1:
            block = jnp.where(at > 0, block, odd_refs[0][...])
        if hop == 2 * count + 1:
            block = jnp.where(at <= count, block, odd_refs[2][...])
    return jnp.where(places[1] >= hop, block.astype(jnp.float32), 0.0)


def pack(cot_ref, halo_ref, packed_ref):
    outs, levels, width, rows = cot_ref.shape
    main = outs * width

    def step(level, carry):
        packed_ref[level, 0:main] = cot_ref[:, level].reshape(main, rows)
        packed_ref[level, main:] = halo_ref[level]
        return carry

    lax.fori_loop(0, levels, step, 0)


def add_grads(first_level, count, reach, skipped, cot_s, weight_ref, left_s, right_s, left_sum, grad_s):
    channels, width, rows = left_s.shape
    groups = channels // GROUP
    size = groups * width
    span = cot_s.shape[1]
    f32, bf16 = jnp.float32, jnp.bfloat16

    def pair_values(at):
        near = cot_s[pl.ds(at, 3)].reshape(3 * span, rows)
        far = cot_s[pl.ds(at + 1, 3)].reshape(3 * span, rows)
        result = jnp.dot(
            weight_ref[...], jnp.concatenate([near, far], axis=1), preferred_element_type=f32
        )
        values = []
        for half in range(2):
            part = result[:, half * rows : (half + 1) * rows]
            total = (
                part[size : 2 * size]
                + roll_zero(part[:size], -1)
                + roll_zero(part[2 * size :], 1)
            )
            values.append(total.astype(bf16).astype(f32))
        return values

    def step(number, carry):
        level = first_level + number * width
        base = reach - first_level - width - number * width
        rights = right_s.at[:, pl.ds(pl.multiple_of(base, width), 2 * width)]
        grads = grad_s.at[:, pl.ds(pl.multiple_of(base - skipped, width), 2 * width)]

        def use(pair, values):
            at = width - 2 * pair
            for group in range(groups):
                ones = [value[group * width : (group + 1) * width] for value in values]
                for c in range(group * GROUP, (group + 1) * GROUP):
                    left = left_s[c]
                    left_sum[c] += (
                        ones[0] * rights[c, at : at + width]
                        + ones[1] * rights[c, at - 1 : at - 1 + width]
                    )
                    grads[c, at : at + width] += ones[0] * left
                    grads[c, at - 1 : at - 1 + width] += ones[1] * left

        waiting = pair_values(level)
        for pair in range(1, width // 2):
            later = pair_values(level + 2 * pair)
            use(pair - 1, waiting)
            waiting = later
        use(width // 2 - 1, waiting)
        return carry

    lax.fori_loop(0, count // width, step, 0)


def upper_grads(reach, far, left_ref, weight_ref, cot_s, right_s, left_sum, grad_out, *rest):
    sent_refs, (left_s, grad_s) = rest[:far], rest[far:]
    width = left_ref.shape[1]
    f32, bf16 = jnp.float32, jnp.bfloat16
    left_s[...] = left_ref[...].astype(f32)
    left_sum[...] = jnp.zeros(left_sum.shape, f32)
    grad_s[...] = jnp.zeros(grad_s.shape, f32)
    add_grads(
        D // 2, D // 2, reach, 0, cot_s, weight_ref, left_s, right_s, left_sum, grad_s
    )
    grad_out[...] = grad_s[:, far * width :]
    for at in range(far):
        sent_refs[at][...] = (
            grad_s[:, at * width : (at + 1) * width] * (1.0 / GROUP)
        ).astype(bf16)


def lower_grads(
    first_level, count, reach, skipped, left_ref, weight_ref, cot_s, right_s, left_part, grad_part,
    left_out, grad_out, *rest
):
    sent_refs, (left_s, left_sum, grad_s) = rest[:-3], rest[-3:]
    channels, width, rows = left_ref.shape
    f32, bf16 = jnp.float32, jnp.bfloat16
    last = first_level == 0
    scale = 1.0 / GROUP if last else 1.0
    left_s[...] = left_ref[...].astype(f32)
    left_sum[...] = left_part[...]
    grad_s[...] = grad_part[...]
    add_grads(
        first_level, count, reach, skipped, cot_s, weight_ref, left_s, right_s, left_sum, grad_s
    )
    left_out[...] = (left_sum[...] * scale).astype(left_out.dtype)
    grad_out[...] = grad_s[:, len(sent_refs) * width :] * scale
    for at, sent_ref in enumerate(sent_refs):
        sent_ref[...] = (grad_s[:, at * width : (at + 1) * width] * (1.0 / GROUP)).astype(bf16)


def kernel_sums(keys, hops, places, *refs):
    block_refs, refs = refs[: len(keys)], refs[len(keys) :]
    pairs = hops // 2
    even_refs, odd_refs, refs = refs[: pairs + 1], refs[pairs + 1 : pairs + 4], refs[pairs + 4 :]
    left_ref, fold_ref, cot_s, right_s, sums_ref, left_s, prod_s, sems = refs
    channels, width, rows = left_ref.shape
    groups = channels // GROUP
    levels, span = block_refs[0].shape[:2]
    outs = span // (width + 2)
    main = outs * width
    size = groups * width
    reach = hops * width
    f32, bf16 = jnp.float32, jnp.bfloat16

    copies = []
    for at, (key, source) in enumerate(zip(keys, block_refs)):
        start = (places[0] ^ key) * levels + 1
        copies.append(pltpu.make_async_copy(source, cot_s.at[pl.ds(start, levels)], sems.at[at]))
    for copy in copies:
        copy.start()
    cot_s[0] = jnp.zeros((span, rows), bf16)
    cot_s[D + 1] = jnp.zeros((span, rows), bf16)
    left_s[...] = left_ref[...].astype(f32)
    for hop in range(hops + 1):
        at = reach - hop * width
        right_s[:, at : at + width] = right_block(places, hop, even_refs, odd_refs)
    for copy in copies:
        copy.wait()
    prod_s[...] = jnp.zeros(prod_s.shape, f32)
    chunk = width // 2

    def step(number, carry):
        level = number * width
        base = pl.multiple_of(reach - width - level, width)
        rights = right_s.at[:, pl.ds(base, 2 * width)]

        def volume_at(d):
            at = width - d
            shifts = ([], [], [])
            for group in range(groups):
                total = None
                for c in range(group * GROUP, (group + 1) * GROUP):
                    term = left_s[c] * rights[c, at : at + width]
                    total = term if total is None else total + term
                value = (total * (1.0 / GROUP)).astype(bf16).astype(f32)
                shifts[0].append(roll_zero(value, 1))
                shifts[1].append(value)
                shifts[2].append(roll_zero(value, -1))
            return jnp.concatenate(shifts[0] + shifts[1] + shifts[2], axis=0).astype(bf16)

        for half in range(2):
            first = half * chunk
            volume = jnp.concatenate([volume_at(first + k) for k in range(chunk)], axis=1)
            for tap in range(3):
                value = jnp.concatenate(
                    [cot_s[level + first + k + tap] for k in range(chunk)], axis=1
                )
                prod_s[tap] += lax.dot_general(
                    value, volume, (((1,), (1,)), ((), ())), preferred_element_type=f32
                )
        return carry

    lax.fori_loop(0, D // width, step, 0)

    col_in = lax.broadcasted_iota(jnp.int32, (width, 3 * size), 0)
    col_out = lax.broadcasted_iota(jnp.int32, (width, 3 * size), 1) % width
    edge = lax.broadcasted_iota(jnp.int32, (outs, 3 * size), 1) % width
    for column_tap in range(3):
        mask = col_out - col_in + 1 == column_tap
        taps = []
        for tap in range(3):
            value = prod_s[tap, 0:main].reshape(outs, width, 3 * size)
            total = jnp.sum(jnp.where(mask[None], value, 0.0), axis=1)
            if column_tap == 2:
                total = total + jnp.where(edge == 0, prod_s[tap, main : main + outs], 0.0)
            if column_tap == 0:
                total = total + jnp.where(edge == width - 1, prod_s[tap, main + outs : span], 0.0)
            taps.append(total)
        gathered = jnp.concatenate(taps, axis=0)
        sums_ref[column_tap] = lax.dot_general(
            fold_ref[...], gathered, (((1,), (1,)), ((), ())),
            precision=HIGHEST, preferred_element_type=f32,
        )


VMEM = pl.BlockSpec(memory_space=pltpu.VMEM)
SMEM = pl.BlockSpec(memory_space=pltpu.SMEM)
ANY = pl.BlockSpec(memory_space=pl.ANY)
MIB = 1024 * 1024


def run(function, operands, outs, scratch, limit, flops):
    return pl.pallas_call(
        function,
        out_shape=[jax.ShapeDtypeStruct(shape, kind) for shape, kind in outs],
        in_specs=[space for space, array in operands],
        out_specs=[VMEM] * len(outs),
        scratch_shapes=scratch,
        compiler_params=pltpu.CompilerParams(vmem_limit_bytes=limit * MIB),
        cost_estimate=pl.CostEstimate(flops=flops, bytes_accessed=1024, transcendentals=0),
    )(*[array for space, array in operands])


def swapped(value, axis, bit):
    count = lax.axis_size(axis)
    return lax.ppermute(value, axis, [(source, source ^ bit) for source in range(count)])


def gather_swapping(value, axis, last_bit=1):
    held = {0: value}
    bit = lax.axis_size(axis) // 2
    while bit >= last_bit:
        held.update({key | bit: swapped(item, axis, bit) for key, item in list(held.items())})
        bit //= 2
    return held


def total_swapping(value, bit):
    return value + swapped(value, "col", bit)


def body(left, right, kernel, cotangent):
    outs, levels, width, rows = cotangent.shape
    parts = lax.axis_size("disp")
    columns = lax.axis_size("col")
    channels = C // parts
    groups = G // parts
    size = groups * width
    span = outs * (width + 2)
    hops = (D + width - 2) // width
    far = D // 2 // width
    first = (hops // 2, hops // 2 + 1)
    near = hops - far
    part, column = lax.axis_index("disp"), lax.axis_index("col")
    places = jnp.stack([part, column]).astype(jnp.int32)
    f32, bf16 = jnp.float32, jnp.bfloat16

    low = jnp.transpose(cotangent[:, :, width - 1], (1, 0, 2))
    high = jnp.transpose(cotangent[:, :, 0], (1, 0, 2))
    low, high, right = lax.optimization_barrier((low, high, right))
    low, high = shifted(low, "col", 1), shifted(high, "col", -1)
    cots = gather_swapping(cotangent, "disp", 2)
    right_own = lax.dynamic_slice_in_dim(right, part * channels, channels, 0)
    left_own = lax.dynamic_slice_in_dim(left, part * channels, channels, 0)
    weights = toeplitz(lax.dynamic_slice_in_dim(kernel, part * groups, groups, 4), width)
    pairs = hops // 2
    evens = [right_own] + [shifted(right_own, "col", 2 * k) for k in range(1, pairs + 1)]
    low, high, left_own, weights, *evens[1:pairs] = lax.optimization_barrier(
        (low, high, left_own, weights, *evens[1:pairs])
    )
    low = jnp.where(column > 0, low, 0).astype(bf16)
    high = jnp.where(column < columns - 1, high, 0).astype(bf16)
    halos = gather_swapping(jnp.concatenate([low, high], axis=1), "disp", 2)
    (joined,) = run(
        join, [(VMEM, item) for item in evens[1:pairs]],
        [((pairs - 1, channels, width, rows), bf16)], [], 4, 1000000,
    )
    odds = [swapped(item, "col", 1) for item in (right_own, joined, evens[pairs])]
    blocks = {}
    across = parts // 2
    cots[across], *odds = lax.optimization_barrier((cots[across], *odds))
    for key in cots:
        (block,) = run(
            pack, [(VMEM, cots[key]), (VMEM, halos[key])],
            [((levels, span, rows), bf16)], [], 4, 1000000,
        )
        blocks[key] = block
        blocks[key | 1] = swapped(block, "disp", 1)

    pad_rows = -(-3 * groups // 8) * 8
    fold = np.zeros((pad_rows, 3 * size), np.float32)
    fold[np.arange(3 * size) // width, np.arange(3 * size)] = 1

    block = (channels, width, rows)
    wide = (channels, (hops + 1) * width, rows)
    f32_block, bf16_block = (block, f32), (block, bf16)
    reach = hops * width
    keys = sorted(blocks)
    cot_wide, right_wide, total = run(
        functools.partial(kernel_sums, keys, hops),
        [(SMEM, places)]
        + [(ANY, blocks[key]) for key in keys]
        + [(VMEM, item) for item in (*evens, *odds, left_own, jnp.asarray(fold))],
        [((D + 2, span, rows), bf16), (wide, f32), ((3, pad_rows, 3 * outs), f32)],
        [
            pltpu.VMEM(block, f32),
            pltpu.VMEM((3, span, 3 * size), f32),
            pltpu.SemaphoreType.DMA((parts,)),
        ],
        12, 8000000000,
    )
    bits = [1 << k for k in reversed(range(columns.bit_length() - 1))]
    left_part, grad_part, *sent = run(
        functools.partial(upper_grads, reach, far),
        [(VMEM, item) for item in (left_own, weights, cot_wide, right_wide)],
        [f32_block, ((channels, (near + 1) * width, rows), f32), *[bf16_block] * far],
        [pltpu.VMEM(block, f32), pltpu.VMEM(wide, f32)],
        12, 8000000000,
    )
    total = total_swapping(total, bits[0])
    sent, grad_part, total = lax.optimization_barrier((sent, grad_part, total))
    arrived = {
        hop: shifted(value, "col", -hop) for hop, value in zip(range(hops, near, -1), sent)
    }
    middle = near - 1

    def lower(first_level, count, done, kind, left_part, grad_part):
        skipped = (far + done) * width
        rest = near + 1 - done
        complete = rest - 1 if first_level == 0 else rest - 2
        return run(
            functools.partial(lower_grads, first_level, count, reach, skipped),
            [
                (VMEM, item)
                for item in (left_own, weights, cot_wide, right_wide, left_part, grad_part)
            ],
            [
                (block, kind),
                ((channels, (rest - complete) * width, rows), f32),
                *[bf16_block] * complete,
            ],
            [
                pltpu.VMEM(block, f32),
                pltpu.VMEM(block, f32),
                pltpu.VMEM((channels, rest * width, rows), f32),
            ],
            8, 1000000,
        )

    left_part, grad_part, *sent = lower(width, D // 2 - width, 0, f32, left_part, grad_part)
    total = total_swapping(total, bits[1])
    grad_part, total = lax.optimization_barrier((grad_part, total))
    grad_left, own, *last = lower(0, width, middle, bf16, left_part, grad_part)
    for bit in bits[2:]:
        total = total_swapping(total, bit)
    distant = sorted(arrived)
    sent, last, total, *items = lax.optimization_barrier(
        (sent, last, total, *[arrived[hop] for hop in distant])
    )
    arrived = dict(zip(distant, items))
    for hop, value in zip(range(near, 0, -1), [*sent, *last]):
        arrived[hop] = shifted(value, "col", -hop)

    total_right = own
    for hop in range(1, hops + 1):
        total_right = total_right + jnp.where(
            column + hop < columns, arrived[hop].astype(f32), 0.0
        )

    pieces = jnp.stack([total] + [swapped(total, "disp", key) for key in range(1, parts)])
    pieces = pieces[jnp.arange(parts) ^ part][:, :, : 3 * groups]
    total = pieces.reshape(parts, 3, 3, groups, 3, outs)
    cell_count = D * width * columns * rows
    grad_kernel = jnp.transpose(total, (4, 1, 2, 5, 0, 3))[::-1].reshape(3, 3, 3, outs, G)
    grad_kernel = grad_kernel * (1.0 / math.sqrt(cell_count))
    return (grad_left, total_right.astype(bf16), grad_kernel)


def solution(mesh):
    return jax.shard_map(
        body,
        mesh=mesh,
        in_specs=(P(None, "col", None), P(None, "col", None), P(), P(None, "disp", "col", None)),
        out_specs=(P("disp", "col", None), P("disp", "col", None), P()),
        check_vma=False,
    )
```

```python
import functools
import math

import jax
import jax.numpy as jnp
import numpy as np
from jax import lax
from jax.experimental import pallas as pl
from jax.experimental.pallas import tpu as pltpu
from jax.sharding import PartitionSpec as P

C = 320
G = 40
D = 48
GROUP = C // G
HIGHEST = lax.Precision.HIGHEST


def shifted(value, axis, steps):
    count = lax.axis_size(axis)
    return lax.ppermute(value, axis, [(source, (source + steps) % count) for source in range(count)])


def conv_rows(outs, width):
    main = np.tile(np.arange(width), outs)
    return np.concatenate([main, np.full(outs, -1), np.full(outs, width)])


def toeplitz(kernel_local, width):
    outs, groups = kernel_local.shape[3:]
    row_col = conv_rows(outs, width)
    row_out = np.concatenate([np.repeat(np.arange(outs), width), np.tile(np.arange(outs), 2)])
    spread = np.zeros((outs, row_col.size), np.float32)
    spread[row_out, np.arange(row_col.size)] = 1
    taps = jnp.transpose(kernel_local[::-1], (1, 2, 4, 0, 3))
    wide = jnp.einsum(
        "qrgpo,ok->qrgpk", taps, jnp.asarray(spread, jnp.bfloat16),
        preferred_element_type=jnp.float32,
    ).astype(jnp.bfloat16)
    out_col = np.arange(width)
    column_tap = out_col[:, None] - row_col[None, :] + 1
    total = jnp.zeros((3, groups, width, 3, row_col.size), jnp.bfloat16)
    for tap in range(3):
        mask = jnp.asarray(column_tap == tap)[None, None, :, None, :]
        total = jnp.where(mask, wide[tap][:, :, None], total)
    return total.reshape(3 * groups * width, 3 * row_col.size)


def roll_zero(value, steps):
    size = value.shape[-1]
    lane = lax.broadcasted_iota(jnp.int32, value.shape, value.ndim - 1)
    moved = pltpu.roll(value, steps % size, value.ndim - 1)
    return jnp.where(lane == (0 if steps > 0 else size - 1), 0.0, moved)


def join(*refs):
    for at, ref in enumerate(refs[:-1]):
        refs[-1][at] = ref[...]


def right_block(places, hop, even_refs, odd_refs):
    if hop % 2 == 0:
        block = even_refs[hop // 2][...]
    else:
        second = places[1] & 1
        at = (hop + 1) // 2 - second
        count = odd_refs[1].shape[0]
        block = odd_refs[1][jnp.clip(at - 1, 0, count - 1)]
        if hop == 1:
            block = jnp.where(at > 0, block, odd_refs[0][...])
        if hop == 2 * count + 1:
            block = jnp.where(at <= count, block, odd_refs[2][...])
    return jnp.where(places[1] >= hop, block.astype(jnp.float32), 0.0)


def pack(cot_ref, halo_ref, packed_ref):
    outs, levels, width, rows = cot_ref.shape
    main = outs * width

    def step(level, carry):
        packed_ref[level, 0:main] = cot_ref[:, level].reshape(main, rows)
        packed_ref[level, main:] = halo_ref[level]
        return carry

    lax.fori_loop(0, levels, step, 0)


def add_grads(first_level, count, reach, skipped, cot_s, weight_ref, left_s, right_s, left_sum, grad_s):
    channels, width, rows = left_s.shape
    groups = channels // GROUP
    size = groups * width
    span = cot_s.shape[1]
    f32, bf16 = jnp.float32, jnp.bfloat16

    def pair_values(at):
        near = cot_s[pl.ds(at, 3)].reshape(3 * span, rows)
        far = cot_s[pl.ds(at + 1, 3)].reshape(3 * span, rows)
        result = jnp.dot(
            weight_ref[...], jnp.concatenate([near, far], axis=1), preferred_element_type=f32
        )
        values = []
        for half in range(2):
            part = result[:, half * rows : (half + 1) * rows]
            total = (
                part[size : 2 * size]
                + roll_zero(part[:size], -1)
                + roll_zero(part[2 * size :], 1)
            )
            values.append(total.astype(bf16).astype(f32))
        return values

    def step(number, carry):
        level = first_level + number * width
        base = reach - first_level - width - number * width
        rights = right_s.at[:, pl.ds(pl.multiple_of(base, width), 2 * width)]
        grads = grad_s.at[:, pl.ds(pl.multiple_of(base - skipped, width), 2 * width)]

        def use(pair, values):
            at = width - 2 * pair
            for group in range(groups):
                ones = [value[group * width : (group + 1) * width] for value in values]
                for c in range(group * GROUP, (group + 1) * GROUP):
                    left = left_s[c]
                    left_sum[c] += (
                        ones[0] * rights[c, at : at + width]
                        + ones[1] * rights[c, at - 1 : at - 1 + width]
                    )
                    grads[c, at : at + width] += ones[0] * left
                    grads[c, at - 1 : at - 1 + width] += ones[1] * left

        waiting = pair_values(level)
        for pair in range(1, width // 2):
            later = pair_values(level + 2 * pair)
            use(pair - 1, waiting)
            waiting = later
        use(width // 2 - 1, waiting)
        return carry

    lax.fori_loop(0, count // width, step, 0)


def upper_grads(reach, far, left_ref, weight_ref, cot_s, right_s, left_sum, grad_out, *rest):
    sent_refs, (left_s, grad_s) = rest[:far], rest[far:]
    width = left_ref.shape[1]
    f32, bf16 = jnp.float32, jnp.bfloat16
    left_s[...] = left_ref[...].astype(f32)
    left_sum[...] = jnp.zeros(left_sum.shape, f32)
    grad_s[...] = jnp.zeros(grad_s.shape, f32)
    add_grads(
        reach - far * width, D - reach + far * width, reach, 0, cot_s, weight_ref, left_s, right_s, left_sum, grad_s
    )
    grad_out[...] = grad_s[:, far * width :]
    for at in range(far):
        sent_refs[at][...] = (
            grad_s[:, at * width : (at + 1) * width] * (1.0 / GROUP)
        ).astype(bf16)


def lower_grads(
    first_level, count, reach, skipped, left_ref, weight_ref, cot_s, right_s, left_part, grad_part,
    left_out, grad_out, *rest
):
    sent_refs, (left_s, left_sum, grad_s) = rest[:-3], rest[-3:]
    channels, width, rows = left_ref.shape
    f32, bf16 = jnp.float32, jnp.bfloat16
    last = first_level == 0
    scale = 1.0 / GROUP if last else 1.0
    left_s[...] = left_ref[...].astype(f32)
    left_sum[...] = left_part[...]
    grad_s[...] = grad_part[...]
    add_grads(
        first_level, count, reach, skipped, cot_s, weight_ref, left_s, right_s, left_sum, grad_s
    )
    left_out[...] = (left_sum[...] * scale).astype(left_out.dtype)
    grad_out[...] = grad_s[:, len(sent_refs) * width :] * scale
    for at, sent_ref in enumerate(sent_refs):
        sent_ref[...] = (grad_s[:, at * width : (at + 1) * width] * (1.0 / GROUP)).astype(bf16)


def kernel_sums(keys, hops, places, *refs):
    block_refs, refs = refs[: len(keys)], refs[len(keys) :]
    pairs = hops // 2
    even_refs, odd_refs, refs = refs[: pairs + 1], refs[pairs + 1 : pairs + 4], refs[pairs + 4 :]
    left_ref, fold_ref, cot_s, right_s, sums_ref, left_s, prod_s, sems = refs
    channels, width, rows = left_ref.shape
    groups = channels // GROUP
    levels, span = block_refs[0].shape[:2]
    outs = span // (width + 2)
    main = outs * width
    size = groups * width
    reach = hops * width
    f32, bf16 = jnp.float32, jnp.bfloat16

    copies = []
    for at, (key, source) in enumerate(zip(keys, block_refs)):
        start = (places[0] ^ key) * levels + 1
        copies.append(pltpu.make_async_copy(source, cot_s.at[pl.ds(start, levels)], sems.at[at]))
    for copy in copies:
        copy.start()
    cot_s[0] = jnp.zeros((span, rows), bf16)
    cot_s[D + 1] = jnp.zeros((span, rows), bf16)
    left_s[...] = left_ref[...].astype(f32)
    for hop in range(hops + 1):
        at = reach - hop * width
        right_s[:, at : at + width] = right_block(places, hop, even_refs, odd_refs)
    for copy in copies:
        copy.wait()
    prod_s[...] = jnp.zeros(prod_s.shape, f32)
    chunk = width // 2

    def step(number, carry):
        level = number * width
        base = pl.multiple_of(reach - width - level, width)
        rights = right_s.at[:, pl.ds(base, 2 * width)]

        def volume_at(d):
            at = width - d
            shifts = ([], [], [])
            for group in range(groups):
                total = None
                for c in range(group * GROUP, (group + 1) * GROUP):
                    term = left_s[c] * rights[c, at : at + width]
                    total = term if total is None else total + term
                value = (total * (1.0 / GROUP)).astype(bf16).astype(f32)
                shifts[0].append(roll_zero(value, 1))
                shifts[1].append(value)
                shifts[2].append(roll_zero(value, -1))
            return jnp.concatenate(shifts[0] + shifts[1] + shifts[2], axis=0).astype(bf16)

        for half in range(2):
            first = half * chunk
            volume = jnp.concatenate([volume_at(first + k) for k in range(chunk)], axis=1)
            for tap in range(3):
                value = jnp.concatenate(
                    [cot_s[level + first + k + tap] for k in range(chunk)], axis=1
                )
                prod_s[tap] += lax.dot_general(
                    value, volume, (((1,), (1,)), ((), ())), preferred_element_type=f32
                )
        return carry

    lax.fori_loop(0, D // width, step, 0)

    col_in = lax.broadcasted_iota(jnp.int32, (width, 3 * size), 0)
    col_out = lax.broadcasted_iota(jnp.int32, (width, 3 * size), 1) % width
    edge = lax.broadcasted_iota(jnp.int32, (outs, 3 * size), 1) % width
    for column_tap in range(3):
        mask = col_out - col_in + 1 == column_tap
        taps = []
        for tap in range(3):
            value = prod_s[tap, 0:main].reshape(outs, width, 3 * size)
            total = jnp.sum(jnp.where(mask[None], value, 0.0), axis=1)
            if column_tap == 2:
                total = total + jnp.where(edge == 0, prod_s[tap, main : main + outs], 0.0)
            if column_tap == 0:
                total = total + jnp.where(edge == width - 1, prod_s[tap, main + outs : span], 0.0)
            taps.append(total)
        gathered = jnp.concatenate(taps, axis=0)
        sums_ref[column_tap] = lax.dot_general(
            fold_ref[...], gathered, (((1,), (1,)), ((), ())),
            precision=HIGHEST, preferred_element_type=f32,
        )


VMEM = pl.BlockSpec(memory_space=pltpu.VMEM)
SMEM = pl.BlockSpec(memory_space=pltpu.SMEM)
ANY = pl.BlockSpec(memory_space=pl.ANY)
MIB = 1024 * 1024


def run(function, operands, outs, scratch, limit, flops):
    return pl.pallas_call(
        function,
        out_shape=[jax.ShapeDtypeStruct(shape, kind) for shape, kind in outs],
        in_specs=[space for space, array in operands],
        out_specs=[VMEM] * len(outs),
        scratch_shapes=scratch,
        compiler_params=pltpu.CompilerParams(vmem_limit_bytes=limit * MIB),
        cost_estimate=pl.CostEstimate(flops=flops, bytes_accessed=1024, transcendentals=0),
    )(*[array for space, array in operands])


def swapped(value, axis, bit):
    count = lax.axis_size(axis)
    return lax.ppermute(value, axis, [(source, source ^ bit) for source in range(count)])


def gather_swapping(value, axis, last_bit=1):
    held = {0: value}
    bit = lax.axis_size(axis) // 2
    while bit >= last_bit:
        held.update({key | bit: swapped(item, axis, bit) for key, item in list(held.items())})
        bit //= 2
    return held


def total_swapping(value, bit):
    return value + swapped(value, "col", bit)


def body(left, right, kernel, cotangent):
    outs, levels, width, rows = cotangent.shape
    parts = lax.axis_size("disp")
    columns = lax.axis_size("col")
    channels = C // parts
    groups = G // parts
    size = groups * width
    span = outs * (width + 2)
    hops = (D + width - 2) // width
    far = 2
    first = (hops // 2, hops // 2 + 1)
    near = hops - far
    part, column = lax.axis_index("disp"), lax.axis_index("col")
    places = jnp.stack([part, column]).astype(jnp.int32)
    f32, bf16 = jnp.float32, jnp.bfloat16

    low = jnp.transpose(cotangent[:, :, width - 1], (1, 0, 2))
    high = jnp.transpose(cotangent[:, :, 0], (1, 0, 2))
    low, high, right = lax.optimization_barrier((low, high, right))
    low, high = shifted(low, "col", 1), shifted(high, "col", -1)
    cots = gather_swapping(cotangent, "disp", 2)
    right_own = lax.dynamic_slice_in_dim(right, part * channels, channels, 0)
    left_own = lax.dynamic_slice_in_dim(left, part * channels, channels, 0)
    weights = toeplitz(lax.dynamic_slice_in_dim(kernel, part * groups, groups, 4), width)
    pairs = hops // 2
    evens = [right_own] + [shifted(right_own, "col", 2 * k) for k in range(1, pairs + 1)]
    swap_own = swapped(right_own, "col", 1)
    low, high, left_own, weights, swap_own, *evens[1:pairs] = lax.optimization_barrier(
        (low, high, left_own, weights, swap_own, *evens[1:pairs])
    )
    low = jnp.where(column > 0, low, 0).astype(bf16)
    high = jnp.where(column < columns - 1, high, 0).astype(bf16)
    halos = gather_swapping(jnp.concatenate([low, high], axis=1), "disp", 2)
    (joined,) = run(
        join, [(VMEM, item) for item in evens[1:pairs]],
        [((pairs - 1, channels, width, rows), bf16)], [], 4, 1000000,
    )
    odds = [swap_own] + [swapped(item, "col", 1) for item in (joined, evens[pairs])]
    blocks = {}
    across = parts // 2
    cots[across], *odds = lax.optimization_barrier((cots[across], *odds))
    for key in cots:
        (block,) = run(
            pack, [(VMEM, cots[key]), (VMEM, halos[key])],
            [((levels, span, rows), bf16)], [], 4, 1000000,
        )
        blocks[key] = block
        blocks[key | 1] = swapped(block, "disp", 1)

    pad_rows = -(-3 * groups // 8) * 8
    fold = np.zeros((pad_rows, 3 * size), np.float32)
    fold[np.arange(3 * size) // width, np.arange(3 * size)] = 1

    block = (channels, width, rows)
    wide = (channels, (hops + 1) * width, rows)
    f32_block, bf16_block = (block, f32), (block, bf16)
    reach = hops * width
    keys = sorted(blocks)
    cot_wide, right_wide, total = run(
        functools.partial(kernel_sums, keys, hops),
        [(SMEM, places)]
        + [(ANY, blocks[key]) for key in keys]
        + [(VMEM, item) for item in (*evens, *odds, left_own, jnp.asarray(fold))],
        [((D + 2, span, rows), bf16), (wide, f32), ((3, pad_rows, 3 * outs), f32)],
        [
            pltpu.VMEM(block, f32),
            pltpu.VMEM((3, span, 3 * size), f32),
            pltpu.SemaphoreType.DMA((parts,)),
        ],
        12, 8000000000,
    )
    bits = [1 << k for k in reversed(range(columns.bit_length() - 1))]
    left_part, grad_part, *sent = run(
        functools.partial(upper_grads, reach, far),
        [(VMEM, item) for item in (left_own, weights, cot_wide, right_wide)],
        [f32_block, ((channels, (near + 1) * width, rows), f32), *[bf16_block] * far],
        [pltpu.VMEM(block, f32), pltpu.VMEM(wide, f32)],
        12, 8000000000,
    )
    total = total_swapping(total, bits[0])
    sent, grad_part, total = lax.optimization_barrier((sent, grad_part, total))
    arrived = {
        hop: shifted(value, "col", -hop) for hop, value in zip(range(hops, near, -1), sent)
    }
    middle = near - 1

    def lower(first_level, count, done, kind, left_part, grad_part):
        skipped = (far + done) * width
        rest = near + 1 - done
        complete = rest - 1 if first_level == 0 else rest - 2
        return run(
            functools.partial(lower_grads, first_level, count, reach, skipped),
            [
                (VMEM, item)
                for item in (left_own, weights, cot_wide, right_wide, left_part, grad_part)
            ],
            [
                (block, kind),
                ((channels, (rest - complete) * width, rows), f32),
                *[bf16_block] * complete,
            ],
            [
                pltpu.VMEM(block, f32),
                pltpu.VMEM(block, f32),
                pltpu.VMEM((channels, rest * width, rows), f32),
            ],
            8, 1000000,
        )

    left_part, grad_part, *sent = lower(
        width, reach - (far + 1) * width, 0, f32, left_part, grad_part
    )
    total = total_swapping(total, bits[1])
    grad_part, total = lax.optimization_barrier((grad_part, total))
    grad_left, own, *last = lower(0, width, middle, bf16, left_part, grad_part)
    for bit in bits[2:]:
        total = total_swapping(total, bit)
    for hop, value in zip(range(near, 2, -1), sent):
        arrived[hop] = shifted(value, "col", -hop)
    waiting, arrived[hops], arrived[hops - 1] = lax.optimization_barrier(
        (sent[-1], arrived[hops], arrived[hops - 1])
    )
    arrived[2] = shifted(waiting, "col", -2)
    waiting, arrived[4], arrived[3] = lax.optimization_barrier(
        (last[0], arrived[4], arrived[3])
    )
    arrived[1] = shifted(waiting, "col", -1)

    total_right = own
    for hop in range(1, hops + 1):
        total_right = total_right + jnp.where(
            column + hop < columns, arrived[hop].astype(f32), 0.0
        )

    pieces = jnp.stack([total] + [swapped(total, "disp", key) for key in range(1, parts)])
    pieces = pieces[jnp.arange(parts) ^ part][:, :, : 3 * groups]
    total = pieces.reshape(parts, 3, 3, groups, 3, outs)
    cell_count = D * width * columns * rows
    grad_kernel = jnp.transpose(total, (4, 1, 2, 5, 0, 3))[::-1].reshape(3, 3, 3, outs, G)
    grad_kernel = grad_kernel * (1.0 / math.sqrt(cell_count))
    return (grad_left, total_right.astype(bf16), grad_kernel)


def solution(mesh):
    return jax.shard_map(
        body,
        mesh=mesh,
        in_specs=(P(None, "col", None), P(None, "col", None), P(), P(None, "disp", "col", None)),
        out_specs=(P("disp", "col", None), P("disp", "col", None), P()),
        check_vma=False,
    )
```

```python
import functools
import math

import jax
import jax.numpy as jnp
import numpy as np
from jax import lax
from jax.experimental import pallas as pl
from jax.experimental.pallas import tpu as pltpu
from jax.sharding import PartitionSpec as P

C = 320
G = 40
D = 48
GROUP = C // G
HIGHEST = lax.Precision.HIGHEST


def shifted(value, axis, steps):
    count = lax.axis_size(axis)
    return lax.ppermute(value, axis, [(source, (source + steps) % count) for source in range(count)])


def conv_rows(outs, width):
    main = np.tile(np.arange(width), outs)
    return np.concatenate([main, np.full(outs, -1), np.full(outs, width)])


def toeplitz(kernel_local, width):
    outs, groups = kernel_local.shape[3:]
    row_col = conv_rows(outs, width)
    row_out = np.concatenate([np.repeat(np.arange(outs), width), np.tile(np.arange(outs), 2)])
    spread = np.zeros((outs, row_col.size), np.float32)
    spread[row_out, np.arange(row_col.size)] = 1
    taps = jnp.transpose(kernel_local[::-1], (1, 2, 4, 0, 3))
    wide = jnp.einsum(
        "qrgpo,ok->qrgpk", taps, jnp.asarray(spread, jnp.bfloat16),
        preferred_element_type=jnp.float32,
    ).astype(jnp.bfloat16)
    out_col = np.arange(width)
    column_tap = out_col[:, None] - row_col[None, :] + 1
    total = jnp.zeros((3, groups, width, 3, row_col.size), jnp.bfloat16)
    for tap in range(3):
        mask = jnp.asarray(column_tap == tap)[None, None, :, None, :]
        total = jnp.where(mask, wide[tap][:, :, None], total)
    return total.reshape(3 * groups * width, 3 * row_col.size)


def roll_zero(value, steps):
    size = value.shape[-1]
    lane = lax.broadcasted_iota(jnp.int32, value.shape, value.ndim - 1)
    moved = pltpu.roll(value, steps % size, value.ndim - 1)
    return jnp.where(lane == (0 if steps > 0 else size - 1), 0.0, moved)


def join(*refs):
    for at, ref in enumerate(refs[:-1]):
        refs[-1][at] = ref[...]


def right_block(places, hop, even_refs, odd_refs):
    if hop % 2 == 0:
        block = even_refs[hop // 2][...]
    else:
        second = places[1] & 1
        at = (hop + 1) // 2 - second
        count = odd_refs[1].shape[0]
        block = odd_refs[1][jnp.clip(at - 1, 0, count - 1)]
        if hop == 1:
            block = jnp.where(at > 0, block, odd_refs[0][...])
        if hop == 2 * count + 1:
            block = jnp.where(at <= count, block, odd_refs[2][...])
    return jnp.where(places[1] >= hop, block.astype(jnp.float32), 0.0)


def pack(cot_ref, halo_ref, packed_ref):
    outs, levels, width, rows = cot_ref.shape
    main = outs * width

    def step(level, carry):
        packed_ref[level, 0:main] = cot_ref[:, level].reshape(main, rows)
        packed_ref[level, main:] = halo_ref[level]
        return carry

    lax.fori_loop(0, levels, step, 0)


def add_grads(first_level, count, reach, skipped, cot_s, weight_ref, left_s, right_s, left_sum, grad_s):
    channels, width, rows = left_s.shape
    groups = channels // GROUP
    size = groups * width
    span = cot_s.shape[1]
    f32, bf16 = jnp.float32, jnp.bfloat16

    def pair_values(at):
        near = cot_s[pl.ds(at, 3)].reshape(3 * span, rows)
        far = cot_s[pl.ds(at + 1, 3)].reshape(3 * span, rows)
        result = jnp.dot(
            weight_ref[...], jnp.concatenate([near, far], axis=1), preferred_element_type=f32
        )
        values = []
        for half in range(2):
            part = result[:, half * rows : (half + 1) * rows]
            total = (
                part[size : 2 * size]
                + roll_zero(part[:size], -1)
                + roll_zero(part[2 * size :], 1)
            )
            values.append(total.astype(bf16).astype(f32))
        return values

    def step(number, carry):
        level = first_level + number * width
        base = reach - first_level - width - number * width
        rights = right_s.at[:, pl.ds(pl.multiple_of(base, width), 2 * width)]
        grads = grad_s.at[:, pl.ds(pl.multiple_of(base - skipped, width), 2 * width)]

        def use(pair, values):
            at = width - 2 * pair
            for group in range(groups):
                ones = [value[group * width : (group + 1) * width] for value in values]
                for c in range(group * GROUP, (group + 1) * GROUP):
                    left = left_s[c]
                    left_sum[c] += (
                        ones[0] * rights[c, at : at + width]
                        + ones[1] * rights[c, at - 1 : at - 1 + width]
                    )
                    grads[c, at : at + width] += ones[0] * left
                    grads[c, at - 1 : at - 1 + width] += ones[1] * left

        waiting = pair_values(level)
        for pair in range(1, width // 2):
            later = pair_values(level + 2 * pair)
            use(pair - 1, waiting)
            waiting = later
        use(width // 2 - 1, waiting)
        return carry

    lax.fori_loop(0, count // width, step, 0)


def upper_grads(reach, far, left_ref, weight_ref, cot_s, right_s, left_sum, grad_out, *rest):
    sent_refs, (left_s, grad_s) = rest[:far], rest[far:]
    width = left_ref.shape[1]
    f32, bf16 = jnp.float32, jnp.bfloat16
    left_s[...] = left_ref[...].astype(f32)
    left_sum[...] = jnp.zeros(left_sum.shape, f32)
    grad_s[...] = jnp.zeros(grad_s.shape, f32)
    add_grads(
        reach - far * width, D - reach + far * width, reach, 0, cot_s, weight_ref, left_s, right_s, left_sum, grad_s
    )
    grad_out[...] = grad_s[:, far * width :]
    for at in range(far):
        sent_refs[at][...] = (
            grad_s[:, at * width : (at + 1) * width] * (1.0 / GROUP)
        ).astype(bf16)


def lower_grads(
    first_level, count, reach, skipped, left_ref, weight_ref, cot_s, right_s, left_part, grad_part,
    left_out, grad_out, *rest
):
    sent_refs, (left_s, left_sum, grad_s) = rest[:-3], rest[-3:]
    channels, width, rows = left_ref.shape
    f32, bf16 = jnp.float32, jnp.bfloat16
    last = first_level == 0
    scale = 1.0 / GROUP if last else 1.0
    left_s[...] = left_ref[...].astype(f32)
    left_sum[...] = left_part[...]
    grad_s[...] = grad_part[...]
    add_grads(
        first_level, count, reach, skipped, cot_s, weight_ref, left_s, right_s, left_sum, grad_s
    )
    left_out[...] = (left_sum[...] * scale).astype(left_out.dtype)
    grad_out[...] = grad_s[:, len(sent_refs) * width :] * scale
    for at, sent_ref in enumerate(sent_refs):
        sent_ref[...] = (grad_s[:, at * width : (at + 1) * width] * (1.0 / GROUP)).astype(bf16)


def kernel_sums(keys, hops, places, *refs):
    block_refs, refs = refs[: len(keys)], refs[len(keys) :]
    pairs = hops // 2
    even_refs, odd_refs, refs = refs[: pairs + 1], refs[pairs + 1 : pairs + 4], refs[pairs + 4 :]
    left_ref, fold_ref, cot_s, right_s, sums_ref, left_s, prod_s, sems = refs
    channels, width, rows = left_ref.shape
    groups = channels // GROUP
    levels, span = block_refs[0].shape[:2]
    outs = span // (width + 2)
    main = outs * width
    size = groups * width
    reach = hops * width
    f32, bf16 = jnp.float32, jnp.bfloat16

    copies = []
    for at, (key, source) in enumerate(zip(keys, block_refs)):
        start = (places[0] ^ key) * levels + 1
        copies.append(pltpu.make_async_copy(source, cot_s.at[pl.ds(start, levels)], sems.at[at]))
    for copy in copies:
        copy.start()
    cot_s[0] = jnp.zeros((span, rows), bf16)
    cot_s[D + 1] = jnp.zeros((span, rows), bf16)
    left_s[...] = left_ref[...].astype(f32)
    for hop in range(hops + 1):
        at = reach - hop * width
        right_s[:, at : at + width] = right_block(places, hop, even_refs, odd_refs)
    for copy in copies:
        copy.wait()
    prod_s[...] = jnp.zeros(prod_s.shape, f32)
    chunk = width // 2

    def step(number, carry):
        level = number * width
        base = pl.multiple_of(reach - width - level, width)
        rights = right_s.at[:, pl.ds(base, 2 * width)]

        def volume_at(d):
            at = width - d
            shifts = ([], [], [])
            for group in range(groups):
                total = None
                for c in range(group * GROUP, (group + 1) * GROUP):
                    term = left_s[c] * rights[c, at : at + width]
                    total = term if total is None else total + term
                value = (total * (1.0 / GROUP)).astype(bf16).astype(f32)
                shifts[0].append(roll_zero(value, 1))
                shifts[1].append(value)
                shifts[2].append(roll_zero(value, -1))
            return jnp.concatenate(shifts[0] + shifts[1] + shifts[2], axis=0).astype(bf16)

        for half in range(2):
            first = half * chunk
            volume = jnp.concatenate([volume_at(first + k) for k in range(chunk)], axis=1)
            for tap in range(3):
                value = jnp.concatenate(
                    [cot_s[level + first + k + tap] for k in range(chunk)], axis=1
                )
                prod_s[tap] += lax.dot_general(
                    value, volume, (((1,), (1,)), ((), ())), preferred_element_type=f32
                )
        return carry

    lax.fori_loop(0, D // width, step, 0)

    col_in = lax.broadcasted_iota(jnp.int32, (width, 3 * size), 0)
    col_out = lax.broadcasted_iota(jnp.int32, (width, 3 * size), 1) % width
    edge = lax.broadcasted_iota(jnp.int32, (outs, 3 * size), 1) % width
    for column_tap in range(3):
        mask = col_out - col_in + 1 == column_tap
        taps = []
        for tap in range(3):
            value = prod_s[tap, 0:main].reshape(outs, width, 3 * size)
            total = jnp.sum(jnp.where(mask[None], value, 0.0), axis=1)
            if column_tap == 2:
                total = total + jnp.where(edge == 0, prod_s[tap, main : main + outs], 0.0)
            if column_tap == 0:
                total = total + jnp.where(edge == width - 1, prod_s[tap, main + outs : span], 0.0)
            taps.append(total)
        gathered = jnp.concatenate(taps, axis=0)
        sums_ref[column_tap] = lax.dot_general(
            fold_ref[...], gathered, (((1,), (1,)), ((), ())),
            precision=HIGHEST, preferred_element_type=f32,
        )


VMEM = pl.BlockSpec(memory_space=pltpu.VMEM)
SMEM = pl.BlockSpec(memory_space=pltpu.SMEM)
ANY = pl.BlockSpec(memory_space=pl.ANY)
MIB = 1024 * 1024


def run(function, operands, outs, scratch, limit, flops):
    return pl.pallas_call(
        function,
        out_shape=[jax.ShapeDtypeStruct(shape, kind) for shape, kind in outs],
        in_specs=[space for space, array in operands],
        out_specs=[VMEM] * len(outs),
        scratch_shapes=scratch,
        compiler_params=pltpu.CompilerParams(vmem_limit_bytes=limit * MIB),
        cost_estimate=pl.CostEstimate(flops=flops, bytes_accessed=1024, transcendentals=0),
    )(*[array for space, array in operands])


def swapped(value, axis, bit):
    count = lax.axis_size(axis)
    return lax.ppermute(value, axis, [(source, source ^ bit) for source in range(count)])


def gather_swapping(value, axis, last_bit=1):
    held = {0: value}
    bit = lax.axis_size(axis) // 2
    while bit >= last_bit:
        held.update({key | bit: swapped(item, axis, bit) for key, item in list(held.items())})
        bit //= 2
    return held


def total_swapping(value, bit):
    return value + swapped(value, "col", bit)


def body(left, right, kernel, cotangent):
    outs, levels, width, rows = cotangent.shape
    parts = lax.axis_size("disp")
    columns = lax.axis_size("col")
    channels = C // parts
    groups = G // parts
    size = groups * width
    span = outs * (width + 2)
    hops = (D + width - 2) // width
    far = 2
    first = (hops // 2, hops // 2 + 1)
    near = hops - far
    part, column = lax.axis_index("disp"), lax.axis_index("col")
    places = jnp.stack([part, column]).astype(jnp.int32)
    f32, bf16 = jnp.float32, jnp.bfloat16

    low = jnp.transpose(cotangent[:, :, width - 1], (1, 0, 2))
    high = jnp.transpose(cotangent[:, :, 0], (1, 0, 2))
    low, high, right = lax.optimization_barrier((low, high, right))
    low, high = shifted(low, "col", 1), shifted(high, "col", -1)
    cots = gather_swapping(cotangent, "disp", 2)
    right_own = lax.dynamic_slice_in_dim(right, part * channels, channels, 0)
    left_own = lax.dynamic_slice_in_dim(left, part * channels, channels, 0)
    weights = toeplitz(lax.dynamic_slice_in_dim(kernel, part * groups, groups, 4), width)
    pairs = hops // 2
    evens = [right_own] + [shifted(right_own, "col", 2 * k) for k in range(1, pairs + 1)]
    swap_own = swapped(right_own, "col", 1)
    low, high, left_own, weights, swap_own, *evens[1:pairs] = lax.optimization_barrier(
        (low, high, left_own, weights, swap_own, *evens[1:pairs])
    )
    low = jnp.where(column > 0, low, 0).astype(bf16)
    high = jnp.where(column < columns - 1, high, 0).astype(bf16)
    halos = gather_swapping(jnp.concatenate([low, high], axis=1), "disp", 2)
    (joined,) = run(
        join, [(VMEM, item) for item in evens[1:pairs]],
        [((pairs - 1, channels, width, rows), bf16)], [], 4, 1000000,
    )
    odds = [swap_own] + [swapped(item, "col", 1) for item in (joined, evens[pairs])]
    blocks = {}
    across = parts // 2
    cots[across], *odds = lax.optimization_barrier((cots[across], *odds))
    for key in cots:
        (block,) = run(
            pack, [(VMEM, cots[key]), (VMEM, halos[key])],
            [((levels, span, rows), bf16)], [], 4, 1000000,
        )
        blocks[key] = block
        blocks[key | 1] = swapped(block, "disp", 1)

    pad_rows = -(-3 * groups // 8) * 8
    fold = np.zeros((pad_rows, 3 * size), np.float32)
    fold[np.arange(3 * size) // width, np.arange(3 * size)] = 1

    block = (channels, width, rows)
    wide = (channels, (hops + 1) * width, rows)
    f32_block, bf16_block = (block, f32), (block, bf16)
    reach = hops * width
    keys = sorted(blocks)
    cot_wide, right_wide, total = run(
        functools.partial(kernel_sums, keys, hops),
        [(SMEM, places)]
        + [(ANY, blocks[key]) for key in keys]
        + [(VMEM, item) for item in (*evens, *odds, left_own, jnp.asarray(fold))],
        [((D + 2, span, rows), bf16), (wide, f32), ((3, pad_rows, 3 * outs), f32)],
        [
            pltpu.VMEM(block, f32),
            pltpu.VMEM((3, span, 3 * size), f32),
            pltpu.SemaphoreType.DMA((parts,)),
        ],
        12, 8000000000,
    )
    bits = [1 << k for k in reversed(range(columns.bit_length() - 1))]
    left_part, grad_part, *sent = run(
        functools.partial(upper_grads, reach, far),
        [(VMEM, item) for item in (left_own, weights, cot_wide, right_wide)],
        [f32_block, ((channels, (near + 1) * width, rows), f32), *[bf16_block] * far],
        [pltpu.VMEM(block, f32), pltpu.VMEM(wide, f32)],
        12, 8000000000,
    )
    total = total_swapping(total, bits[0])
    sent, grad_part, total = lax.optimization_barrier((sent, grad_part, total))
    arrived = {
        hop: shifted(value, "col", -hop) for hop, value in zip(range(hops, near, -1), sent)
    }

    def lower(first_level, count, done, kind, left_part, grad_part):
        skipped = (far + done) * width
        rest = near + 1 - done
        complete = rest - 1 if first_level == 0 else rest - 2
        return run(
            functools.partial(lower_grads, first_level, count, reach, skipped),
            [
                (VMEM, item)
                for item in (left_own, weights, cot_wide, right_wide, left_part, grad_part)
            ],
            [
                (block, kind),
                ((channels, (rest - complete) * width, rows), f32),
                *[bf16_block] * complete,
            ],
            [
                pltpu.VMEM(block, f32),
                pltpu.VMEM(block, f32),
                pltpu.VMEM((channels, rest * width, rows), f32),
            ],
            8, 1000000,
        )

    grad_left, own, *sent = lower(0, reach - far * width, 0, bf16, left_part, grad_part)
    total = total_swapping(total, bits[1])
    own, total = lax.optimization_barrier((own, total))
    sent[2:], arrived[hops], arrived[hops - 1] = lax.optimization_barrier(
        (sent[2:], arrived[hops], arrived[hops - 1])
    )
    for hop, value in zip(range(near, 0, -1), sent):
        arrived[hop] = shifted(value, "col", -hop)
    for bit in bits[2:]:
        total = total_swapping(total, bit)

    total_right = own
    for hop in range(1, hops + 1):
        total_right = total_right + jnp.where(
            column + hop < columns, arrived[hop].astype(f32), 0.0
        )

    pieces = jnp.stack([total] + [swapped(total, "disp", key) for key in range(1, parts)])
    pieces = pieces[jnp.arange(parts) ^ part][:, :, : 3 * groups]
    total = pieces.reshape(parts, 3, 3, groups, 3, outs)
    cell_count = D * width * columns * rows
    grad_kernel = jnp.transpose(total, (4, 1, 2, 5, 0, 3))[::-1].reshape(3, 3, 3, outs, G)
    grad_kernel = grad_kernel * (1.0 / math.sqrt(cell_count))
    return (grad_left, total_right.astype(bf16), grad_kernel)


def solution(mesh):
    return jax.shard_map(
        body,
        mesh=mesh,
        in_specs=(P(None, "col", None), P(None, "col", None), P(), P(None, "disp", "col", None)),
        out_specs=(P("disp", "col", None), P("disp", "col", None), P()),
        check_vma=False,
    )
```
